32 devices in a mesh: group: 2 (over y), tile: 4 (over z), chan: 4 (over x, core).
Axes of the slice: x: 2, y: 2, z: 4, core: 2. Of those that a mesh axis runs over, the one named last changes fastest.
Arguments:
- source: bfloat16 [128, 16384], P('chan', ('group', 'tile')), parts along dimension 1, may hold values from -6 to 6
- send_list: int32 [4, 4, 8], P('tile'), may hold values from 0 to 15, as said below
- block_slot: int32 [512, 6], P('tile'), may hold values from 0 to 31, as said below
- weight_index: int32 [512, 6], P('tile'), may hold values from 0 to 31
- remap_table: bfloat16 [32, 128, 128], replicated, may hold values from -0.21875 to 0.21875
- neighbour_tile: int32 [4, 4], P('tile'), may hold values from 0 to 3, as said below
- neighbour_edge: int32 [4, 4], P('tile'), may hold values from 0 to 7, as said below
- conv_weight: bfloat16 [3, 3, 128, 256], P(None, None, None, 'chan'), may hold values from -0.1875 to 0.1875
Outputs:
- convolved: bfloat16 [256, 1024, 128], P('chan', ('group', 'tile')), parts along dimension 1
The draws below stay inside these ranges and needn't reach their ends.
There are 2 independent parts, one for each index of `group`. The reference program is written for one: setup_inputs(seed, part) draws one part's arguments, and reference() takes and returns one part's arrays. A program takes and returns all parts, laid end to end along the dimension named above; an argument that names none is the same for every part. Nothing has to cross between parts.
Inputs may be any that keep to these rules, and one draw needn't show every extreme that they name: `send_list`: within one band and tile the 8 entries are distinct local block numbers of that band. `block_slot`: A tile reads from a band only the first slots of that band's list to it, at least one; every such slot is read by some row of the tile; every band has some tile, a different one for each band, that reads all 8 slots of that band's list to it. `neighbour_tile`: sides pair up: if side s of tile u borders edge e of tile v, then side e of tile v borders edge s of tile u with the same reversal. `neighbour_edge`: an edge number 0 to 3, plus 4 where the order is reversed; consistent with neighbour_tile as stated there.
All inputs are finite; a program needn't handle non-finite values.
Results may differ from the reference program's by a relative error of at most 0.0049.
Values may be sent and summed in bfloat16 or wider, within the bound.
No kernel may reach another device: no remote copies, remote signals or barrier semaphores. Data moves between devices by JAX's collectives and lax.ppermute only.
A program may use at most 128 MiB of HBM per device.

```python
import jax
import jax.numpy as jnp
from jax import lax

C = 128
COUT = 256
S = 128
K = 6
NW = 32
CAP = 8
SB = 16
SRC = 8192
PROWS = 512
N_TILE = 4


def edge_pairs(key):
    shuffled = jax.random.permutation(jax.random.fold_in(key, 11), 4 * N_TILE).astype(jnp.int32)
    flip_bits = jax.random.randint(jax.random.fold_in(key, 12), (2 * N_TILE,), 0, 2).astype(jnp.int32)
    firsts = shuffled[0::2]
    seconds = shuffled[1::2]
    holds_three = (firsts == 3) | (seconds == 3)
    holds_zero = (firsts == 0) | (seconds == 0)
    flip_bits = jnp.where(holds_three, 1, jnp.where(holds_zero, 0, flip_bits)).astype(jnp.int32)
    partner = jnp.zeros((4 * N_TILE,), jnp.int32).at[firsts].set(seconds).at[seconds].set(firsts)
    reversal = jnp.zeros((4 * N_TILE,), jnp.int32).at[firsts].set(flip_bits).at[seconds].set(flip_bits)
    return (partner.reshape(N_TILE, 4), reversal.reshape(N_TILE, 4))


def draw_neighbour_tile(key, part):
    partner, reversal = edge_pairs(key)
    return (partner // 4).astype(jnp.int32)


def draw_neighbour_edge(key, part):
    partner, reversal = edge_pairs(key)
    return (partner % 4 + 4 * reversal).astype(jnp.int32)


def draw_send_list(key, part):
    key = jax.random.fold_in(key, 1)
    scores = jax.random.randint(key, (N_TILE, N_TILE, SB), 0, 1 << 20) * SB + jnp.arange(SB, dtype=jnp.int32)
    ranking = jnp.argsort(scores, axis=-1)
    return ranking[:, :, :CAP].astype(jnp.int32)


def draw_block_slot(key, part):
    key = jax.random.fold_in(key, 2)
    keys = jax.random.split(key, 5)
    receivers = jnp.arange(N_TILE, dtype=jnp.int32)[None, :]
    polar = (receivers < N_TILE // 4) | (receivers >= N_TILE - N_TILE // 4)
    counts = jax.random.randint(keys[0], (N_TILE, N_TILE), 1, CAP + 1) + jnp.where(polar, CAP // 2, 0)
    shuffled = jax.random.permutation(keys[1], N_TILE).astype(jnp.int32)
    counts = jnp.where(shuffled[:, None] == receivers, CAP, jnp.minimum(counts, CAP)).astype(jnp.int32)
    references = S * K
    position = jnp.arange(references, dtype=jnp.int32)
    base_sender = jnp.minimum(position // CAP, N_TILE - 1)
    base_slot = position % CAP
    base_count = jnp.transpose(counts[base_sender, :])
    valid = (position < N_TILE * CAP)[None, :] & (base_slot[None, :] < base_count)
    tile_ids = jnp.arange(N_TILE, dtype=jnp.int32)[:, None]
    rand_sender = jax.random.randint(keys[2], (N_TILE, references), 0, N_TILE).astype(jnp.int32)
    rand_count = counts[rand_sender, tile_ids]
    rand_slot = jax.random.randint(keys[3], (N_TILE, references), 0, rand_count).astype(jnp.int32)
    chosen = jnp.where(valid, base_sender * CAP + base_slot, rand_sender * CAP + rand_slot)
    scores = jax.random.randint(keys[4], (N_TILE, references), 0, 1 << 20) * references + position
    ranking = jnp.argsort(scores, axis=1)
    chosen = jnp.take_along_axis(chosen, ranking, axis=1)
    return chosen.reshape(N_TILE * S, K).astype(jnp.int32)


def touch_ends(drawn, rng, low, high):
    extent = drawn.shape
    index_at = [jax.random.randint(jax.random.fold_in(rng, axis), (), 0, extent[axis]) for axis in range(len(extent))]
    drawn = drawn.at[tuple(index_at)].set(low)
    longest = extent.index(max(extent))
    index_at[longest] = (index_at[longest] + 1) % extent[longest]
    return drawn.at[tuple(index_at)].set(high)


def block_levels(key, extent, cuts, low, top_value):
    factor_of = 1.0
    for dim, parts in cuts:
        draws = jax.random.uniform(jax.random.fold_in(jax.random.fold_in(key, 6), dim), (parts,), jnp.float32, low / len(cuts), top_value / len(cuts))
        factor_of = factor_of * jnp.repeat(jnp.exp(draws), extent[dim] // parts).reshape((-1,) + (1,) * (len(extent) - 1 - dim))
    return factor_of


def bell_draw(own_key, extent, spread, reach, cuts=(), kind=jnp.bfloat16):
    drawn = jax.random.normal(own_key, extent, jnp.float32) * spread
    if len(cuts) > 0:
        drawn = block_levels(own_key, extent, cuts, -0.22, 0.18) * drawn
    return jnp.clip(drawn, min=-reach, max=reach).astype(kind)


def setup_inputs(seed: int = 0, part: int = 0) -> dict:
    splits = jax.random.split(jax.random.key(seed), 9)
    part_splits = jax.random.split(jax.random.fold_in(splits[8], part), 9)
    return {
        "source": bell_draw(part_splits[0], (C, SRC), 1.0, 6.0, ((0, 4), (1, 4))),
        "send_list": draw_send_list(jax.random.fold_in(splits[8], 71), part),
        "block_slot": draw_block_slot(jax.random.fold_in(splits[8], 71), part),
        "weight_index": touch_ends(jax.random.randint(splits[3], (PROWS, K), 0, NW), jax.random.fold_in(splits[3], 1), 0, NW - 1).astype(jnp.int32),
        "remap_table": bell_draw(splits[4], (NW, S, S), (K * S) ** -0.5, 0.21875),
        "neighbour_tile": draw_neighbour_tile(jax.random.fold_in(splits[8], 71), part),
        "neighbour_edge": draw_neighbour_edge(jax.random.fold_in(splits[8], 71), part),
        "conv_weight": bell_draw(splits[7], (3, 3, C, COUT), (9 * C) ** -0.5, 0.1875, ((3, 4),)),
    }


def reference(source, send_list, block_slot, weight_index, remap_table, neighbour_tile, neighbour_edge, conv_weight):
    band_blocks = source.reshape(C, N_TILE, SB, S)

    def remap_tile(tile_idx):
        slots = lax.dynamic_slice_in_dim(block_slot, tile_idx * S, S, 0)
        table_rows = lax.dynamic_slice_in_dim(weight_index, tile_idx * S, S, 0)
        sender = slots // CAP
        local_block = send_list[sender, tile_idx, slots % CAP]
        picked = band_blocks[:, sender, local_block, :].astype(jnp.float32)
        matrices = remap_table[table_rows].astype(jnp.float32)
        summed = jnp.einsum("crkq,rkqp->crp", picked, matrices, precision=lax.Precision.HIGHEST)
        return summed.astype(jnp.bfloat16)

    remapped = lax.map(remap_tile, jnp.arange(N_TILE, dtype=jnp.int32))
    borders = jnp.stack([remapped[:, :, 0, :], remapped[:, :, -1, :], remapped[:, :, :, 0], remapped[:, :, :, -1]], axis=1)
    incoming = borders[neighbour_tile, neighbour_edge % 4]
    incoming = jnp.where((neighbour_edge >= 4)[:, :, None, None], incoming[:, :, :, ::-1], incoming)
    padded = jnp.pad(remapped, ((0, 0), (0, 0), (1, 1), (1, 1)))
    padded = padded.at[:, :, 0, 1:-1].set(incoming[:, 0])
    padded = padded.at[:, :, -1, 1:-1].set(incoming[:, 1])
    padded = padded.at[:, :, 1:-1, 0].set(incoming[:, 2])
    padded = padded.at[:, :, 1:-1, -1].set(incoming[:, 3])
    filters = conv_weight.astype(jnp.float32)

    def conv_tile(tile_in):
        result = lax.conv_general_dilated(tile_in[None].astype(jnp.float32), filters, (1, 1), "VALID", dimension_numbers=("NCHW", "HWIO", "NCHW"), precision=lax.Precision.HIGHEST)
        return result[0].astype(jnp.bfloat16)

    convolved = lax.map(conv_tile, padded)
    return jnp.transpose(convolved, (1, 0, 2, 3)).reshape(COUT, N_TILE * S, S)
```

```python
import functools

import jax
import jax.numpy as jnp
from jax import lax
from jax.experimental import pallas as pl
from jax.experimental.pallas import tpu as pltpu
from jax.sharding import PartitionSpec as P

F32 = jnp.float32
BF16 = jnp.bfloat16
VMEM = pl.BlockSpec(memory_space=pltpu.VMEM)
SMEM = pl.BlockSpec(memory_space=pltpu.SMEM)
ANY = pl.BlockSpec(memory_space=pl.ANY)
LIMIT = 48 * 2**20


def round_up(value, step):
    return -(-value // step) * step


def dot(a, b):
    return jnp.dot(a, b, preferred_element_type=F32)


def pack_kernel(side, slots_ref, weights_ref, lists_ref, source_ref, out_ref):
    chans = source_ref.shape[0]
    blocks = source_ref.shape[1] // side
    for block in range(blocks):
        out_ref[block * chans : (block + 1) * chans, :] = source_ref[:, block * side : (block + 1) * side]
    base = blocks * chans
    taps = slots_ref.shape[1]
    tiles, cap = lists_ref.shape[1], lists_ref.shape[2]
    rows = out_ref.shape[0] - base
    wide = jnp.concatenate(
        [slots_ref[...], weights_ref[...], jnp.zeros((side, side - 2 * taps), jnp.int32)], axis=1
    ).astype(F32)
    tables = wide.T[: 2 * taps]
    lists = jnp.concatenate(
        [lists_ref[0].astype(F32), jnp.zeros((tiles, side - cap), F32)], axis=1
    )
    parts = [tables, lists]
    if rows > 2 * taps + tiles:
        parts.append(jnp.zeros((rows - 2 * taps - tiles, side), F32))
    out_ref[base:, :] = jnp.concatenate(parts, axis=0).astype(BF16)


def edge_kernel(
    dims, neigh_ref, codes_ref, gathered_ref, table_ref, out_ref, ints, few_v, few_s, picked, columns, sem
):
    side, chans, blocks, tiles, cap, taps, rows = dims
    count = tiles * cap
    base = blocks * chans
    kinds = table_ref.shape[0]
    me = lax.axis_index("tile")
    for band in range(tiles):
        ints[band * rows : (band + 1) * rows, :] = gathered_ref[band, base:, :].astype(F32).astype(jnp.int32)
    owners = [me] + [neigh_ref[0, s] for s in range(4)]
    for which, owner in enumerate(owners):
        for band in range(tiles):
            few_v[pl.ds(which * tiles + band, 1), :] = ints[pl.ds(band * rows + 2 * taps + owner, 1), :]
    lists_end = 5 * tiles
    for s in range(4):
        for k in range(2 * taps):
            few_v[pl.ds(lists_end + s * 2 * taps + k, 1), :] = ints[pl.ds(owners[s + 1] * rows + k, 1), :]
    copy = pltpu.make_async_copy(few_v, few_s, sem)
    copy.start()
    column_of = lax.broadcasted_iota(jnp.int32, (side, side), 0)
    lane = lax.broadcasted_iota(jnp.int32, (side, side), 1)
    total = jnp.zeros((side, side), F32)
    for kind in range(kinds):
        pick = ((column_of == 0) & (lane == kind)) | ((column_of == side - 1) & (lane == kinds + kind))
        total = total + dot(table_ref[kind], pick.astype(BF16))
    columns[...] = total
    copy.wait()

    def block_of(which, slot):
        band = slot // cap
        local = few_s[which * tiles + band, slot % cap]
        return gathered_ref[band, pl.ds(pl.multiple_of(local * chans, chans), chans), :]

    for slot in range(count):
        out_ref[slot * chans : (slot + 1) * chans, :] = block_of(0, slot)
    per_group = side // kinds
    flip = (lane + column_of == side - 1).astype(BF16)
    for s in range(4):
        code = codes_ref[0, s]
        edge = code % 4
        dest = pl.ds((count + s) * chans, chans)

        @pl.when(edge < 2)
        def _():
            at = jnp.where(edge == 0, 0, side - 1)
            acc = jnp.zeros((chans, side), F32)
            for k in range(taps):
                slot = few_s[lists_end + s * 2 * taps + k, at]
                kind = few_s[lists_end + s * 2 * taps + taps + k, at]
                acc = acc + dot(block_of(1 + s, slot), table_ref[kind])
            out_ref[dest, :] = acc.astype(BF16)

        @pl.when(edge >= 2)
        def _():
            for slot in range(count):
                group, member = slot // per_group, slot % per_group
                picked[group * chans : (group + 1) * chans, member * side : (member + 1) * side] = block_of(1 + s, slot)
            col = columns[...]
            col = jnp.where(edge == 2, col, pltpu.roll(col, side - kinds, 1))
            col = jnp.where(lane < kinds, col, 0.0)
            spread = jnp.concatenate(
                [col if m == 0 else pltpu.roll(col, m * kinds, 1) for m in range(per_group)], axis=0
            ).astype(BF16)
            z = dot(picked[...], spread)
            z_hi = z.astype(BF16)
            z_lo = (z - z_hi.astype(F32)).astype(BF16)
            keys = [
                few_v[pl.ds(lists_end + s * 2 * taps + k, 1), :] * kinds
                + few_v[pl.ds(lists_end + s * 2 * taps + taps + k, 1), :]
                for k in range(taps)
            ]
            acc = jnp.zeros((2 * chans, side), F32)
            for group in range(count // per_group):
                seat = lax.broadcasted_iota(jnp.int32, (side, side), 0) + group * side
                hits = jnp.zeros((side, side), F32)
                for key in keys:
                    hits = hits + jnp.where(seat == key, 1.0, 0.0)
                at = slice(group * chans, (group + 1) * chans)
                acc = acc + dot(jnp.concatenate([z_hi[at], z_lo[at]], axis=0), hits.astype(BF16))
            out_ref[dest, :] = (acc[:chans] + acc[chans:]).astype(BF16)

        @pl.when(code >= 4)
        def _():
            out_ref[dest, :] = dot(out_ref[dest, :], flip).astype(BF16)


def tile_kernel(dims, order, *refs):
    side, chans, tiles, cap, taps, unroll_a, unroll_b = dims
    parts = refs[: len(order)]
    slots_ref, weights_ref, table_ref, filters_ref, out_ref, blocks, image, acc, sems = refs[len(order) :]
    count = tiles * cap
    all_chans = chans * len(order)
    outs = out_ref.shape[0]
    me = lax.axis_index("chan")
    copies = []
    for n, (flip, part) in enumerate(zip(order, parts)):
        off = pl.multiple_of((me ^ flip) * chans, chans)
        copies.append(pltpu.make_async_copy(part, blocks.at[:, pl.ds(off, chans), :], sems.at[n]))
    for copy in copies:
        copy.start()
    for copy in copies:
        copy.wait()

    def remap_row(r):
        lhs = jnp.concatenate([blocks[slots_ref[r, k]] for k in range(taps)], axis=1)
        rhs = jnp.concatenate([table_ref[weights_ref[r, k]] for k in range(taps)], axis=0)
        image[pl.ds(pl.multiple_of((r + 1) * all_chans, all_chans), all_chans), :] = dot(lhs, rhs).astype(BF16)

    def remap_step(t, carry):
        for u in range(unroll_a):
            remap_row(t * unroll_a + u)
        return carry

    lax.fori_loop(0, side // unroll_a, remap_step, 0)
    image[0:all_chans, :] = blocks[count]
    image[(side + 1) * all_chans :, :] = blocks[count + 1]

    lane = lax.broadcasted_iota(jnp.int32, (outs, side), 1)
    wide = lax.broadcasted_iota(jnp.int32, (all_chans, side), 1)

    def shifted(edge):
        value = blocks[count + edge].astype(F32)
        before = jnp.where(wide == 0, 0.0, pltpu.roll(value, 1, 1))
        after = jnp.where(wide == side - 1, 0.0, pltpu.roll(value, side - 1, 1))
        return jnp.concatenate([before, value, after], axis=0).astype(BF16)

    left = dot(filters_ref[0:outs, :], shifted(2))
    right = dot(filters_ref[2 * outs : 3 * outs, :], shifted(3))

    def conv_pair(i):
        x0 = image[pl.ds(pl.multiple_of(i * all_chans, all_chans), 3 * all_chans), :]
        x1 = image[pl.ds(pl.multiple_of((i + 1) * all_chans, all_chans), 3 * all_chans), :]
        y = dot(filters_ref[...], jnp.concatenate([x0, x1], axis=1))
        for h in range(2):
            yy = y[:, h * side : (h + 1) * side]
            from_left = jnp.where(lane == 0, pltpu.roll(left, lax.rem(side - (i + h), side), 1), pltpu.roll(yy[0:outs], 1, 1))
            from_right = jnp.where(
                lane == side - 1, pltpu.roll(right, side - 1 - (i + h), 1), pltpu.roll(yy[2 * outs :], side - 1, 1)
            )
            acc[:, i + h, :] = yy[outs : 2 * outs] + from_left + from_right

    def conv_step(t, carry):
        for u in range(unroll_b):
            conv_pair((t * unroll_b + u) * 2)
        return carry

    lax.fori_loop(0, side // (2 * unroll_b), conv_step, 0)

    def finish(t, carry):
        out_ref[pl.ds(t * 4, 4)] = acc[pl.ds(t * 4, 4)].astype(BF16)
        return carry

    lax.fori_loop(0, outs // 4, finish, 0)


def body(source, send_list, block_slot, weight_index, remap_table, neighbour_tile, neighbour_edge, conv_weight):
    kinds, side = remap_table.shape[:2]
    chans = source.shape[0]
    tiles, cap = send_list.shape[1:]
    taps = block_slot.shape[1]
    blocks = source.shape[1] // side
    count = tiles * cap
    outs = conv_weight.shape[3]
    parts = lax.axis_size("chan")
    rows = round_up(2 * taps + tiles, 16)
    params = pltpu.CompilerParams(vmem_limit_bytes=LIMIT)
    packed = pl.pallas_call(
        functools.partial(pack_kernel, side),
        out_shape=jax.ShapeDtypeStruct((blocks * chans + rows, side), BF16),
        in_specs=[VMEM] * 4,
        out_specs=VMEM,
        compiler_params=params,
        name="pack",
    )(block_slot, weight_index, send_list, source)
    gathered = lax.all_gather(packed, "tile")
    few = 5 * tiles + 4 * 2 * taps
    mine = pl.pallas_call(
        functools.partial(edge_kernel, (side, chans, blocks, tiles, cap, taps, rows)),
        out_shape=jax.ShapeDtypeStruct(((count + 4) * chans, side), BF16),
        in_specs=[SMEM, SMEM, VMEM, VMEM],
        out_specs=VMEM,
        scratch_shapes=[
            pltpu.VMEM((tiles * rows, side), jnp.int32),
            pltpu.VMEM((few, side), jnp.int32),
            pltpu.SMEM((few, side), jnp.int32),
            pltpu.VMEM((count * kinds // side * chans, side * side // kinds), BF16),
            pltpu.VMEM((side, side), F32),
            pltpu.SemaphoreType.DMA,
        ],
        compiler_params=params,
        name="edges",
    )(neighbour_tile, neighbour_edge, gathered, remap_table)

    def swap(value, flip):
        return lax.ppermute(value, "chan", [(i, i ^ flip) for i in range(parts)])

    held = {0: mine}
    bit = parts // 2
    while bit:
        for flip in list(held):
            held[flip ^ bit] = swap(held[flip], bit)
        bit //= 2
    order = tuple(sorted(held))
    filters = conv_weight.transpose(1, 3, 0, 2).reshape(3 * outs, 3 * conv_weight.shape[2])
    all_chans = chans * parts
    return pl.pallas_call(
        functools.partial(tile_kernel, (side, chans, tiles, cap, taps, 16, 8), order),
        out_shape=jax.ShapeDtypeStruct((outs, side, side), BF16),
        in_specs=[ANY] * len(order) + [SMEM, SMEM, VMEM, VMEM],
        out_specs=VMEM,
        scratch_shapes=[
            pltpu.VMEM((count + 4, all_chans, side), BF16),
            pltpu.VMEM(((side + 2) * all_chans, side), BF16),
            pltpu.VMEM((outs, side, side), F32),
            pltpu.SemaphoreType.DMA((len(order),)),
        ],
        compiler_params=params,
        name="tile",
    )(*[held[f].reshape(count + 4, chans, side) for f in order], block_slot, weight_index, remap_table, filters)


def solution(mesh):
    in_specs = (
        P("chan", ("group", "tile")),
        P("tile", None, None),
        P("tile", None),
        P("tile", None),
        P(),
        P("tile", None),
        P("tile", None),
        P(None, None, None, "chan"),
    )
    out_specs = P("chan", ("group", "tile"), None)
    return jax.shard_map(body, mesh=mesh, in_specs=in_specs, out_specs=out_specs, check_vma=False)
```

```python
import functools

import jax
import jax.numpy as jnp
from jax import lax
from jax.experimental import pallas as pl
from jax.experimental.pallas import tpu as pltpu
from jax.sharding import PartitionSpec as P

F32 = jnp.float32
BF16 = jnp.bfloat16
VMEM = pl.BlockSpec(memory_space=pltpu.VMEM)
HBM = pl.BlockSpec(memory_space=pltpu.HBM)
LIMIT = 32 * 2**20
STEP = 16


def round_up(value, step):
    return -(-value // step) * step


def dot(a, b):
    return jnp.dot(a, b, preferred_element_type=F32)


def start_all(sems, pairs):
    copies = [pltpu.make_async_copy(src, dst, sems.at[n]) for n, (src, dst) in enumerate(pairs)]
    for copy in copies:
        copy.start()
    return copies


def pack_kernel(slots_hbm, weights_hbm, lists_hbm, source_hbm, table_hbm, out_ref, table_ref, slots, weights, lists, sems):
    side = out_ref.shape[1]
    chans = source_hbm.shape[0]
    blocks = source_hbm.shape[1] // side
    base = blocks * chans
    copies = start_all(
        sems,
        [(slots_hbm, slots), (weights_hbm, weights), (lists_hbm.at[0], lists)]
        + [
            (source_hbm.at[:, pl.ds(block * side, side)], out_ref.at[pl.ds(block * chans, chans), :])
            for block in range(blocks)
        ]
        + [(table_hbm, table_ref)],
    )
    for copy in copies[:3]:
        copy.wait()
    taps = slots.shape[0]
    tiles, cap = lists.shape
    rows = out_ref.shape[0] - base
    wide = jnp.concatenate([lists[...].astype(F32), jnp.zeros((tiles, side - cap), F32)], axis=1)
    parts = [slots[...].astype(F32), weights[...].astype(F32), wide]
    if rows > 2 * taps + tiles:
        parts.append(jnp.zeros((rows - 2 * taps - tiles, side), F32))
    out_ref[base:, :] = jnp.concatenate(parts, axis=0).astype(BF16)
    for copy in copies[3:]:
        copy.wait()


def edge_kernel(
    dims, neigh_hbm, codes_hbm, gathered_ref, table_ref, out_ref,
    neigh, codes, ints, few_v, few_s, picked, columns, sems,
):
    side, chans, blocks, tiles, cap, taps, rows = dims
    count = tiles * cap
    base = blocks * chans
    kinds = table_ref.shape[0]
    per_group = side // kinds
    me = lax.axis_index("tile")
    scalars = start_all(sems, [(neigh_hbm, neigh), (codes_hbm, codes)])
    for band in range(tiles):
        ints[band * rows : (band + 1) * rows, :] = gathered_ref[band, base:, :].astype(F32).astype(jnp.int32)
    for copy in scalars:
        copy.wait()
    owners = [me] + [neigh[0, s] for s in range(4)]
    for which, owner in enumerate(owners):
        for band in range(tiles):
            few_v[pl.ds(which * tiles + band, 1), :] = ints[pl.ds(band * rows + 2 * taps + owner, 1), :]
    lists_end = 5 * tiles
    for s in range(4):
        for k in range(2 * taps):
            few_v[pl.ds(lists_end + s * 2 * taps + k, 1), :] = ints[pl.ds(owners[s + 1] * rows + k, 1), :]
    copy = pltpu.make_async_copy(few_v, few_s, sems.at[2])
    copy.start()
    lane = lax.broadcasted_iota(jnp.int32, (side, side), 1)
    total = jnp.zeros((side, side), F32)
    for kind in range(kinds):
        moved = pltpu.roll(table_ref[kind].astype(F32), per_group * kind + 1, 1)
        total = jnp.where(lane // per_group == kind, moved, total)
    columns[...] = total
    copy.wait()

    def block_of(which, slot):
        band = slot // cap
        local = few_s[which * tiles + band, slot % cap]
        return gathered_ref[band, pl.ds(pl.multiple_of(local * chans, chans), chans), :]

    for slot in range(count):
        out_ref[slot * chans : (slot + 1) * chans, :] = block_of(0, slot)
    for s in range(4):
        edge = codes[0, s] % 4
        dest = pl.ds((count + s) * chans, chans)

        @pl.when(edge < 2)
        def _():
            at = jnp.where(edge == 0, 0, side - 1)
            acc = jnp.zeros((chans, side), F32)
            for k in range(taps):
                slot = few_s[lists_end + s * 2 * taps + k, at]
                kind = few_s[lists_end + s * 2 * taps + taps + k, at]
                acc = acc + dot(block_of(1 + s, slot), table_ref[kind])
            out_ref[dest, :] = acc.astype(BF16)

        @pl.when(edge >= 2)
        def _():
            for slot in range(count):
                group, member = slot // per_group, slot % per_group
                picked[group * chans : (group + 1) * chans, member * side : (member + 1) * side] = block_of(1 + s, slot)
            col = columns[...]
            col = jnp.where(edge == 2, pltpu.roll(col, side - 1, 1), col)
            col = jnp.where(lane % per_group == 0, col, 0.0)
            spread = jnp.concatenate(
                [col if m == 0 else pltpu.roll(col, m, 1) for m in range(per_group)], axis=0
            ).astype(BF16)
            z = dot(picked[...], spread)
            z_hi = z.astype(BF16)
            z_lo = (z - z_hi.astype(F32)).astype(BF16)
            keys = []
            for k in range(taps):
                slot = few_v[pl.ds(lists_end + s * 2 * taps + k, 1), :]
                kind = few_v[pl.ds(lists_end + s * 2 * taps + taps + k, 1), :]
                keys.append(slot // per_group * side + kind * per_group + slot % per_group)
            acc = jnp.zeros((2 * chans, side), F32)
            for group in range(count // per_group):
                seat = lax.broadcasted_iota(jnp.int32, (side, side), 0) + group * side
                hits = jnp.zeros((side, side), F32)
                for key in keys:
                    hits = hits + jnp.where(seat == key, 1.0, 0.0)
                at = slice(group * chans, (group + 1) * chans)
                acc = acc + dot(jnp.concatenate([z_hi[at], z_lo[at]], axis=0), hits.astype(BF16))
            out_ref[dest, :] = (acc[:chans] + acc[chans:]).astype(BF16)

    row = lax.broadcasted_iota(jnp.int32, (side, side), 0)
    flip = (lane + row == side - 1).astype(BF16)
    plain = out_ref[count * chans :, :]
    turned = dot(plain, flip).astype(BF16)
    for s in range(4):
        at = slice(s * chans, (s + 1) * chans)
        out_ref[(count + s) * chans : (count + s + 1) * chans, :] = jnp.where(codes[0, s] >= 4, turned[at], plain[at])


def tile_kernel(dims, last, many, *refs):
    side, chans, cap, tiles, all_chans, outs = dims
    parts = refs[:many]
    refs = refs[many:]
    if last:
        before_ref, *refs = refs
    slots_hbm, weights_hbm, table_ref, filters_hbm, out_ref, slots, weights, filters, matrix, image, *refs = refs
    if last:
        spread, staged, out_sems, sems = refs
    else:
        (sems,) = refs
    taps = slots.shape[0]
    count = tiles * cap
    half = chans * many
    copies = start_all(sems, [(filters_hbm, filters), (slots_hbm, slots), (weights_hbm, weights)])
    me = lax.axis_index("chan")

    def channels(index):
        return jnp.concatenate([part[index] for part in parts], axis=0)

    copies[0].wait()
    lane = lax.broadcasted_iota(jnp.int32, (outs, all_chans), 1)
    for b in range(3):
        low, high = [], []
        for a in range(3):
            value = filters[a, b].astype(F32)
            width = chans
            bit = 1
            while width < all_chans:
                other = jnp.where(
                    lane // width % 2 == 0, pltpu.roll(value, all_chans - width, 1), pltpu.roll(value, width, 1)
                )
                value = jnp.where((me & bit) != 0, other, value)
                width *= 2
                bit *= 2
            turned = pltpu.roll(value, half, 1)
            low.append(turned if last else value)
            high.append(value if last else turned)
        at = slice(b * outs, (b + 1) * outs)
        matrix[at, :all_chans] = jnp.where(lane < half, low[0], high[1]).astype(BF16)
        matrix[at, all_chans:] = low[2][:, :half].astype(BF16)

    image[0:half, :] = channels(count)
    image[(side + 1) * half :, :] = channels(count + 1)
    wide = lax.broadcasted_iota(jnp.int32, (half, side), 1)

    def around(edge):
        value = channels(count + edge).astype(F32)
        before = jnp.where(wide == 0, 0.0, pltpu.roll(value, 1, 1))
        after = jnp.where(wide == side - 1, 0.0, pltpu.roll(value, side - 1, 1))
        return jnp.concatenate([before, value, after], axis=0).astype(BF16)

    left = dot(matrix[0:outs, :], around(2))
    right = dot(matrix[2 * outs :, :], around(3))
    if last:
        left = left + before_ref[side]
        right = right + before_ref[side + 1]
    else:
        out_ref[side] = left
        out_ref[side + 1] = right
    for copy in copies[1:]:
        copy.wait()

    def remap(r):
        lhs = jnp.concatenate([channels(slots[k, r]) for k in range(taps)], axis=1)
        rhs = jnp.concatenate([table_ref[weights[k, r]] for k in range(taps)], axis=0)
        return dot(lhs, rhs).astype(BF16)

    def place(r, value):
        image[pl.ds(pl.multiple_of((r + 1) * half, half), half), :] = value

    lane = lax.broadcasted_iota(jnp.int32, (outs, side), 1)

    def convolve(first):
        ys = []
        for u in range(0, STEP, 2):
            x0 = image[pl.ds(pl.multiple_of((first + u) * half, half), 3 * half), :]
            x1 = image[pl.ds(pl.multiple_of((first + u + 1) * half, half), 3 * half), :]
            ys.append(dot(matrix[...], jnp.concatenate([x0, x1], axis=1)))
        for u in range(STEP):
            i = first + u
            y = ys[u // 2][:, u % 2 * side : (u % 2 + 1) * side]
            at_left = pltpu.roll(left, lax.rem(side - i, side), 1) if last else 0.0
            at_right = pltpu.roll(right, side - 1 - i, 1) if last else 0.0
            from_left = jnp.where(lane == 0, at_left, pltpu.roll(y[:outs], 1, 1))
            from_right = jnp.where(lane == side - 1, at_right, pltpu.roll(y[2 * outs :], side - 1, 1))
            total = y[outs : 2 * outs] + from_left + from_right
            if last:
                spread[:, u, :] = total + before_ref[i]
            else:
                out_ref[i] = total
        if last:
            rows = pl.ds(pl.multiple_of(first, STEP), STEP)
            staged[:, rows, :] = spread[...].astype(BF16)
            pltpu.make_async_copy(staged.at[:, rows, :], out_ref.at[:, rows, :], out_sems.at[first // STEP]).start()

    for r in range(STEP + 1):
        place(r, remap(r))

    def step(t, carry):
        first = t * STEP
        convolve(first)
        for u in range(STEP):
            r = jnp.minimum(first + STEP + 1 + u, side - 1)
            place(r, remap(r))
        return carry

    lax.fori_loop(0, side // STEP - 1, step, 0)
    convolve(side - STEP)
    if last:
        for t in range(side // STEP):
            rows = pl.ds(t * STEP, STEP)
            pltpu.make_async_copy(staged.at[:, rows, :], out_ref.at[:, rows, :], out_sems.at[t]).wait()


def body(source, send_list, block_slot, weight_index, remap_table, neighbour_tile, neighbour_edge, conv_weight):
    kinds, side = remap_table.shape[:2]
    chans = source.shape[0]
    tiles, cap = send_list.shape[1:]
    taps = block_slot.shape[1]
    blocks = source.shape[1] // side
    count = tiles * cap
    all_chans, outs = conv_weight.shape[2:]
    parts = lax.axis_size("chan")
    rows = round_up(2 * taps + tiles, 16)
    params = pltpu.CompilerParams(vmem_limit_bytes=LIMIT)
    slots, weights = block_slot.T, weight_index.T
    filters = conv_weight.transpose(0, 1, 3, 2)
    packed, table = pl.pallas_call(
        pack_kernel,
        out_shape=[
            jax.ShapeDtypeStruct((blocks * chans + rows, side), BF16),
            jax.ShapeDtypeStruct(remap_table.shape, BF16),
        ],
        in_specs=[HBM] * 5,
        out_specs=[VMEM] * 2,
        scratch_shapes=[
            pltpu.VMEM(slots.shape, jnp.int32),
            pltpu.VMEM(weights.shape, jnp.int32),
            pltpu.VMEM((tiles, cap), jnp.int32),
            pltpu.SemaphoreType.DMA((blocks + 4,)),
        ],
        compiler_params=params,
        name="pack",
    )(slots, weights, send_list, source, remap_table)
    gathered = lax.all_gather(packed, "tile")
    few = 5 * tiles + 4 * 2 * taps
    mine = pl.pallas_call(
        functools.partial(edge_kernel, (side, chans, blocks, tiles, cap, taps, rows)),
        out_shape=jax.ShapeDtypeStruct(((count + 4) * chans, side), BF16),
        in_specs=[HBM, HBM, VMEM, VMEM],
        out_specs=VMEM,
        scratch_shapes=[
            pltpu.SMEM(neighbour_tile.shape, jnp.int32),
            pltpu.SMEM(neighbour_edge.shape, jnp.int32),
            pltpu.VMEM((tiles * rows, side), jnp.int32),
            pltpu.VMEM((few, side), jnp.int32),
            pltpu.SMEM((few, side), jnp.int32),
            pltpu.VMEM((count * kinds // side * chans, side * side // kinds), BF16),
            pltpu.VMEM((side, side), F32),
            pltpu.SemaphoreType.DMA((3,)),
        ],
        compiler_params=params,
        name="edges",
    )(neighbour_tile, neighbour_edge, gathered, table)

    def swap(value, flip):
        return lax.ppermute(value, "chan", [(i, i ^ flip) for i in range(parts)])

    held = {0: mine}
    bit = parts // 2
    while bit:
        for flip in list(held):
            held[flip ^ bit] = swap(held[flip], bit)
        bit //= 2
    many = parts // 2
    half = all_chans // 2
    held = [held[f].reshape(count + 4, chans, side) for f in sorted(held)]
    dims = (side, chans, cap, tiles, all_chans, outs)
    scratch = [
        pltpu.SMEM(slots.shape, jnp.int32),
        pltpu.SMEM(weights.shape, jnp.int32),
        pltpu.VMEM(filters.shape, BF16),
        pltpu.VMEM((3 * outs, 3 * half), BF16),
        pltpu.VMEM(((side + 2) * half, side), BF16),
    ]
    flops = 2 * side * half * taps * side * side + 2 * side * side * 9 * half * outs
    cost = pl.CostEstimate(flops=flops, bytes_accessed=(side + 2) * outs * side * 4, transcendentals=0)
    so_far = pl.pallas_call(
        functools.partial(tile_kernel, dims, False, many),
        out_shape=jax.ShapeDtypeStruct((side + 2, outs, side), F32),
        in_specs=[VMEM] * many + [HBM, HBM, VMEM, HBM],
        out_specs=VMEM,
        scratch_shapes=scratch + [pltpu.SemaphoreType.DMA((3,))],
        compiler_params=params,
        cost_estimate=cost,
        name="near",
    )(*held[:many], slots, weights, table, filters)
    return pl.pallas_call(
        functools.partial(tile_kernel, dims, True, many),
        out_shape=jax.ShapeDtypeStruct((outs, side, side), BF16),
        in_specs=[VMEM] * (many + 1) + [HBM, HBM, VMEM, HBM],
        out_specs=HBM,
        scratch_shapes=scratch
        + [
            pltpu.VMEM((outs, STEP, side), F32),
            pltpu.VMEM((outs, side, side), BF16),
            pltpu.SemaphoreType.DMA((side // STEP,)),
            pltpu.SemaphoreType.DMA((3,)),
        ],
        compiler_params=params,
        cost_estimate=cost,
        name="far",
    )(*held[many:], so_far, slots, weights, table, filters)


def solution(mesh):
    in_specs = (
        P("chan", ("group", "tile")),
        P("tile", None, None),
        P("tile", None),
        P("tile", None),
        P(),
        P("tile", None),
        P("tile", None),
        P(None, None, None, "chan"),
    )
    out_specs = P("chan", ("group", "tile"), None)
    return jax.shard_map(body, mesh=mesh, in_specs=in_specs, out_specs=out_specs, check_vma=False)
```

```python
import functools

import jax
import jax.numpy as jnp
from jax import lax
from jax.experimental import pallas as pl
from jax.experimental.pallas import tpu as pltpu
from jax.sharding import PartitionSpec as P

F32 = jnp.float32
BF16 = jnp.bfloat16
VMEM = pl.BlockSpec(memory_space=pltpu.VMEM)
HBM = pl.BlockSpec(memory_space=pltpu.HBM)
LIMIT = 32 * 2**20
STEP = 16


def round_up(value, step):
    return -(-value // step) * step


def in_hbm(value):
    return pltpu.with_memory_space_constraint(value, pltpu.HBM)


def dot(a, b):
    return jnp.dot(a, b, preferred_element_type=F32)


def start_all(sems, pairs):
    copies = [pltpu.make_async_copy(src, dst, sems.at[n]) for n, (src, dst) in enumerate(pairs)]
    for copy in copies:
        copy.start()
    return copies


def pack_kernel(slots_hbm, weights_hbm, lists_hbm, source_hbm, table_hbm, out_ref, table_ref, slots, weights, lists, sems):
    side = out_ref.shape[1]
    chans = source_hbm.shape[0]
    blocks = source_hbm.shape[1] // side
    base = blocks * chans
    copies = start_all(
        sems,
        [(slots_hbm, slots), (weights_hbm, weights), (lists_hbm.at[0], lists)]
        + [
            (source_hbm.at[:, pl.ds(block * side, side)], out_ref.at[pl.ds(block * chans, chans), :])
            for block in range(blocks)
        ]
        + [(table_hbm, table_ref)],
    )
    for copy in copies[:3]:
        copy.wait()
    taps = slots.shape[0]
    tiles, cap = lists.shape
    rows = out_ref.shape[0] - base
    wide = jnp.concatenate([lists[...].astype(F32), jnp.zeros((tiles, side - cap), F32)], axis=1)
    parts = [slots[...].astype(F32), weights[...].astype(F32), wide]
    if rows > 2 * taps + tiles:
        parts.append(jnp.zeros((rows - 2 * taps - tiles, side), F32))
    out_ref[base:, :] = jnp.concatenate(parts, axis=0).astype(BF16)
    for copy in copies[3:]:
        copy.wait()


def edge_kernel(
    dims, neigh_hbm, codes_hbm, gathered_ref, table_ref, out_ref,
    neigh, codes, ints, few_v, few_s, picked, columns, sems,
):
    side, chans, blocks, tiles, cap, taps, rows = dims
    count = tiles * cap
    base = blocks * chans
    kinds = table_ref.shape[0]
    per_group = side // kinds
    me = lax.axis_index("tile")
    scalars = start_all(sems, [(neigh_hbm, neigh), (codes_hbm, codes)])
    for band in range(tiles):
        ints[band * rows : (band + 1) * rows, :] = gathered_ref[band, base:, :].astype(F32).astype(jnp.int32)
    for copy in scalars:
        copy.wait()
    owners = [me] + [neigh[0, s] for s in range(4)]
    for which, owner in enumerate(owners):
        for band in range(tiles):
            few_v[pl.ds(which * tiles + band, 1), :] = ints[pl.ds(band * rows + 2 * taps + owner, 1), :]
    lists_end = 5 * tiles
    for s in range(4):
        for k in range(2 * taps):
            few_v[pl.ds(lists_end + s * 2 * taps + k, 1), :] = ints[pl.ds(owners[s + 1] * rows + k, 1), :]
    copy = pltpu.make_async_copy(few_v, few_s, sems.at[2])
    copy.start()
    lane = lax.broadcasted_iota(jnp.int32, (side, side), 1)
    total = jnp.zeros((side, side), F32)
    for kind in range(kinds):
        moved = pltpu.roll(table_ref[kind].astype(F32), per_group * kind + 1, 1)
        total = jnp.where(lane // per_group == kind, moved, total)
    columns[...] = total
    copy.wait()

    def block_of(which, slot):
        band = slot // cap
        local = few_s[which * tiles + band, slot % cap]
        return gathered_ref[band, pl.ds(pl.multiple_of(local * chans, chans), chans), :]

    for slot in range(count):
        out_ref[slot * chans : (slot + 1) * chans, :] = block_of(0, slot)
    for s in range(4):
        edge = codes[0, s] % 4
        dest = pl.ds((count + s) * chans, chans)

        @pl.when(edge < 2)
        def _():
            at = jnp.where(edge == 0, 0, side - 1)
            acc = jnp.zeros((chans, side), F32)
            for k in range(taps):
                slot = few_s[lists_end + s * 2 * taps + k, at]
                kind = few_s[lists_end + s * 2 * taps + taps + k, at]
                acc = acc + dot(block_of(1 + s, slot), table_ref[kind])
            out_ref[dest, :] = acc.astype(BF16)

        @pl.when(edge >= 2)
        def _():
            for slot in range(count):
                group, member = slot // per_group, slot % per_group
                picked[group * chans : (group + 1) * chans, member * side : (member + 1) * side] = block_of(1 + s, slot)
            col = columns[...]
            col = jnp.where(edge == 2, pltpu.roll(col, side - 1, 1), col)
            col = jnp.where(lane % per_group == 0, col, 0.0)
            spread = jnp.concatenate(
                [col if m == 0 else pltpu.roll(col, m, 1) for m in range(per_group)], axis=0
            ).astype(BF16)
            z = dot(picked[...], spread)
            z_hi = z.astype(BF16)
            z_lo = (z - z_hi.astype(F32)).astype(BF16)
            keys = []
            for k in range(taps):
                slot = few_v[pl.ds(lists_end + s * 2 * taps + k, 1), :]
                kind = few_v[pl.ds(lists_end + s * 2 * taps + taps + k, 1), :]
                keys.append(slot // per_group * side + kind * per_group + slot % per_group)
            acc = jnp.zeros((2 * chans, side), F32)
            for group in range(count // per_group):
                seat = lax.broadcasted_iota(jnp.int32, (side, side), 0) + group * side
                hits = jnp.zeros((side, side), F32)
                for key in keys:
                    hits = hits + jnp.where(seat == key, 1.0, 0.0)
                at = slice(group * chans, (group + 1) * chans)
                acc = acc + dot(jnp.concatenate([z_hi[at], z_lo[at]], axis=0), hits.astype(BF16))
            out_ref[dest, :] = (acc[:chans] + acc[chans:]).astype(BF16)

    row = lax.broadcasted_iota(jnp.int32, (side, side), 0)
    flip = (lane + row == side - 1).astype(BF16)
    plain = out_ref[count * chans :, :]
    turned = dot(plain, flip).astype(BF16)
    for s in range(4):
        at = slice(s * chans, (s + 1) * chans)
        out_ref[(count + s) * chans : (count + s + 1) * chans, :] = jnp.where(codes[0, s] >= 4, turned[at], plain[at])


def tile_kernel(dims, last, many, *refs):
    side, chans, cap, tiles, all_chans, outs = dims
    parts = refs[:many]
    refs = refs[many:]
    if last:
        before_ref, *refs = refs
    slots_hbm, weights_hbm, table_ref, filters_hbm, out_ref, slots, weights, filters, matrix, image, *refs = refs
    if last:
        spread, staged, out_sems, sems = refs
    else:
        (sems,) = refs
    taps = slots.shape[0]
    count = tiles * cap
    half = chans * many
    copies = start_all(sems, [(filters_hbm, filters), (slots_hbm, slots), (weights_hbm, weights)])
    me = lax.axis_index("chan")

    def channels(index):
        return jnp.concatenate([part[index] for part in parts], axis=0)

    copies[0].wait()
    lane = lax.broadcasted_iota(jnp.int32, (outs, all_chans), 1)
    for b in range(3):
        low, high = [], []
        for a in range(3):
            value = filters[a, b].astype(F32)
            width = chans
            bit = 1
            while width < all_chans:
                other = jnp.where(
                    lane // width % 2 == 0, pltpu.roll(value, all_chans - width, 1), pltpu.roll(value, width, 1)
                )
                value = jnp.where((me & bit) != 0, other, value)
                width *= 2
                bit *= 2
            turned = pltpu.roll(value, half, 1)
            low.append(turned if last else value)
            high.append(value if last else turned)
        at = slice(b * outs, (b + 1) * outs)
        matrix[at, :all_chans] = jnp.where(lane < half, low[0], high[1]).astype(BF16)
        matrix[at, all_chans:] = low[2][:, :half].astype(BF16)

    image[0:half, :] = channels(count)
    image[(side + 1) * half :, :] = channels(count + 1)
    wide = lax.broadcasted_iota(jnp.int32, (half, side), 1)

    def around(edge):
        value = channels(count + edge).astype(F32)
        before = jnp.where(wide == 0, 0.0, pltpu.roll(value, 1, 1))
        after = jnp.where(wide == side - 1, 0.0, pltpu.roll(value, side - 1, 1))
        return jnp.concatenate([before, value, after], axis=0).astype(BF16)

    left = dot(matrix[0:outs, :], around(2))
    right = dot(matrix[2 * outs :, :], around(3))
    if last:
        left = left + before_ref[side]
        right = right + before_ref[side + 1]
    else:
        out_ref[side] = left
        out_ref[side + 1] = right
    for copy in copies[1:]:
        copy.wait()

    def remap(r):
        lhs = jnp.concatenate([channels(slots[k, r]) for k in range(taps)], axis=1)
        rhs = jnp.concatenate([table_ref[weights[k, r]] for k in range(taps)], axis=0)
        return dot(lhs, rhs).astype(BF16)

    def place(r, value):
        image[pl.ds(pl.multiple_of((r + 1) * half, half), half), :] = value

    lane = lax.broadcasted_iota(jnp.int32, (outs, side), 1)

    def convolve(first):
        ys = []
        for u in range(0, STEP, 2):
            x0 = image[pl.ds(pl.multiple_of((first + u) * half, half), 3 * half), :]
            x1 = image[pl.ds(pl.multiple_of((first + u + 1) * half, half), 3 * half), :]
            ys.append(dot(matrix[...], jnp.concatenate([x0, x1], axis=1)))
        for u in range(STEP):
            i = first + u
            y = ys[u // 2][:, u % 2 * side : (u % 2 + 1) * side]
            at_left = pltpu.roll(left, lax.rem(side - i, side), 1) if last else 0.0
            at_right = pltpu.roll(right, side - 1 - i, 1) if last else 0.0
            from_left = jnp.where(lane == 0, at_left, pltpu.roll(y[:outs], 1, 1))
            from_right = jnp.where(lane == side - 1, at_right, pltpu.roll(y[2 * outs :], side - 1, 1))
            total = y[outs : 2 * outs] + from_left + from_right
            if last:
                spread[pl.ds(u * (outs + 1), outs), :] = total + before_ref[i]
            else:
                out_ref[i] = total
        if last:
            rows = pl.ds(pl.multiple_of(first, STEP), STEP)
            for o in range(outs):
                staged[o, rows, :] = spread[pl.ds(o, STEP, stride=outs + 1), :].astype(BF16)
            pltpu.make_async_copy(staged.at[:, rows, :], out_ref.at[:, rows, :], out_sems.at[first // STEP]).start()

    for r in range(STEP + 1):
        place(r, remap(r))

    def step(t, carry):
        first = t * STEP
        convolve(first)
        for u in range(STEP):
            r = jnp.minimum(first + STEP + 1 + u, side - 1)
            place(r, remap(r))
        return carry

    lax.fori_loop(0, side // STEP - 1, step, 0)
    convolve(side - STEP)
    if last:
        for t in range(side // STEP):
            rows = pl.ds(t * STEP, STEP)
            pltpu.make_async_copy(staged.at[:, rows, :], out_ref.at[:, rows, :], out_sems.at[t]).wait()


def body(source, send_list, block_slot, weight_index, remap_table, neighbour_tile, neighbour_edge, conv_weight):
    kinds, side = remap_table.shape[:2]
    chans = source.shape[0]
    tiles, cap = send_list.shape[1:]
    taps = block_slot.shape[1]
    blocks = source.shape[1] // side
    count = tiles * cap
    all_chans, outs = conv_weight.shape[2:]
    parts = lax.axis_size("chan")
    rows = round_up(2 * taps + tiles, 16)
    params = pltpu.CompilerParams(vmem_limit_bytes=LIMIT)
    slots, weights = in_hbm(block_slot.T), in_hbm(weight_index.T)
    filters = in_hbm(conv_weight.transpose(0, 1, 3, 2))
    packed, table = pl.pallas_call(
        pack_kernel,
        out_shape=[
            jax.ShapeDtypeStruct((blocks * chans + rows, side), BF16),
            jax.ShapeDtypeStruct(remap_table.shape, BF16),
        ],
        in_specs=[HBM] * 5,
        out_specs=[VMEM] * 2,
        scratch_shapes=[
            pltpu.VMEM(slots.shape, jnp.int32),
            pltpu.VMEM(weights.shape, jnp.int32),
            pltpu.VMEM((tiles, cap), jnp.int32),
            pltpu.SemaphoreType.DMA((blocks + 4,)),
        ],
        compiler_params=params,
        name="pack",
    )(slots, weights, in_hbm(send_list), in_hbm(source), in_hbm(remap_table))
    gathered = lax.all_gather(packed, "tile")
    few = 5 * tiles + 4 * 2 * taps
    mine = pl.pallas_call(
        functools.partial(edge_kernel, (side, chans, blocks, tiles, cap, taps, rows)),
        out_shape=jax.ShapeDtypeStruct(((count + 4) * chans, side), BF16),
        in_specs=[HBM, HBM, VMEM, VMEM],
        out_specs=VMEM,
        scratch_shapes=[
            pltpu.SMEM(neighbour_tile.shape, jnp.int32),
            pltpu.SMEM(neighbour_edge.shape, jnp.int32),
            pltpu.VMEM((tiles * rows, side), jnp.int32),
            pltpu.VMEM((few, side), jnp.int32),
            pltpu.SMEM((few, side), jnp.int32),
            pltpu.VMEM((count * kinds // side * chans, side * side // kinds), BF16),
            pltpu.VMEM((side, side), F32),
            pltpu.SemaphoreType.DMA((3,)),
        ],
        compiler_params=params,
        name="edges",
    )(in_hbm(neighbour_tile), in_hbm(neighbour_edge), gathered, table)

    def swap(value, flip):
        return lax.ppermute(value, "chan", [(i, i ^ flip) for i in range(parts)])

    def spread(held, bit):
        while bit:
            for flip in list(held):
                held[flip ^ bit] = swap(held[flip], bit)
            bit //= 2
        return [held[f].reshape(count + 4, chans, side) for f in sorted(held)]

    many = parts // 2
    half = all_chans // 2
    near = spread({0: mine}, many // 2)
    mine, *near = lax.optimization_barrier((mine, *near))
    across = swap(mine, many)
    dims = (side, chans, cap, tiles, all_chans, outs)
    scratch = [
        pltpu.SMEM(slots.shape, jnp.int32),
        pltpu.SMEM(weights.shape, jnp.int32),
        pltpu.VMEM(filters.shape, BF16),
        pltpu.VMEM((3 * outs, 3 * half), BF16),
        pltpu.VMEM(((side + 2) * half, side), BF16),
    ]
    flops = 2 * side * half * taps * side * side + 2 * side * side * 9 * half * outs
    cost = pl.CostEstimate(flops=flops, bytes_accessed=(side + 2) * outs * side * 4, transcendentals=0)
    so_far = pl.pallas_call(
        functools.partial(tile_kernel, dims, False, many),
        out_shape=jax.ShapeDtypeStruct((side + 2, outs, side), F32),
        in_specs=[VMEM] * many + [HBM, HBM, VMEM, HBM],
        out_specs=VMEM,
        scratch_shapes=scratch + [pltpu.SemaphoreType.DMA((3,))],
        compiler_params=params,
        cost_estimate=cost,
        name="near",
    )(*near, slots, weights, table, filters)
    across, so_far = lax.optimization_barrier((across, so_far))
    far = spread({many: across}, many // 2)
    return pl.pallas_call(
        functools.partial(tile_kernel, dims, True, many),
        out_shape=jax.ShapeDtypeStruct((outs, side, side), BF16),
        in_specs=[VMEM] * (many + 1) + [HBM, HBM, VMEM, HBM],
        out_specs=HBM,
        scratch_shapes=scratch
        + [
            pltpu.VMEM((round_up(STEP * (outs + 1), 8), side), F32),
            pltpu.VMEM((outs, side, side), BF16),
            pltpu.SemaphoreType.DMA((side // STEP,)),
            pltpu.SemaphoreType.DMA((3,)),
        ],
        compiler_params=params,
        cost_estimate=cost,
        name="far",
    )(*far, so_far, slots, weights, table, filters)


def solution(mesh):
    in_specs = (
        P("chan", ("group", "tile")),
        P("tile", None, None),
        P("tile", None),
        P("tile", None),
        P(),
        P("tile", None),
        P("tile", None),
        P(None, None, None, "chan"),
    )
    out_specs = P("chan", ("group", "tile"), None)
    return jax.shard_map(body, mesh=mesh, in_specs=in_specs, out_specs=out_specs, check_vma=False)
```

```python
import functools

import jax
import jax.numpy as jnp
from jax import lax
from jax.experimental import pallas as pl
from jax.experimental.pallas import tpu as pltpu
from jax.sharding import PartitionSpec as P

F32 = jnp.float32
BF16 = jnp.bfloat16
VMEM = pl.BlockSpec(memory_space=pltpu.VMEM)
HBM = pl.BlockSpec(memory_space=pltpu.HBM)
LIMIT = 32 * 2**20
STEP = 16


def round_up(value, step):
    return -(-value // step) * step


def in_hbm(value):
    return pltpu.with_memory_space_constraint(value, pltpu.HBM)


def dot(a, b):
    return jnp.dot(a, b, preferred_element_type=F32)


def start_all(sems, pairs):
    copies = [pltpu.make_async_copy(src, dst, sems.at[n]) for n, (src, dst) in enumerate(pairs)]
    for copy in copies:
        copy.start()
    return copies


def pack_kernel(
    slots_hbm, weights_hbm, lists_hbm, neigh_hbm, codes_hbm, source_hbm, table_hbm, filters_hbm,
    out_ref, slots, weights, table_ref, filters, lists, neigh, codes, sems,
):
    side = out_ref.shape[1]
    chans = source_hbm.shape[0]
    blocks = source_hbm.shape[1] // side
    base = blocks * chans
    copies = start_all(
        sems,
        [(slots_hbm, slots), (weights_hbm, weights), (lists_hbm.at[0], lists), (neigh_hbm, neigh), (codes_hbm, codes)]
        + [
            (source_hbm.at[:, pl.ds(block * side, side)], out_ref.at[pl.ds(block * chans, chans), :])
            for block in range(blocks)
        ]
        + [(table_hbm, table_ref), (filters_hbm, filters)],
    )
    for copy in copies[:5]:
        copy.wait()
    taps = slots.shape[0]
    tiles, cap = lists.shape
    rows = out_ref.shape[0] - base
    sides = jnp.concatenate([neigh[...], codes[...]], axis=1).astype(F32)
    wide = jnp.concatenate(
        [
            lists[...].astype(F32),
            jnp.concatenate([sides, jnp.zeros((tiles - 1, sides.shape[1]), F32)], axis=0),
            jnp.zeros((tiles, side - cap - sides.shape[1]), F32),
        ],
        axis=1,
    )
    parts = [slots[...].astype(F32), weights[...].astype(F32), wide]
    if rows > 2 * taps + tiles:
        parts.append(jnp.zeros((rows - 2 * taps - tiles, side), F32))
    out_ref[base:, :] = jnp.concatenate(parts, axis=0).astype(BF16)
    for copy in copies[5:]:
        copy.wait()


def edge_kernel(dims, gathered_ref, table_ref, out_ref, ints, scalars, picked, columns, sem):
    side, chans, blocks, tiles, cap, taps, rows = dims
    count = tiles * cap
    base = blocks * chans
    kinds = table_ref.shape[0]
    per_group = side // kinds
    me = lax.axis_index("tile")
    for band in range(tiles):
        ints[band * rows : (band + 1) * rows, :] = gathered_ref[band, base:, :].astype(F32).astype(jnp.int32)
    copy = pltpu.make_async_copy(ints, scalars, sem)
    copy.start()
    lane = lax.broadcasted_iota(jnp.int32, (side, side), 1)
    total = jnp.zeros((side, side), F32)
    for kind in range(kinds):
        moved = pltpu.roll(table_ref[kind].astype(F32), per_group * kind + 1, 1)
        total = jnp.where(lane // per_group == kind, moved, total)
    columns[...] = total
    copy.wait()
    own_row = me * rows + 2 * taps
    neigh = [scalars[own_row, cap + s] for s in range(4)]
    codes = [scalars[own_row, cap + 4 + s] for s in range(4)]

    def block_of(owner, slot):
        band = slot // cap
        local = scalars[band * rows + 2 * taps + owner, slot % cap]
        return gathered_ref[band, pl.ds(pl.multiple_of(local * chans, chans), chans), :]

    for slot in range(count):
        out_ref[slot * chans : (slot + 1) * chans, :] = block_of(me, slot)
    for s in range(4):
        owner = neigh[s]
        edge = codes[s] % 4
        dest = pl.ds((count + s) * chans, chans)

        @pl.when(edge < 2)
        def _():
            at = jnp.where(edge == 0, 0, side - 1)
            acc = jnp.zeros((chans, side), F32)
            for k in range(taps):
                slot = scalars[owner * rows + k, at]
                kind = scalars[owner * rows + taps + k, at]
                acc = acc + dot(block_of(owner, slot), table_ref[kind])
            out_ref[dest, :] = acc.astype(BF16)

        @pl.when(edge >= 2)
        def _():
            for slot in range(count):
                group, member = slot // per_group, slot % per_group
                picked[group * chans : (group + 1) * chans, member * side : (member + 1) * side] = block_of(owner, slot)
            col = columns[...]
            col = jnp.where(edge == 2, pltpu.roll(col, side - 1, 1), col)
            col = jnp.where(lane % per_group == 0, col, 0.0)
            spread = jnp.concatenate(
                [col if m == 0 else pltpu.roll(col, m, 1) for m in range(per_group)], axis=0
            ).astype(BF16)
            z = dot(picked[...], spread)
            z_hi = z.astype(BF16)
            z_lo = (z - z_hi.astype(F32)).astype(BF16)
            keys = []
            for k in range(taps):
                slot = ints[pl.ds(owner * rows + k, 1), :]
                kind = ints[pl.ds(owner * rows + taps + k, 1), :]
                keys.append(slot // per_group * side + kind * per_group + slot % per_group)
            acc = jnp.zeros((2 * chans, side), F32)
            for group in range(count // per_group):
                seat = lax.broadcasted_iota(jnp.int32, (side, side), 0) + group * side
                hits = jnp.zeros((side, side), F32)
                for key in keys:
                    hits = hits + jnp.where(seat == key, 1.0, 0.0)
                at = slice(group * chans, (group + 1) * chans)
                acc = acc + dot(jnp.concatenate([z_hi[at], z_lo[at]], axis=0), hits.astype(BF16))
            out_ref[dest, :] = (acc[:chans] + acc[chans:]).astype(BF16)

    row = lax.broadcasted_iota(jnp.int32, (side, side), 0)
    flip = (lane + row == side - 1).astype(BF16)
    plain = out_ref[count * chans :, :]
    turned = dot(plain, flip).astype(BF16)
    for s in range(4):
        at = slice(s * chans, (s + 1) * chans)
        out_ref[(count + s) * chans : (count + s + 1) * chans, :] = jnp.where(codes[s] >= 4, turned[at], plain[at])


def filter_kernel(chans, filters, near_ref, far_ref):
    outs, all_chans = filters.shape[2:]
    half = all_chans // 2
    me = lax.axis_index("chan")
    lane = lax.broadcasted_iota(jnp.int32, (outs, all_chans), 1)
    for b in range(3):
        first, second = [], []
        for a in range(3):
            value = filters[a, b].astype(F32)
            width = chans
            bit = 1
            while width < all_chans:
                other = jnp.where(
                    lane // width % 2 == 0, pltpu.roll(value, all_chans - width, 1), pltpu.roll(value, width, 1)
                )
                value = jnp.where((me & bit) != 0, other, value)
                width *= 2
                bit *= 2
            first.append(value)
            second.append(pltpu.roll(value, half, 1))
        at = slice(b * outs, (b + 1) * outs)
        near_ref[at, :all_chans] = jnp.where(lane < half, first[0], second[1]).astype(BF16)
        near_ref[at, all_chans:] = first[2][:, :half].astype(BF16)
        far_ref[at, :all_chans] = jnp.where(lane < half, second[0], first[1]).astype(BF16)
        far_ref[at, all_chans:] = second[2][:, :half].astype(BF16)


def tile_kernel(dims, last, many, *refs):
    side, chans, cap, tiles, all_chans, outs = dims
    parts = refs[:many]
    refs = refs[many:]
    if last:
        before_ref, *refs = refs
    slots_ref, weights_ref, table_ref, matrix, out_ref, slots, weights, image, *refs = refs
    if last:
        spread, staged, out_sems, sems = refs
    else:
        (sems,) = refs
    taps = slots.shape[0]
    count = tiles * cap
    half = chans * many
    copies = start_all(sems, [(slots_ref, slots), (weights_ref, weights)])

    def channels(index):
        return jnp.concatenate([part[index] for part in parts], axis=0)

    image[0:half, :] = channels(count)
    image[(side + 1) * half :, :] = channels(count + 1)
    wide = lax.broadcasted_iota(jnp.int32, (half, side), 1)

    def around(edge):
        value = channels(count + edge).astype(F32)
        before = jnp.where(wide == 0, 0.0, pltpu.roll(value, 1, 1))
        after = jnp.where(wide == side - 1, 0.0, pltpu.roll(value, side - 1, 1))
        return jnp.concatenate([before, value, after], axis=0).astype(BF16)

    left = dot(matrix[0:outs, :], around(2))
    right = dot(matrix[2 * outs :, :], around(3))
    if last:
        left = left + before_ref[side]
        right = right + before_ref[side + 1]
    else:
        out_ref[side] = left
        out_ref[side + 1] = right
    for copy in copies:
        copy.wait()

    def remap(r):
        lhs = jnp.concatenate([channels(slots[k, r]) for k in range(taps)], axis=1)
        rhs = jnp.concatenate([table_ref[weights[k, r]] for k in range(taps)], axis=0)
        return dot(lhs, rhs).astype(BF16)

    def place(r, value):
        image[pl.ds(pl.multiple_of((r + 1) * half, half), half), :] = value

    lane = lax.broadcasted_iota(jnp.int32, (outs, side), 1)

    def convolve(first):
        ys = []
        for u in range(0, STEP, 2):
            x0 = image[pl.ds(pl.multiple_of((first + u) * half, half), 3 * half), :]
            x1 = image[pl.ds(pl.multiple_of((first + u + 1) * half, half), 3 * half), :]
            ys.append(dot(matrix[...], jnp.concatenate([x0, x1], axis=1)))
        for u in range(STEP):
            i = first + u
            y = ys[u // 2][:, u % 2 * side : (u % 2 + 1) * side]
            at_left = pltpu.roll(left, lax.rem(side - i, side), 1) if last else 0.0
            at_right = pltpu.roll(right, side - 1 - i, 1) if last else 0.0
            from_left = jnp.where(lane == 0, at_left, pltpu.roll(y[:outs], 1, 1))
            from_right = jnp.where(lane == side - 1, at_right, pltpu.roll(y[2 * outs :], side - 1, 1))
            total = y[outs : 2 * outs] + from_left + from_right
            if last:
                spread[pl.ds(u * (outs + 1), outs), :] = total + before_ref[i]
            else:
                out_ref[i] = total
        if last:
            rows = pl.ds(pl.multiple_of(first, STEP), STEP)
            for o in range(outs):
                staged[o, rows, :] = spread[pl.ds(o, STEP, stride=outs + 1), :].astype(BF16)
            pltpu.make_async_copy(staged.at[:, rows, :], out_ref.at[:, rows, :], out_sems.at[first // STEP]).start()

    for r in range(STEP + 1):
        place(r, remap(r))

    def step(t, carry):
        first = t * STEP
        convolve(first)
        for u in range(STEP):
            r = jnp.minimum(first + STEP + 1 + u, side - 1)
            place(r, remap(r))
        return carry

    lax.fori_loop(0, side // STEP - 1, step, 0)
    convolve(side - STEP)
    if last:
        for t in range(side // STEP):
            rows = pl.ds(t * STEP, STEP)
            pltpu.make_async_copy(staged.at[:, rows, :], out_ref.at[:, rows, :], out_sems.at[t]).wait()


def body(source, send_list, block_slot, weight_index, remap_table, neighbour_tile, neighbour_edge, conv_weight):
    kinds, side = remap_table.shape[:2]
    chans = source.shape[0]
    tiles, cap = send_list.shape[1:]
    taps = block_slot.shape[1]
    blocks = source.shape[1] // side
    count = tiles * cap
    all_chans, outs = conv_weight.shape[2:]
    parts = lax.axis_size("chan")
    rows = round_up(2 * taps + tiles, 16)
    params = pltpu.CompilerParams(vmem_limit_bytes=LIMIT)
    slots, weights = in_hbm(block_slot.T), in_hbm(weight_index.T)
    filters = in_hbm(conv_weight.transpose(0, 1, 3, 2))
    packed, slots, weights, table, filters = pl.pallas_call(
        pack_kernel,
        out_shape=[
            jax.ShapeDtypeStruct((blocks * chans + rows, side), BF16),
            jax.ShapeDtypeStruct(slots.shape, jnp.int32),
            jax.ShapeDtypeStruct(weights.shape, jnp.int32),
            jax.ShapeDtypeStruct(remap_table.shape, BF16),
            jax.ShapeDtypeStruct(filters.shape, BF16),
        ],
        in_specs=[HBM] * 8,
        out_specs=[VMEM] * 5,
        scratch_shapes=[
            pltpu.VMEM((tiles, cap), jnp.int32),
            pltpu.VMEM(neighbour_tile.shape, jnp.int32),
            pltpu.VMEM(neighbour_edge.shape, jnp.int32),
            pltpu.SemaphoreType.DMA((blocks + 7,)),
        ],
        compiler_params=params,
        name="pack",
    )(
        slots, weights, in_hbm(send_list), in_hbm(neighbour_tile), in_hbm(neighbour_edge), in_hbm(source),
        in_hbm(remap_table), filters,
    )
    gathered = lax.all_gather(packed, "tile")
    mine = pl.pallas_call(
        functools.partial(edge_kernel, (side, chans, blocks, tiles, cap, taps, rows)),
        out_shape=jax.ShapeDtypeStruct(((count + 4) * chans, side), BF16),
        in_specs=[VMEM, VMEM],
        out_specs=VMEM,
        scratch_shapes=[
            pltpu.VMEM((tiles * rows, side), jnp.int32),
            pltpu.SMEM((tiles * rows, side), jnp.int32),
            pltpu.VMEM((count * kinds // side * chans, side * side // kinds), BF16),
            pltpu.VMEM((side, side), F32),
            pltpu.SemaphoreType.DMA,
        ],
        compiler_params=params,
        name="edges",
    )(gathered, table)

    def swap(value, flip):
        return lax.ppermute(value, "chan", [(i, i ^ flip) for i in range(parts)])

    def spread(held, bit):
        while bit:
            for flip in list(held):
                held[flip ^ bit] = swap(held[flip], bit)
            bit //= 2
        return [held[f].reshape(count + 4, chans, side) for f in sorted(held)]

    many = parts // 2
    half = all_chans // 2
    mine, filters = lax.optimization_barrier((mine, filters))
    near = spread({0: mine}, many // 2)
    near_filters, far_filters = pl.pallas_call(
        functools.partial(filter_kernel, chans),
        out_shape=[jax.ShapeDtypeStruct((3 * outs, 3 * half), BF16)] * 2,
        in_specs=[VMEM],
        out_specs=[VMEM] * 2,
        compiler_params=params,
        name="filters",
    )(filters)
    mine, near_filters = lax.optimization_barrier((mine, near_filters))
    across = swap(mine, many)
    dims = (side, chans, cap, tiles, all_chans, outs)
    scratch = [
        pltpu.SMEM(slots.shape, jnp.int32),
        pltpu.SMEM(weights.shape, jnp.int32),
        pltpu.VMEM(((side + 2) * half, side), BF16),
    ]
    flops = 2 * side * half * taps * side * side + 2 * side * side * 9 * half * outs
    cost = pl.CostEstimate(flops=flops, bytes_accessed=(side + 2) * outs * side * 4, transcendentals=0)
    so_far = pl.pallas_call(
        functools.partial(tile_kernel, dims, False, many),
        out_shape=jax.ShapeDtypeStruct((side + 2, outs, side), F32),
        in_specs=[VMEM] * (many + 4),
        out_specs=VMEM,
        scratch_shapes=scratch + [pltpu.SemaphoreType.DMA((2,))],
        compiler_params=params,
        cost_estimate=cost,
        name="near",
    )(*near, slots, weights, table, near_filters)
    across, so_far = lax.optimization_barrier((across, so_far))
    far = spread({many: across}, many // 2)
    return pl.pallas_call(
        functools.partial(tile_kernel, dims, True, many),
        out_shape=jax.ShapeDtypeStruct((outs, side, side), BF16),
        in_specs=[VMEM] * (many + 5),
        out_specs=HBM,
        scratch_shapes=scratch
        + [
            pltpu.VMEM((round_up(STEP * (outs + 1), 8), side), F32),
            pltpu.VMEM((outs, side, side), BF16),
            pltpu.SemaphoreType.DMA((side // STEP,)),
            pltpu.SemaphoreType.DMA((2,)),
        ],
        compiler_params=params,
        cost_estimate=cost,
        name="far",
    )(*far, so_far, slots, weights, table, far_filters)


def solution(mesh):
    in_specs = (
        P("chan", ("group", "tile")),
        P("tile", None, None),
        P("tile", None),
        P("tile", None),
        P(),
        P("tile", None),
        P("tile", None),
        P(None, None, None, "chan"),
    )
    out_specs = P("chan", ("group", "tile"), None)
    return jax.shard_map(body, mesh=mesh, in_specs=in_specs, out_specs=out_specs, check_vma=False)
```

```python
import functools

import jax
import jax.numpy as jnp
from jax import lax
from jax.experimental import pallas as pl
from jax.experimental.pallas import tpu as pltpu
from jax.sharding import PartitionSpec as P

F32 = jnp.float32
BF16 = jnp.bfloat16
VMEM = pl.BlockSpec(memory_space=pltpu.VMEM)
HBM = pl.BlockSpec(memory_space=pltpu.HBM)
LIMIT = 32 * 2**20
STEP = 16


def round_up(value, step):
    return -(-value // step) * step


def in_hbm(value):
    return pltpu.with_memory_space_constraint(value, pltpu.HBM)


def dot(a, b):
    return jnp.dot(a, b, preferred_element_type=F32)


def start_all(sems, pairs):
    copies = [pltpu.make_async_copy(src, dst, sems.at[n]) for n, (src, dst) in enumerate(pairs)]
    for copy in copies:
        copy.start()
    return copies


def pack_kernel(
    slots_hbm, weights_hbm, lists_hbm, neigh_hbm, codes_hbm, source_hbm, table_hbm, filters_hbm,
    out_ref, slots, weights, table_ref, filters, lists, neigh, codes, sems,
):
    side = out_ref.shape[1]
    chans = source_hbm.shape[0]
    blocks = source_hbm.shape[1] // side
    base = blocks * chans
    copies = start_all(
        sems,
        [(slots_hbm, slots), (weights_hbm, weights), (lists_hbm.at[0], lists), (neigh_hbm, neigh), (codes_hbm, codes)]
        + [
            (source_hbm.at[:, pl.ds(block * side, side)], out_ref.at[pl.ds(block * chans, chans), :])
            for block in range(blocks)
        ]
        + [(table_hbm, table_ref), (filters_hbm, filters)],
    )
    for copy in copies[:5]:
        copy.wait()
    taps = slots.shape[0]
    tiles, cap = lists.shape
    rows = out_ref.shape[0] - base
    sides = jnp.concatenate([neigh[...], codes[...]], axis=1).astype(F32)
    wide = jnp.concatenate(
        [
            lists[...].astype(F32),
            jnp.concatenate([sides, jnp.zeros((tiles - 1, sides.shape[1]), F32)], axis=0),
            jnp.zeros((tiles, side - cap - sides.shape[1]), F32),
        ],
        axis=1,
    )
    parts = [slots[...].astype(F32), weights[...].astype(F32), wide]
    if rows > 2 * taps + tiles:
        parts.append(jnp.zeros((rows - 2 * taps - tiles, side), F32))
    out_ref[base:, :] = jnp.concatenate(parts, axis=0).astype(BF16)
    for copy in copies[5:]:
        copy.wait()


def edge_kernel(dims, gathered_ref, table_ref, out_ref, ints, scalars, picked, columns, sem):
    side, chans, blocks, tiles, cap, taps, rows = dims
    count = tiles * cap
    base = blocks * chans
    kinds = table_ref.shape[0]
    per_group = side // kinds
    me = lax.axis_index("tile")
    tables = jnp.concatenate([gathered_ref[band, base:, :] for band in range(tiles)], axis=0)
    ints[: tiles * rows, :] = tables.astype(F32).astype(jnp.int32)
    copy = pltpu.make_async_copy(ints.at[pl.ds(0, tiles * rows), :], scalars, sem)
    copy.start()
    row = lax.broadcasted_iota(jnp.int32, (side, side), 0)
    flip = (lax.broadcasted_iota(jnp.int32, (side, side), 1) + row == side - 1).astype(BF16)
    ints[tiles * rows :, :] = dot(tables, flip).astype(jnp.int32)
    lane = lax.broadcasted_iota(jnp.int32, (side, side), 1)
    total = jnp.zeros((side, side), F32)
    for kind in range(kinds):
        moved = pltpu.roll(table_ref[kind].astype(F32), per_group * kind + 1, 1)
        total = jnp.where(lane // per_group == kind, moved, total)
    columns[...] = total
    copy.wait()
    own_row = me * rows + 2 * taps
    neigh = [scalars[own_row, cap + s] for s in range(4)]
    codes = [scalars[own_row, cap + 4 + s] for s in range(4)]

    def block_of(owner, slot):
        band = slot // cap
        local = scalars[band * rows + 2 * taps + owner, slot % cap]
        return gathered_ref[band, pl.ds(pl.multiple_of(local * chans, chans), chans), :]

    for slot in range(count):
        out_ref[slot * chans : (slot + 1) * chans, :] = block_of(me, slot)
    for s in range(4):
        owner = neigh[s]
        edge = codes[s] % 4
        dest = pl.ds((count + s) * chans, chans)

        @pl.when(edge < 2)
        def _():
            at = jnp.where(edge == 0, 0, side - 1)
            acc = jnp.zeros((chans, side), F32)
            for k in range(taps):
                slot = scalars[owner * rows + k, at]
                kind = scalars[owner * rows + taps + k, at]
                acc = acc + dot(block_of(owner, slot), table_ref[kind])
            out_ref[dest, :] = acc.astype(BF16)

            @pl.when(codes[s] >= 4)
            def _():
                out_ref[dest, :] = dot(acc.astype(BF16), flip).astype(BF16)

        @pl.when(edge >= 2)
        def _():
            for slot in range(count):
                group, member = slot // per_group, slot % per_group
                picked[group * chans : (group + 1) * chans, member * side : (member + 1) * side] = block_of(owner, slot)
            col = columns[...]
            col = jnp.where(edge == 2, pltpu.roll(col, side - 1, 1), col)
            col = jnp.where(lane % per_group == 0, col, 0.0)
            spread = jnp.concatenate(
                [col if m == 0 else pltpu.roll(col, m, 1) for m in range(per_group)], axis=0
            ).astype(BF16)
            z = dot(picked[...], spread)
            z_hi = z.astype(BF16)
            z_lo = (z - z_hi.astype(F32)).astype(BF16)
            first = owner * rows + jnp.where(codes[s] >= 4, tiles * rows, 0)
            slots = ints[pl.ds(first, taps), :]
            inside = slots % per_group + ints[pl.ds(first + taps, taps), :] * per_group
            spots = [jnp.where(row == inside[k : k + 1], 1.0, 0.0).astype(BF16) for k in range(taps)]
            acc = jnp.zeros((2 * chans, side), F32)
            for group in range(count // per_group):
                here = jnp.where(slots // per_group == group, 1.0, 0.0).astype(BF16)
                hits = sum(spots[k] * here[k : k + 1] for k in range(taps))
                at = slice(group * chans, (group + 1) * chans)
                acc = acc + dot(jnp.concatenate([z_hi[at], z_lo[at]], axis=0), hits)
            out_ref[dest, :] = (acc[:chans] + acc[chans:]).astype(BF16)


def filter_kernel(chans, filters, near_ref, far_ref):
    outs, all_chans = filters.shape[2:]
    half = all_chans // 2
    me = lax.axis_index("chan")
    lane = lax.broadcasted_iota(jnp.int32, (outs, all_chans), 1)
    for b in range(3):
        first, second = [], []
        for a in range(3):
            value = filters[a, b].astype(F32)
            width = chans
            bit = 1
            while width < all_chans:
                other = jnp.where(
                    lane // width % 2 == 0, pltpu.roll(value, all_chans - width, 1), pltpu.roll(value, width, 1)
                )
                value = jnp.where((me & bit) != 0, other, value)
                width *= 2
                bit *= 2
            first.append(value)
            second.append(pltpu.roll(value, half, 1))
        at = slice(b * outs, (b + 1) * outs)
        near_ref[at, :all_chans] = jnp.where(lane < half, first[0], second[1]).astype(BF16)
        near_ref[at, all_chans:] = first[2][:, :half].astype(BF16)
        far_ref[at, :all_chans] = jnp.where(lane < half, second[0], first[1]).astype(BF16)
        far_ref[at, all_chans:] = second[2][:, :half].astype(BF16)


def tile_kernel(dims, last, many, *refs):
    side, chans, cap, tiles, all_chans, outs = dims
    parts = refs[:many]
    refs = refs[many:]
    if last:
        before_ref, *refs = refs
    slots_ref, weights_ref, table_ref, matrix, out_ref, slots, weights, image, *refs = refs
    if last:
        spread, staged, out_sems, sems = refs
    else:
        (sems,) = refs
    taps = slots.shape[0]
    count = tiles * cap
    half = chans * many
    copies = start_all(sems, [(slots_ref, slots), (weights_ref, weights)])

    def channels(index):
        return jnp.concatenate([part[index] for part in parts], axis=0)

    image[0:half, :] = channels(count)
    image[(side + 1) * half :, :] = channels(count + 1)
    wide = lax.broadcasted_iota(jnp.int32, (half, side), 1)

    def around(edge):
        value = channels(count + edge).astype(F32)
        before = jnp.where(wide == 0, 0.0, pltpu.roll(value, 1, 1))
        after = jnp.where(wide == side - 1, 0.0, pltpu.roll(value, side - 1, 1))
        return jnp.concatenate([before, value, after], axis=0).astype(BF16)

    left = dot(matrix[0:outs, :], around(2))
    right = dot(matrix[2 * outs :, :], around(3))
    if last:
        left = left + before_ref[side]
        right = right + before_ref[side + 1]
    else:
        out_ref[side] = left
        out_ref[side + 1] = right
    for copy in copies:
        copy.wait()

    def remap(r):
        lhs = jnp.concatenate([channels(slots[k, r]) for k in range(taps)], axis=1)
        rhs = jnp.concatenate([table_ref[weights[k, r]] for k in range(taps)], axis=0)
        return dot(lhs, rhs).astype(BF16)

    def place(r, value):
        image[pl.ds(pl.multiple_of((r + 1) * half, half), half), :] = value

    lane = lax.broadcasted_iota(jnp.int32, (outs, side), 1)

    def convolve(first):
        ys = []
        for u in range(0, STEP, 2):
            x0 = image[pl.ds(pl.multiple_of((first + u) * half, half), 3 * half), :]
            x1 = image[pl.ds(pl.multiple_of((first + u + 1) * half, half), 3 * half), :]
            ys.append(dot(matrix[...], jnp.concatenate([x0, x1], axis=1)))
        for u in range(STEP):
            i = first + u
            y = ys[u // 2][:, u % 2 * side : (u % 2 + 1) * side]
            at_left = pltpu.roll(left, lax.rem(side - i, side), 1) if last else 0.0
            at_right = pltpu.roll(right, side - 1 - i, 1) if last else 0.0
            from_left = jnp.where(lane == 0, at_left, pltpu.roll(y[:outs], 1, 1))
            from_right = jnp.where(lane == side - 1, at_right, pltpu.roll(y[2 * outs :], side - 1, 1))
            total = y[outs : 2 * outs] + from_left + from_right
            if last:
                spread[pl.ds(u * (outs + 1), outs), :] = total + before_ref[i]
            else:
                out_ref[i] = total
        if last:
            rows = pl.ds(pl.multiple_of(first, STEP), STEP)
            for o in range(outs):
                staged[o, rows, :] = spread[pl.ds(o, STEP, stride=outs + 1), :].astype(BF16)
            pltpu.make_async_copy(staged.at[:, rows, :], out_ref.at[:, rows, :], out_sems.at[first // STEP]).start()

    for r in range(STEP + 1):
        place(r, remap(r))

    def step(t, carry):
        first = t * STEP
        convolve(first)
        for u in range(STEP):
            r = jnp.minimum(first + STEP + 1 + u, side - 1)
            place(r, remap(r))
        return carry

    lax.fori_loop(0, side // STEP - 1, step, 0)
    convolve(side - STEP)
    if last:
        for t in range(side // STEP):
            rows = pl.ds(t * STEP, STEP)
            pltpu.make_async_copy(staged.at[:, rows, :], out_ref.at[:, rows, :], out_sems.at[t]).wait()


def body(source, send_list, block_slot, weight_index, remap_table, neighbour_tile, neighbour_edge, conv_weight):
    kinds, side = remap_table.shape[:2]
    chans = source.shape[0]
    tiles, cap = send_list.shape[1:]
    taps = block_slot.shape[1]
    blocks = source.shape[1] // side
    count = tiles * cap
    all_chans, outs = conv_weight.shape[2:]
    parts = lax.axis_size("chan")
    rows = round_up(2 * taps + tiles, 16)
    params = pltpu.CompilerParams(vmem_limit_bytes=LIMIT)
    slots, weights = in_hbm(block_slot.T), in_hbm(weight_index.T)
    filters = in_hbm(conv_weight.transpose(0, 1, 3, 2))
    packed, slots, weights, table, filters = pl.pallas_call(
        pack_kernel,
        out_shape=[
            jax.ShapeDtypeStruct((blocks * chans + rows, side), BF16),
            jax.ShapeDtypeStruct(slots.shape, jnp.int32),
            jax.ShapeDtypeStruct(weights.shape, jnp.int32),
            jax.ShapeDtypeStruct(remap_table.shape, BF16),
            jax.ShapeDtypeStruct(filters.shape, BF16),
        ],
        in_specs=[HBM] * 8,
        out_specs=[VMEM] * 5,
        scratch_shapes=[
            pltpu.VMEM((tiles, cap), jnp.int32),
            pltpu.VMEM(neighbour_tile.shape, jnp.int32),
            pltpu.VMEM(neighbour_edge.shape, jnp.int32),
            pltpu.SemaphoreType.DMA((blocks + 7,)),
        ],
        compiler_params=params,
        name="pack",
    )(
        slots, weights, in_hbm(send_list), in_hbm(neighbour_tile), in_hbm(neighbour_edge), in_hbm(source),
        in_hbm(remap_table), filters,
    )
    gathered = lax.all_gather(packed, "tile")
    mine = pl.pallas_call(
        functools.partial(edge_kernel, (side, chans, blocks, tiles, cap, taps, rows)),
        out_shape=jax.ShapeDtypeStruct(((count + 4) * chans, side), BF16),
        in_specs=[VMEM, VMEM],
        out_specs=VMEM,
        scratch_shapes=[
            pltpu.VMEM((2 * tiles * rows, side), jnp.int32),
            pltpu.SMEM((tiles * rows, side), jnp.int32),
            pltpu.VMEM((count * kinds // side * chans, side * side // kinds), BF16),
            pltpu.VMEM((side, side), F32),
            pltpu.SemaphoreType.DMA,
        ],
        compiler_params=params,
        name="edges",
    )(gathered, table)

    def swap(value, flip):
        return lax.ppermute(value, "chan", [(i, i ^ flip) for i in range(parts)])

    def spread(held, bit):
        while bit:
            for flip in list(held):
                held[flip ^ bit] = swap(held[flip], bit)
            bit //= 2
        return [held[f].reshape(count + 4, chans, side) for f in sorted(held)]

    many = parts // 2
    half = all_chans // 2
    mine, filters = lax.optimization_barrier((mine, filters))
    near = spread({0: mine}, many // 2)
    near_filters, far_filters = pl.pallas_call(
        functools.partial(filter_kernel, chans),
        out_shape=[jax.ShapeDtypeStruct((3 * outs, 3 * half), BF16)] * 2,
        in_specs=[VMEM],
        out_specs=[VMEM] * 2,
        compiler_params=params,
        name="filters",
    )(filters)
    mine, near_filters = lax.optimization_barrier((mine, near_filters))
    across = swap(mine, many)
    dims = (side, chans, cap, tiles, all_chans, outs)
    scratch = [
        pltpu.SMEM(slots.shape, jnp.int32),
        pltpu.SMEM(weights.shape, jnp.int32),
        pltpu.VMEM(((side + 2) * half, side), BF16),
    ]
    flops = 2 * side * half * taps * side * side + 2 * side * side * 9 * half * outs
    cost = pl.CostEstimate(flops=flops, bytes_accessed=(side + 2) * outs * side * 4, transcendentals=0)
    so_far = pl.pallas_call(
        functools.partial(tile_kernel, dims, False, many),
        out_shape=jax.ShapeDtypeStruct((side + 2, outs, side), F32),
        in_specs=[VMEM] * (many + 4),
        out_specs=VMEM,
        scratch_shapes=scratch + [pltpu.SemaphoreType.DMA((2,))],
        compiler_params=params,
        cost_estimate=cost,
        name="near",
    )(*near, slots, weights, table, near_filters)
    across, so_far = lax.optimization_barrier((across, so_far))
    far = spread({many: across}, many // 2)
    return pl.pallas_call(
        functools.partial(tile_kernel, dims, True, many),
        out_shape=jax.ShapeDtypeStruct((outs, side, side), BF16),
        in_specs=[VMEM] * (many + 5),
        out_specs=HBM,
        scratch_shapes=scratch
        + [
            pltpu.VMEM((round_up(STEP * (outs + 1), 8), side), F32),
            pltpu.VMEM((outs, side, side), BF16),
            pltpu.SemaphoreType.DMA((side // STEP,)),
            pltpu.SemaphoreType.DMA((2,)),
        ],
        compiler_params=params,
        cost_estimate=cost,
        name="far",
    )(*far, so_far, slots, weights, table, far_filters)


def solution(mesh):
    in_specs = (
        P("chan", ("group", "tile")),
        P("tile", None, None),
        P("tile", None),
        P("tile", None),
        P(),
        P("tile", None),
        P("tile", None),
        P(None, None, None, "chan"),
    )
    out_specs = P("chan", ("group", "tile"), None)
    return jax.shard_map(body, mesh=mesh, in_specs=in_specs, out_specs=out_specs, check_vma=False)
```

```python
import functools

import jax
import jax.numpy as jnp
from jax import lax
from jax.experimental import pallas as pl
from jax.experimental.pallas import tpu as pltpu
from jax.sharding import PartitionSpec as P

F32 = jnp.float32
BF16 = jnp.bfloat16
VMEM = pl.BlockSpec(memory_space=pltpu.VMEM)
HBM = pl.BlockSpec(memory_space=pltpu.HBM)
LIMIT = 32 * 2**20
STEP = 16


def round_up(value, step):
    return -(-value // step) * step


def in_hbm(value):
    return pltpu.with_memory_space_constraint(value, pltpu.HBM)


def dot(a, b):
    return jnp.dot(a, b, preferred_element_type=F32)


def start_all(sems, pairs):
    copies = [pltpu.make_async_copy(src, dst, sems.at[n]) for n, (src, dst) in enumerate(pairs)]
    for copy in copies:
        copy.start()
    return copies


def pack_kernel(
    slots_hbm, weights_hbm, lists_hbm, neigh_hbm, codes_hbm, source_hbm, table_hbm, filters_hbm,
    out_ref, slots, weights, table_ref, filters, lists, neigh, codes, sems,
):
    side = out_ref.shape[1]
    chans = source_hbm.shape[0]
    blocks = source_hbm.shape[1] // side
    base = blocks * chans
    copies = start_all(
        sems,
        [(slots_hbm, slots), (weights_hbm, weights), (lists_hbm.at[0], lists), (neigh_hbm, neigh), (codes_hbm, codes)]
        + [
            (source_hbm.at[:, pl.ds(block * side, side)], out_ref.at[pl.ds(block * chans, chans), :])
            for block in range(blocks)
        ]
        + [(table_hbm, table_ref), (filters_hbm, filters)],
    )
    for copy in copies[:5]:
        copy.wait()
    taps = slots.shape[0]
    tiles, cap = lists.shape
    rows = out_ref.shape[0] - base
    sides = jnp.concatenate([neigh[...], codes[...]], axis=1).astype(F32)
    wide = jnp.concatenate(
        [
            lists[...].astype(F32),
            jnp.concatenate([sides, jnp.zeros((tiles - 1, sides.shape[1]), F32)], axis=0),
            jnp.zeros((tiles, side - cap - sides.shape[1]), F32),
        ],
        axis=1,
    )
    parts = [slots[...].astype(F32), weights[...].astype(F32), wide]
    if rows > 2 * taps + tiles:
        parts.append(jnp.zeros((rows - 2 * taps - tiles, side), F32))
    out_ref[base:, :] = jnp.concatenate(parts, axis=0).astype(BF16)
    for copy in copies[5:]:
        copy.wait()


def edge_kernel(dims, gathered_ref, table_ref, out_ref, ints, scalars, picked, columns, sem):
    side, chans, blocks, tiles, cap, taps, rows = dims
    count = tiles * cap
    base = blocks * chans
    kinds = table_ref.shape[0]
    per_group = side // kinds
    me = lax.axis_index("tile")
    tables = jnp.concatenate([gathered_ref[base:, band * side : (band + 1) * side] for band in range(tiles)], axis=0)
    ints[: tiles * rows, :] = tables.astype(F32).astype(jnp.int32)
    copy = pltpu.make_async_copy(ints.at[pl.ds(0, tiles * rows), :], scalars, sem)
    copy.start()
    row = lax.broadcasted_iota(jnp.int32, (side, side), 0)
    flip = (lax.broadcasted_iota(jnp.int32, (side, side), 1) + row == side - 1).astype(BF16)
    ints[tiles * rows :, :] = dot(tables, flip).astype(jnp.int32)
    lane = lax.broadcasted_iota(jnp.int32, (side, side), 1)
    total = jnp.zeros((side, side), F32)
    for kind in range(kinds):
        moved = pltpu.roll(table_ref[kind].astype(F32), per_group * kind + 1, 1)
        total = jnp.where(lane // per_group == kind, moved, total)
    columns[...] = total
    copy.wait()
    own_row = me * rows + 2 * taps
    neigh = [scalars[own_row, cap + s] for s in range(4)]
    codes = [scalars[own_row, cap + 4 + s] for s in range(4)]

    def block_of(owner, slot):
        band = slot // cap
        local = scalars[band * rows + 2 * taps + owner, slot % cap]
        return gathered_ref[pl.ds(pl.multiple_of(local * chans, chans), chans), pl.ds(pl.multiple_of(band * side, side), side)]

    for slot in range(count):
        out_ref[slot * chans : (slot + 1) * chans, :] = block_of(me, slot)
    for s in range(4):
        owner = neigh[s]
        edge = codes[s] % 4
        dest = pl.ds((count + s) * chans, chans)

        @pl.when(edge < 2)
        def _():
            at = jnp.where(edge == 0, 0, side - 1)
            acc = jnp.zeros((chans, side), F32)
            for k in range(taps):
                slot = scalars[owner * rows + k, at]
                kind = scalars[owner * rows + taps + k, at]
                acc = acc + dot(block_of(owner, slot), table_ref[kind])
            out_ref[dest, :] = acc.astype(BF16)

            @pl.when(codes[s] >= 4)
            def _():
                out_ref[dest, :] = dot(acc.astype(BF16), flip).astype(BF16)

        @pl.when(edge >= 2)
        def _():
            for slot in range(count):
                group, member = slot // per_group, slot % per_group
                picked[group * chans : (group + 1) * chans, member * side : (member + 1) * side] = block_of(owner, slot)
            col = columns[...]
            col = jnp.where(edge == 2, pltpu.roll(col, side - 1, 1), col)
            col = jnp.where(lane % per_group == 0, col, 0.0)
            spread = jnp.concatenate(
                [col if m == 0 else pltpu.roll(col, m, 1) for m in range(per_group)], axis=0
            ).astype(BF16)
            z = dot(picked[...], spread)
            z_hi = z.astype(BF16)
            z_lo = (z - z_hi.astype(F32)).astype(BF16)
            first = owner * rows + jnp.where(codes[s] >= 4, tiles * rows, 0)
            slots = ints[pl.ds(first, taps), :]
            inside = slots % per_group + ints[pl.ds(first + taps, taps), :] * per_group
            spots = [jnp.where(row == inside[k : k + 1], 1.0, 0.0).astype(BF16) for k in range(taps)]
            acc = jnp.zeros((2 * chans, side), F32)
            for group in range(count // per_group):
                here = jnp.where(slots // per_group == group, 1.0, 0.0).astype(BF16)
                hits = sum(spots[k] * here[k : k + 1] for k in range(taps))
                at = slice(group * chans, (group + 1) * chans)
                acc = acc + dot(jnp.concatenate([z_hi[at], z_lo[at]], axis=0), hits)
            out_ref[dest, :] = (acc[:chans] + acc[chans:]).astype(BF16)


def filter_kernel(chans, filters, near_ref, far_ref):
    outs, all_chans = filters.shape[2:]
    half = all_chans // 2
    me = lax.axis_index("chan")
    lane = lax.broadcasted_iota(jnp.int32, (outs, all_chans), 1)
    for b in range(3):
        first, second = [], []
        for a in range(3):
            value = filters[a, b].astype(F32)
            width = chans
            bit = 1
            while width < all_chans:
                other = jnp.where(
                    lane // width % 2 == 0, pltpu.roll(value, all_chans - width, 1), pltpu.roll(value, width, 1)
                )
                value = jnp.where((me & bit) != 0, other, value)
                width *= 2
                bit *= 2
            first.append(value)
            second.append(pltpu.roll(value, half, 1))
        at = slice(b * outs, (b + 1) * outs)
        near_ref[at, :all_chans] = jnp.where(lane < half, first[0], second[1]).astype(BF16)
        near_ref[at, all_chans:] = first[2][:, :half].astype(BF16)
        far_ref[at, :all_chans] = jnp.where(lane < half, second[0], first[1]).astype(BF16)
        far_ref[at, all_chans:] = second[2][:, :half].astype(BF16)


def tile_kernel(dims, last, many, *refs):
    side, chans, cap, tiles, all_chans, outs = dims
    parts = refs[:many]
    refs = refs[many:]
    if last:
        before_ref, *refs = refs
    slots_ref, weights_ref, table_ref, matrix, out_ref, slots, weights, image, *refs = refs
    if last:
        spread, staged, out_sems, sems = refs
    else:
        (sems,) = refs
    taps = slots.shape[0]
    count = tiles * cap
    half = chans * many
    copies = start_all(sems, [(slots_ref, slots), (weights_ref, weights)])

    def channels(index):
        return jnp.concatenate([part[index] for part in parts], axis=0)

    image[0:half, :] = channels(count)
    image[(side + 1) * half :, :] = channels(count + 1)
    wide = lax.broadcasted_iota(jnp.int32, (half, side), 1)

    def around(edge):
        value = channels(count + edge).astype(F32)
        before = jnp.where(wide == 0, 0.0, pltpu.roll(value, 1, 1))
        after = jnp.where(wide == side - 1, 0.0, pltpu.roll(value, side - 1, 1))
        return jnp.concatenate([before, value, after], axis=0).astype(BF16)

    left = dot(matrix[0:outs, :], around(2))
    right = dot(matrix[2 * outs :, :], around(3))
    if last:
        left = left + before_ref[side]
        right = right + before_ref[side + 1]
    else:
        out_ref[side] = left
        out_ref[side + 1] = right
    for copy in copies:
        copy.wait()

    def remap(r):
        lhs = jnp.concatenate([channels(slots[k, r]) for k in range(taps)], axis=1)
        rhs = jnp.concatenate([table_ref[weights[k, r]] for k in range(taps)], axis=0)
        return dot(lhs, rhs).astype(BF16)

    def place(r, value):
        image[pl.ds(pl.multiple_of((r + 1) * half, half), half), :] = value

    lane = lax.broadcasted_iota(jnp.int32, (outs, side), 1)

    def convolve(first):
        ys = []
        for u in range(0, STEP, 2):
            x0 = image[pl.ds(pl.multiple_of((first + u) * half, half), 3 * half), :]
            x1 = image[pl.ds(pl.multiple_of((first + u + 1) * half, half), 3 * half), :]
            ys.append(dot(matrix[...], jnp.concatenate([x0, x1], axis=1)))
        for u in range(STEP):
            i = first + u
            y = ys[u // 2][:, u % 2 * side : (u % 2 + 1) * side]
            at_left = pltpu.roll(left, lax.rem(side - i, side), 1) if last else 0.0
            at_right = pltpu.roll(right, side - 1 - i, 1) if last else 0.0
            from_left = jnp.where(lane == 0, at_left, pltpu.roll(y[:outs], 1, 1))
            from_right = jnp.where(lane == side - 1, at_right, pltpu.roll(y[2 * outs :], side - 1, 1))
            total = y[outs : 2 * outs] + from_left + from_right
            if last:
                spread[pl.ds(u * (outs + 1), outs), :] = total + before_ref[i]
            else:
                out_ref[i] = total
        if last:
            rows = pl.ds(pl.multiple_of(first, STEP), STEP)
            for o in range(outs):
                staged[o, rows, :] = spread[pl.ds(o, STEP, stride=outs + 1), :].astype(BF16)
            pltpu.make_async_copy(staged.at[:, rows, :], out_ref.at[:, rows, :], out_sems.at[first // STEP]).start()

    for r in range(STEP + 1):
        place(r, remap(r))

    def step(t, carry):
        first = t * STEP
        convolve(first)
        for u in range(STEP):
            r = jnp.minimum(first + STEP + 1 + u, side - 1)
            place(r, remap(r))
        return carry

    lax.fori_loop(0, side // STEP - 1, step, 0)
    convolve(side - STEP)
    if last:
        for t in range(side // STEP):
            rows = pl.ds(t * STEP, STEP)
            pltpu.make_async_copy(staged.at[:, rows, :], out_ref.at[:, rows, :], out_sems.at[t]).wait()


def body(source, send_list, block_slot, weight_index, remap_table, neighbour_tile, neighbour_edge, conv_weight):
    kinds, side = remap_table.shape[:2]
    chans = source.shape[0]
    tiles, cap = send_list.shape[1:]
    taps = block_slot.shape[1]
    blocks = source.shape[1] // side
    count = tiles * cap
    all_chans, outs = conv_weight.shape[2:]
    parts = lax.axis_size("chan")
    rows = round_up(2 * taps + tiles, 16)
    params = pltpu.CompilerParams(vmem_limit_bytes=LIMIT)
    slots, weights = in_hbm(block_slot.T), in_hbm(weight_index.T)
    filters = in_hbm(conv_weight.transpose(0, 1, 3, 2))
    packed, slots, weights, table, filters = pl.pallas_call(
        pack_kernel,
        out_shape=[
            jax.ShapeDtypeStruct((blocks * chans + rows, side), BF16),
            jax.ShapeDtypeStruct(slots.shape, jnp.int32),
            jax.ShapeDtypeStruct(weights.shape, jnp.int32),
            jax.ShapeDtypeStruct(remap_table.shape, BF16),
            jax.ShapeDtypeStruct(filters.shape, BF16),
        ],
        in_specs=[HBM] * 8,
        out_specs=[VMEM] * 5,
        scratch_shapes=[
            pltpu.VMEM((tiles, cap), jnp.int32),
            pltpu.VMEM(neighbour_tile.shape, jnp.int32),
            pltpu.VMEM(neighbour_edge.shape, jnp.int32),
            pltpu.SemaphoreType.DMA((blocks + 7,)),
        ],
        compiler_params=params,
        name="pack",
    )(
        slots, weights, in_hbm(send_list), in_hbm(neighbour_tile), in_hbm(neighbour_edge), in_hbm(source),
        in_hbm(remap_table), filters,
    )
    gathered = lax.all_gather(packed, "tile", axis=1, tiled=True)
    mine = pl.pallas_call(
        functools.partial(edge_kernel, (side, chans, blocks, tiles, cap, taps, rows)),
        out_shape=jax.ShapeDtypeStruct(((count + 4) * chans, side), BF16),
        in_specs=[VMEM, VMEM],
        out_specs=VMEM,
        scratch_shapes=[
            pltpu.VMEM((2 * tiles * rows, side), jnp.int32),
            pltpu.SMEM((tiles * rows, side), jnp.int32),
            pltpu.VMEM((count * kinds // side * chans, side * side // kinds), BF16),
            pltpu.VMEM((side, side), F32),
            pltpu.SemaphoreType.DMA,
        ],
        compiler_params=params,
        name="edges",
    )(gathered, table)

    def swap(value, flip):
        return lax.ppermute(value, "chan", [(i, i ^ flip) for i in range(parts)])

    def spread(held, bit):
        while bit:
            for flip in list(held):
                held[flip ^ bit] = swap(held[flip], bit)
            bit //= 2
        return [held[f].reshape(count + 4, chans, side) for f in sorted(held)]

    many = parts // 2
    half = all_chans // 2
    mine, filters = lax.optimization_barrier((mine, filters))
    near = spread({0: mine}, many // 2)
    near_filters, far_filters = pl.pallas_call(
        functools.partial(filter_kernel, chans),
        out_shape=[jax.ShapeDtypeStruct((3 * outs, 3 * half), BF16)] * 2,
        in_specs=[VMEM],
        out_specs=[VMEM] * 2,
        compiler_params=params,
        name="filters",
    )(filters)
    mine, near_filters = lax.optimization_barrier((mine, near_filters))
    across = swap(mine, many)
    dims = (side, chans, cap, tiles, all_chans, outs)
    scratch = [
        pltpu.SMEM(slots.shape, jnp.int32),
        pltpu.SMEM(weights.shape, jnp.int32),
        pltpu.VMEM(((side + 2) * half, side), BF16),
    ]
    flops = 2 * side * half * taps * side * side + 2 * side * side * 9 * half * outs
    cost = pl.CostEstimate(flops=flops, bytes_accessed=(side + 2) * outs * side * 4, transcendentals=0)
    so_far = pl.pallas_call(
        functools.partial(tile_kernel, dims, False, many),
        out_shape=jax.ShapeDtypeStruct((side + 2, outs, side), F32),
        in_specs=[VMEM] * (many + 4),
        out_specs=VMEM,
        scratch_shapes=scratch + [pltpu.SemaphoreType.DMA((2,))],
        compiler_params=params,
        cost_estimate=cost,
        name="near",
    )(*near, slots, weights, table, near_filters)
    across, so_far = lax.optimization_barrier((across, so_far))
    far = spread({many: across}, many // 2)
    return pl.pallas_call(
        functools.partial(tile_kernel, dims, True, many),
        out_shape=jax.ShapeDtypeStruct((outs, side, side), BF16),
        in_specs=[VMEM] * (many + 5),
        out_specs=HBM,
        scratch_shapes=scratch
        + [
            pltpu.VMEM((round_up(STEP * (outs + 1), 8), side), F32),
            pltpu.VMEM((outs, side, side), BF16),
            pltpu.SemaphoreType.DMA((side // STEP,)),
            pltpu.SemaphoreType.DMA((2,)),
        ],
        compiler_params=params,
        cost_estimate=cost,
        name="far",
    )(*far, so_far, slots, weights, table, far_filters)


def solution(mesh):
    in_specs = (
        P("chan", ("group", "tile")),
        P("tile", None, None),
        P("tile", None),
        P("tile", None),
        P(),
        P("tile", None),
        P("tile", None),
        P(None, None, None, "chan"),
    )
    out_specs = P("chan", ("group", "tile"), None)
    return jax.shard_map(body, mesh=mesh, in_specs=in_specs, out_specs=out_specs, check_vma=False)
```

```python
import functools

import jax
import jax.numpy as jnp
from jax import lax
from jax.experimental import pallas as pl
from jax.experimental.pallas import tpu as pltpu
from jax.sharding import PartitionSpec as P

F32 = jnp.float32
BF16 = jnp.bfloat16
VMEM = pl.BlockSpec(memory_space=pltpu.VMEM)
HBM = pl.BlockSpec(memory_space=pltpu.HBM)
LIMIT = 32 * 2**20
STEP = 16


def round_up(value, step):
    return -(-value // step) * step


def in_hbm(value):
    return pltpu.with_memory_space_constraint(value, pltpu.HBM)


def dot(a, b):
    return jnp.dot(a, b, preferred_element_type=F32)


def start_all(sems, pairs):
    copies = [pltpu.make_async_copy(src, dst, sems.at[n]) for n, (src, dst) in enumerate(pairs)]
    for copy in copies:
        copy.start()
    return copies


def pack_kernel(
    slots_hbm, weights_hbm, lists_hbm, neigh_hbm, codes_hbm, source_hbm, table_hbm, filters_hbm,
    out_ref, slots, weights, table_ref, filters, lists, neigh, codes, sems,
):
    side = out_ref.shape[1]
    chans = source_hbm.shape[0]
    blocks = source_hbm.shape[1] // side
    base = blocks * chans
    copies = start_all(
        sems,
        [(slots_hbm, slots), (weights_hbm, weights), (lists_hbm.at[0], lists), (neigh_hbm, neigh), (codes_hbm, codes)]
        + [
            (source_hbm.at[:, pl.ds(block * side, side)], out_ref.at[pl.ds(block * chans, chans), :])
            for block in range(blocks)
        ]
        + [(table_hbm, table_ref), (filters_hbm, filters)],
    )
    for copy in copies[:5]:
        copy.wait()
    taps = slots.shape[0]
    tiles, cap = lists.shape
    rows = out_ref.shape[0] - base
    sides = jnp.concatenate([neigh[...], codes[...]], axis=1).astype(F32)
    wide = jnp.concatenate(
        [
            lists[...].astype(F32),
            jnp.concatenate([sides, jnp.zeros((tiles - 1, sides.shape[1]), F32)], axis=0),
            jnp.zeros((tiles, side - cap - sides.shape[1]), F32),
        ],
        axis=1,
    )
    parts = [slots[...].astype(F32), weights[...].astype(F32), wide]
    if rows > 2 * taps + tiles:
        parts.append(jnp.zeros((rows - 2 * taps - tiles, side), F32))
    out_ref[base:, :] = jnp.concatenate(parts, axis=0).astype(BF16)
    for copy in copies[5:]:
        copy.wait()


def edge_kernel(dims, gathered_ref, table_ref, out_ref, ints, scalars, picked, columns, sem):
    side, chans, blocks, tiles, cap, taps, rows = dims
    count = tiles * cap
    base = blocks * chans
    kinds = table_ref.shape[0]
    per_group = side // kinds
    me = lax.axis_index("tile")
    tables = jnp.concatenate([gathered_ref[base:, band * side : (band + 1) * side] for band in range(tiles)], axis=0)
    ints[: tiles * rows, :] = tables.astype(F32).astype(jnp.int32)
    copy = pltpu.make_async_copy(ints.at[pl.ds(0, tiles * rows), :], scalars, sem)
    copy.start()
    row = lax.broadcasted_iota(jnp.int32, (side, side), 0)
    flip = (lax.broadcasted_iota(jnp.int32, (side, side), 1) + row == side - 1).astype(BF16)
    ints[tiles * rows :, :] = dot(tables, flip).astype(jnp.int32)
    lane = lax.broadcasted_iota(jnp.int32, (side, side), 1)
    total = jnp.zeros((side, side), F32)
    for kind in range(kinds):
        moved = pltpu.roll(table_ref[kind].astype(F32), per_group * kind + 1, 1)
        total = jnp.where(lane // per_group == kind, moved, total)
    columns[...] = total
    copy.wait()
    own_row = me * rows + 2 * taps
    neigh = [scalars[own_row, cap + s] for s in range(4)]
    codes = [scalars[own_row, cap + 4 + s] for s in range(4)]

    def block_of(owner, slot):
        band = slot // cap
        local = scalars[band * rows + 2 * taps + owner, slot % cap]
        return gathered_ref[pl.ds(pl.multiple_of(local * chans, chans), chans), pl.ds(pl.multiple_of(band * side, side), side)]

    for slot in range(count):
        out_ref[slot * chans : (slot + 1) * chans, :] = block_of(me, slot)
    for s in range(4):
        owner = neigh[s]
        edge = codes[s] % 4
        dest = pl.ds((count + s) * chans, chans)

        @pl.when(edge < 2)
        def _():
            at = jnp.where(edge == 0, 0, side - 1)
            acc = jnp.zeros((chans, side), F32)
            for k in range(taps):
                slot = scalars[owner * rows + k, at]
                kind = scalars[owner * rows + taps + k, at]
                acc = acc + dot(block_of(owner, slot), table_ref[kind])
            out_ref[dest, :] = acc.astype(BF16)

            @pl.when(codes[s] >= 4)
            def _():
                out_ref[dest, :] = dot(acc.astype(BF16), flip).astype(BF16)

        @pl.when(edge >= 2)
        def _():
            for slot in range(count):
                group, member = slot // per_group, slot % per_group
                picked[group * chans : (group + 1) * chans, member * side : (member + 1) * side] = block_of(owner, slot)
            col = columns[...]
            col = jnp.where(edge == 2, pltpu.roll(col, side - 1, 1), col)
            col = jnp.where(lane % per_group == 0, col, 0.0)
            spread = jnp.concatenate(
                [col if m == 0 else pltpu.roll(col, m, 1) for m in range(per_group)], axis=0
            ).astype(BF16)
            z = dot(picked[...], spread)
            z_hi = z.astype(BF16)
            z_lo = (z - z_hi.astype(F32)).astype(BF16)
            first = owner * rows + jnp.where(codes[s] >= 4, tiles * rows, 0)
            slots = ints[pl.ds(first, taps), :]
            inside = slots % per_group + ints[pl.ds(first + taps, taps), :] * per_group
            spots = [jnp.where(row == inside[k : k + 1], 1.0, 0.0).astype(BF16) for k in range(taps)]
            acc = jnp.zeros((2 * chans, side), F32)
            for group in range(count // per_group):
                here = jnp.where(slots // per_group == group, 1.0, 0.0).astype(BF16)
                hits = sum(spots[k] * here[k : k + 1] for k in range(taps))
                at = slice(group * chans, (group + 1) * chans)
                acc = acc + dot(jnp.concatenate([z_hi[at], z_lo[at]], axis=0), hits)
            out_ref[dest, :] = (acc[:chans] + acc[chans:]).astype(BF16)


def filter_kernel(chans, filters, partner_filters, near_ref, far_ref):
    outs, all_chans = filters.shape[2:]
    half = all_chans // 2
    me = lax.axis_index("chan")
    lane = lax.broadcasted_iota(jnp.int32, (outs, all_chans), 1)
    for n, source in enumerate([partner_filters, filters]):
        for b in range(3):
            first, second = [], []
            for a in range(3):
                value = source[a, b].astype(F32)
                width = chans
                bit = 1
                while width < all_chans:
                    other = jnp.where(
                        lane // width % 2 == 0, pltpu.roll(value, all_chans - width, 1), pltpu.roll(value, width, 1)
                    )
                    value = jnp.where((me & bit) != 0, other, value)
                    width *= 2
                    bit *= 2
                first.append(value)
                second.append(pltpu.roll(value, half, 1))
            at = slice((3 * n + b) * outs, (3 * n + b + 1) * outs)
            near_ref[at, :all_chans] = jnp.where(lane < half, first[0], second[1]).astype(BF16)
            near_ref[at, all_chans:] = first[2][:, :half].astype(BF16)
            far_ref[at, :all_chans] = jnp.where(lane < half, second[0], first[1]).astype(BF16)
            far_ref[at, all_chans:] = second[2][:, :half].astype(BF16)


class Remap:
    def __init__(self, dims, parts, slots_ref, weights_ref, table_ref, slots, weights, image, sems):
        self.side, self.chans, self.cap, self.tiles, self.outs = dims
        self.parts, self.table, self.slots, self.weights, self.image = parts, table_ref, slots, weights, image
        self.half = self.chans * len(parts)
        self.rows = self.side // 2
        self.count = self.tiles * self.cap
        self.lower = lax.rem(lax.axis_index("chan"), 2)
        self.copies = start_all(sems, [(slots_ref, slots), (weights_ref, weights)])

    def channels(self, index):
        return jnp.concatenate([part[index] for part in self.parts], axis=0)

    def around(self, edge):
        value = self.channels(self.count + edge).astype(F32)
        wide = lax.broadcasted_iota(jnp.int32, value.shape, 1)
        before = jnp.where(wide == 0, 0.0, pltpu.roll(value, 1, 1))
        after = jnp.where(wide == self.side - 1, 0.0, pltpu.roll(value, self.side - 1, 1))
        return jnp.concatenate([before, value, after], axis=0).astype(BF16)

    def row(self, at):
        taps = self.slots.shape[0]
        r = jnp.clip(self.lower * self.rows + at - 1, 0, self.side - 1)
        lhs = jnp.concatenate([self.channels(self.slots[k, r]) for k in range(taps)], axis=1)
        rhs = jnp.concatenate([self.table[self.weights[k, r]] for k in range(taps)], axis=0)
        return dot(lhs, rhs).astype(BF16)

    def run(self, convolve):
        for copy in self.copies:
            copy.wait()
        half, image = self.half, self.image
        image[0:half, :] = jnp.where(self.lower == 0, self.channels(self.count), self.row(0))
        for at in range(1, STEP + 2):
            image[at * half : (at + 1) * half, :] = self.row(at)

        def step(t, carry):
            first = t * STEP
            convolve(first)
            for u in range(STEP):
                at = first + STEP + 2 + u
                image[pl.ds(pl.multiple_of(at * half, half), half), :] = self.row(at)
            return carry

        lax.fori_loop(0, self.rows // STEP - 1, step, 0)
        end = slice((self.rows + 1) * half, (self.rows + 2) * half)
        image[end, :] = jnp.where(self.lower == 1, self.channels(self.count + 1), image[end, :])
        convolve(self.rows - STEP)


def convolve_step(outs, matrix, image, first, left, right, emit):
    half = matrix.shape[1] // 3
    side = image.shape[1]
    lane = lax.broadcasted_iota(jnp.int32, (outs, side), 1)
    ys = []
    for u in range(0, STEP, 2):
        x0 = image[pl.ds(pl.multiple_of((first + u) * half, half), 3 * half), :]
        x1 = image[pl.ds(pl.multiple_of((first + u + 1) * half, half), 3 * half), :]
        ys.append(dot(matrix, jnp.concatenate([x0, x1], axis=1)))
    for u in range(STEP):
        for n in range(matrix.shape[0] // (3 * outs)):
            y = ys[u // 2][3 * n * outs : 3 * (n + 1) * outs, u % 2 * side : (u % 2 + 1) * side]
            from_left = jnp.where(lane == 0, left(first + u), pltpu.roll(y[:outs], 1, 1))
            from_right = jnp.where(lane == side - 1, right(first + u), pltpu.roll(y[2 * outs :], side - 1, 1))
            emit(n, u, y[outs : 2 * outs] + from_left + from_right)


def near_kernel(dims, many, *refs):
    parts = refs[:many]
    slots_ref, weights_ref, table_ref, matrix, sums_ref, ends_ref, slots, weights, image, sems = refs[many:]
    work = Remap(dims, parts, slots_ref, weights_ref, table_ref, slots, weights, image, sems)
    outs = work.outs
    for n in range(2):
        ends_ref[n, 0] = dot(matrix[3 * n * outs : (3 * n + 1) * outs, :], work.around(2))
        ends_ref[n, 1] = dot(matrix[(3 * n + 2) * outs : (3 * n + 3) * outs, :], work.around(3))

    def convolve(first):
        def emit(n, u, total):
            sums_ref[first + u, n] = total

        convolve_step(outs, matrix[...], image, first, lambda i: 0.0, lambda i: 0.0, emit)

    work.run(convolve)


def finish_step(outs, matrix, image, first, base, ends, sums_ref, n, spread, dest):
    side = image.shape[1]

    def left(i):
        return pltpu.roll(ends[0], lax.rem(side - (base + i), side), 1)

    def right(i):
        return pltpu.roll(ends[1], side - 1 - (base + i), 1)

    def emit(_, u, total):
        spread[pl.ds(u * (outs + 1), outs), :] = total + sums_ref[first + u, n]

    convolve_step(outs, matrix, image, first, left, right, emit)
    rows = pl.ds(pl.multiple_of(first, STEP), STEP)
    for o in range(outs):
        dest[o, rows, :] = spread[pl.ds(o, STEP, stride=outs + 1), :].astype(BF16)


def far_kernel(dims, many, *refs):
    parts = refs[:many]
    (
        slots_ref, weights_ref, table_ref, matrix, sums_ref, ends_ref,
        done_ref, image, own_ends_ref, slots, weights, spread, sems,
    ) = refs[many:]
    work = Remap(dims, parts, slots_ref, weights_ref, table_ref, slots, weights, image, sems)
    outs = work.outs
    base = work.lower * work.rows
    ends = []
    for n in range(2):
        ends.append([
            ends_ref[n, 0] + dot(matrix[3 * n * outs : (3 * n + 1) * outs, :], work.around(2)),
            ends_ref[n, 1] + dot(matrix[(3 * n + 2) * outs : (3 * n + 3) * outs, :], work.around(3)),
        ])
    own_ends_ref[0] = ends[1][0]
    own_ends_ref[1] = ends[1][1]

    def convolve(first):
        finish_step(outs, matrix[: 3 * outs, :], image, first, base, ends[0], sums_ref, 0, spread, done_ref)

    work.run(convolve)


def own_kernel(dims, steps, *refs):
    side, chans, cap, tiles, outs = dims
    rows = side // 2
    image, matrix, sums_ref, ends_ref, *refs = refs
    received = None
    if len(refs) > 4:
        received, _, *refs = refs
    out_hbm, spread, staged, sems = refs
    lower = lax.rem(lax.axis_index("chan"), 2)
    base = lower * rows
    copies = []
    if received is not None:
        there = pl.ds(pl.multiple_of((1 - lower) * rows, rows), rows)
        copies.append(pltpu.make_async_copy(received, out_hbm.at[:, there, :], sems.at[len(steps)]))
        copies[0].start()
    for n, step in enumerate(steps):
        first = step * STEP
        finish_step(
            outs, matrix[3 * outs :, :], image, first, base, [ends_ref[0], ends_ref[1]], sums_ref, 1, spread, staged
        )
        to = pl.ds(pl.multiple_of(base + first, STEP), STEP)
        copies.append(pltpu.make_async_copy(staged.at[:, pl.ds(first, STEP), :], out_hbm.at[:, to, :], sems.at[n]))
        copies[-1].start()
    for copy in copies:
        copy.wait()


def body(source, send_list, block_slot, weight_index, remap_table, neighbour_tile, neighbour_edge, conv_weight):
    kinds, side = remap_table.shape[:2]
    chans = source.shape[0]
    tiles, cap = send_list.shape[1:]
    taps = block_slot.shape[1]
    blocks = source.shape[1] // side
    count = tiles * cap
    all_chans, outs = conv_weight.shape[2:]
    parts = lax.axis_size("chan")
    rows = round_up(2 * taps + tiles, 16)
    params = pltpu.CompilerParams(vmem_limit_bytes=LIMIT)
    slots, weights = in_hbm(block_slot.T), in_hbm(weight_index.T)
    filters = in_hbm(conv_weight.transpose(0, 1, 3, 2))
    packed, slots, weights, table, filters = pl.pallas_call(
        pack_kernel,
        out_shape=[
            jax.ShapeDtypeStruct((blocks * chans + rows, side), BF16),
            jax.ShapeDtypeStruct(slots.shape, jnp.int32),
            jax.ShapeDtypeStruct(weights.shape, jnp.int32),
            jax.ShapeDtypeStruct(remap_table.shape, BF16),
            jax.ShapeDtypeStruct(filters.shape, BF16),
        ],
        in_specs=[HBM] * 8,
        out_specs=[VMEM] * 5,
        scratch_shapes=[
            pltpu.VMEM((tiles, cap), jnp.int32),
            pltpu.VMEM(neighbour_tile.shape, jnp.int32),
            pltpu.VMEM(neighbour_edge.shape, jnp.int32),
            pltpu.SemaphoreType.DMA((blocks + 7,)),
        ],
        compiler_params=params,
        name="pack",
    )(
        slots, weights, in_hbm(send_list), in_hbm(neighbour_tile), in_hbm(neighbour_edge), in_hbm(source),
        in_hbm(remap_table), filters,
    )
    def swap(value, flip):
        return lax.ppermute(value, "chan", [(i, i ^ flip) for i in range(parts)])

    def spread(held, bit):
        while bit:
            for flip in list(held):
                held[flip ^ bit] = swap(held[flip], bit)
            bit //= 2
        return [held[f].reshape(count + 4, chans, side) for f in sorted(held)]

    partner_filters = swap(filters, 1)
    gathered = lax.all_gather(packed, "tile", axis=1, tiled=True)
    mine = pl.pallas_call(
        functools.partial(edge_kernel, (side, chans, blocks, tiles, cap, taps, rows)),
        out_shape=jax.ShapeDtypeStruct(((count + 4) * chans, side), BF16),
        in_specs=[VMEM, VMEM],
        out_specs=VMEM,
        scratch_shapes=[
            pltpu.VMEM((2 * tiles * rows, side), jnp.int32),
            pltpu.SMEM((tiles * rows, side), jnp.int32),
            pltpu.VMEM((count * kinds // side * chans, side * side // kinds), BF16),
            pltpu.VMEM((side, side), F32),
            pltpu.SemaphoreType.DMA,
        ],
        compiler_params=params,
        name="edges",
    )(gathered, table)

    many = parts // 2
    half = all_chans // 2
    mine, filters, partner_filters = lax.optimization_barrier((mine, filters, partner_filters))
    near = spread({0: mine}, many // 2)
    near_matrix, far_matrix = pl.pallas_call(
        functools.partial(filter_kernel, chans),
        out_shape=[jax.ShapeDtypeStruct((6 * outs, 3 * half), BF16)] * 2,
        in_specs=[VMEM] * 2,
        out_specs=[VMEM] * 2,
        compiler_params=params,
        name="filters",
    )(filters, partner_filters)
    mine, near_matrix = lax.optimization_barrier((mine, near_matrix))
    across = swap(mine, many)
    dims = (side, chans, cap, tiles, outs)
    half_rows = side // 2
    image_shape = ((half_rows + 2) * half, side)
    scratch = [pltpu.SMEM(slots.shape, jnp.int32), pltpu.SMEM(weights.shape, jnp.int32)]
    turning = pltpu.VMEM((round_up(STEP * (outs + 1), 8), side), F32)
    remap_flops = 2 * half_rows * half * taps * side * side
    conv_flops = 2 * half_rows * side * 9 * half * outs

    def cost(flops):
        return pl.CostEstimate(flops=flops, bytes_accessed=side * outs * side * 4, transcendentals=0)

    sums, ends = pl.pallas_call(
        functools.partial(near_kernel, dims, many),
        out_shape=[
            jax.ShapeDtypeStruct((half_rows, 2, outs, side), F32),
            jax.ShapeDtypeStruct((2, 2, outs, side), F32),
        ],
        in_specs=[VMEM] * (many + 4),
        out_specs=[VMEM] * 2,
        scratch_shapes=scratch + [pltpu.VMEM(image_shape, BF16), pltpu.SemaphoreType.DMA((2,))],
        compiler_params=params,
        cost_estimate=cost(remap_flops + 2 * conv_flops),
        name="near",
    )(*near, slots, weights, table, near_matrix)
    across, sums = lax.optimization_barrier((across, sums))
    far = spread({many: across}, many // 2)
    done, image, own_ends = pl.pallas_call(
        functools.partial(far_kernel, dims, many),
        out_shape=[
            jax.ShapeDtypeStruct((outs, half_rows, side), BF16),
            jax.ShapeDtypeStruct(image_shape, BF16),
            jax.ShapeDtypeStruct((2, outs, side), F32),
        ],
        in_specs=[VMEM] * (many + 6),
        out_specs=[VMEM] * 3,
        scratch_shapes=scratch + [turning, pltpu.SemaphoreType.DMA((2,))],
        compiler_params=params,
        cost_estimate=cost(remap_flops + conv_flops),
        name="far",
    )(*far, slots, weights, table, far_matrix, sums, ends)
    received = swap(done, 1)
    steps = list(range(half_rows // STEP))
    shared = (image, far_matrix, sums, own_ends)
    last_scratch = [turning, pltpu.VMEM((outs, half_rows, side), BF16), pltpu.SemaphoreType.DMA((len(steps) + 1,))]
    begun = pl.pallas_call(
        functools.partial(own_kernel, dims, steps[:-1]),
        out_shape=jax.ShapeDtypeStruct((outs, side, side), BF16),
        in_specs=[VMEM] * 4,
        out_specs=HBM,
        scratch_shapes=last_scratch,
        compiler_params=params,
        cost_estimate=cost(conv_flops),
        name="own",
    )(*shared)
    return pl.pallas_call(
        functools.partial(own_kernel, dims, steps[-1:]),
        out_shape=jax.ShapeDtypeStruct((outs, side, side), BF16),
        in_specs=[VMEM] * 5 + [HBM],
        out_specs=HBM,
        scratch_shapes=last_scratch,
        input_output_aliases={5: 0},
        compiler_params=params,
        cost_estimate=cost(conv_flops // 4),
        name="last",
    )(*shared, received, begun)


def solution(mesh):
    in_specs = (
        P("chan", ("group", "tile")),
        P("tile", None, None),
        P("tile", None),
        P("tile", None),
        P(),
        P("tile", None),
        P("tile", None),
        P(None, None, None, "chan"),
    )
    out_specs = P("chan", ("group", "tile"), None)
    return jax.shard_map(body, mesh=mesh, in_specs=in_specs, out_specs=out_specs, check_vma=False)
```

```python
import functools

import jax
import jax.numpy as jnp
from jax import lax
from jax.experimental import pallas as pl
from jax.experimental.pallas import tpu as pltpu
from jax.sharding import PartitionSpec as P

F32 = jnp.float32
BF16 = jnp.bfloat16
VMEM = pl.BlockSpec(memory_space=pltpu.VMEM)
HBM = pl.BlockSpec(memory_space=pltpu.HBM)
LIMIT = 32 * 2**20
SEND = 16
AHEAD = 8


def round_up(value, step):
    return -(-value // step) * step


def in_hbm(value):
    return pltpu.with_memory_space_constraint(value, pltpu.HBM)


def dot(a, b):
    return jnp.dot(a, b, preferred_element_type=F32)


def start_all(sems, pairs):
    copies = [pltpu.make_async_copy(src, dst, sems.at[n]) for n, (src, dst) in enumerate(pairs)]
    for copy in copies:
        copy.start()
    return copies


def pack_kernel(
    slots_hbm, weights_hbm, lists_hbm, neigh_hbm, codes_hbm, source_hbm, table_hbm, filters_hbm,
    out_ref, slots, weights, table_ref, filters, lists, neigh, codes, sems,
):
    side = out_ref.shape[1]
    chans = source_hbm.shape[0]
    blocks = source_hbm.shape[1] // side
    base = blocks * chans
    copies = start_all(
        sems,
        [(slots_hbm, slots), (weights_hbm, weights), (lists_hbm.at[0], lists), (neigh_hbm, neigh), (codes_hbm, codes)]
        + [
            (source_hbm.at[:, pl.ds(block * side, side)], out_ref.at[pl.ds(block * chans, chans), :])
            for block in range(blocks)
        ]
        + [(table_hbm, table_ref), (filters_hbm, filters)],
    )
    for copy in copies[:5]:
        copy.wait()
    taps = slots.shape[0]
    tiles, cap = lists.shape
    rows = out_ref.shape[0] - base
    sides = jnp.concatenate([neigh[...], codes[...]], axis=1).astype(F32)
    wide = jnp.concatenate(
        [
            lists[...].astype(F32),
            jnp.concatenate([sides, jnp.zeros((tiles - 1, sides.shape[1]), F32)], axis=0),
            jnp.zeros((tiles, side - cap - sides.shape[1]), F32),
        ],
        axis=1,
    )
    parts = [slots[...].astype(F32), weights[...].astype(F32), wide]
    if rows > 2 * taps + tiles:
        parts.append(jnp.zeros((rows - 2 * taps - tiles, side), F32))
    out_ref[base:, :] = jnp.concatenate(parts, axis=0).astype(BF16)
    for copy in copies[5:]:
        copy.wait()


def edge_kernel(dims, gathered_ref, table_ref, out_ref, ints, scalars, picked, columns, sem):
    side, chans, blocks, tiles, cap, taps, rows = dims
    count = tiles * cap
    base = blocks * chans
    kinds = table_ref.shape[0]
    per_group = side // kinds
    me = lax.axis_index("tile")
    tables = jnp.concatenate([gathered_ref[base:, band * side : (band + 1) * side] for band in range(tiles)], axis=0)
    ints[: tiles * rows, :] = tables.astype(F32).astype(jnp.int32)
    copy = pltpu.make_async_copy(ints.at[pl.ds(0, tiles * rows), :], scalars, sem)
    copy.start()
    row = lax.broadcasted_iota(jnp.int32, (side, side), 0)
    flip = (lax.broadcasted_iota(jnp.int32, (side, side), 1) + row == side - 1).astype(BF16)
    ints[tiles * rows :, :] = dot(tables, flip).astype(jnp.int32)
    lane = lax.broadcasted_iota(jnp.int32, (side, side), 1)
    total = jnp.zeros((side, side), F32)
    for kind in range(kinds):
        moved = pltpu.roll(table_ref[kind].astype(F32), per_group * kind + 1, 1)
        total = jnp.where(lane // per_group == kind, moved, total)
    columns[...] = total
    copy.wait()
    own_row = me * rows + 2 * taps
    neigh = [scalars[own_row, cap + s] for s in range(4)]
    codes = [scalars[own_row, cap + 4 + s] for s in range(4)]

    def block_of(owner, slot):
        band = slot // cap
        local = scalars[band * rows + 2 * taps + owner, slot % cap]
        return gathered_ref[pl.ds(pl.multiple_of(local * chans, chans), chans), pl.ds(pl.multiple_of(band * side, side), side)]

    for slot in range(count):
        out_ref[slot * chans : (slot + 1) * chans, :] = block_of(me, slot)
    for s in range(4):
        owner = neigh[s]
        edge = codes[s] % 4
        dest = pl.ds((count + s) * chans, chans)

        @pl.when(edge < 2)
        def _():
            at = jnp.where(edge == 0, 0, side - 1)
            acc = jnp.zeros((chans, side), F32)
            for k in range(taps):
                slot = scalars[owner * rows + k, at]
                kind = scalars[owner * rows + taps + k, at]
                acc = acc + dot(block_of(owner, slot), table_ref[kind])
            out_ref[dest, :] = acc.astype(BF16)

            @pl.when(codes[s] >= 4)
            def _():
                out_ref[dest, :] = dot(acc.astype(BF16), flip).astype(BF16)

        @pl.when(edge >= 2)
        def _():
            for slot in range(count):
                group, member = slot // per_group, slot % per_group
                picked[group * chans : (group + 1) * chans, member * side : (member + 1) * side] = block_of(owner, slot)
            col = columns[...]
            col = jnp.where(edge == 2, pltpu.roll(col, side - 1, 1), col)
            col = jnp.where(lane % per_group == 0, col, 0.0)
            spread = jnp.concatenate(
                [col if m == 0 else pltpu.roll(col, m, 1) for m in range(per_group)], axis=0
            ).astype(BF16)
            z = dot(picked[...], spread)
            z_hi = z.astype(BF16)
            z_lo = (z - z_hi.astype(F32)).astype(BF16)
            first = owner * rows + jnp.where(codes[s] >= 4, tiles * rows, 0)
            slots = ints[pl.ds(first, taps), :]
            inside = slots % per_group + ints[pl.ds(first + taps, taps), :] * per_group
            spots = [jnp.where(row == inside[k : k + 1], 1.0, 0.0).astype(BF16) for k in range(taps)]
            acc = jnp.zeros((2 * chans, side), F32)
            for group in range(count // per_group):
                here = jnp.where(slots // per_group == group, 1.0, 0.0).astype(BF16)
                hits = sum(spots[k] * here[k : k + 1] for k in range(taps))
                at = slice(group * chans, (group + 1) * chans)
                acc = acc + dot(jnp.concatenate([z_hi[at], z_lo[at]], axis=0), hits)
            out_ref[dest, :] = (acc[:chans] + acc[chans:]).astype(BF16)


def filter_kernel(chans, last, filters, out_ref):
    outs, all_chans = filters.shape[2:]
    half = all_chans // 2
    me = lax.axis_index("chan")
    lane = lax.broadcasted_iota(jnp.int32, (outs, all_chans), 1)
    for b in range(3):
        first, second = [], []
        for a in range(3):
            value = filters[a, b].astype(F32)
            width = chans
            bit = 1
            while width < all_chans:
                other = jnp.where(
                    lane // width % 2 == 0, pltpu.roll(value, all_chans - width, 1), pltpu.roll(value, width, 1)
                )
                value = jnp.where((me & bit) != 0, other, value)
                width *= 2
                bit *= 2
            first.append(value)
            second.append(pltpu.roll(value, half, 1))
        low, high = (second, first) if last else (first, second)
        at = slice(b * outs, (b + 1) * outs)
        out_ref[at, :all_chans] = jnp.where(lane < half, low[0], high[1]).astype(BF16)
        out_ref[at, all_chans:] = low[2][:, :half].astype(BF16)


def tile_kernel(dims, last, many, *refs):
    side, chans, cap, tiles, all_chans, outs = dims
    parts = refs[:many]
    refs = refs[many:]
    if last:
        before_ref, *refs = refs
    slots_ref, weights_ref, table_ref, matrix, out_ref, slots, weights, image, *refs = refs
    if last:
        spread, staged, out_sems, sems = refs
    else:
        (sems,) = refs
    taps = slots.shape[0]
    count = tiles * cap
    half = chans * many
    copies = start_all(sems, [(slots_ref, slots), (weights_ref, weights)])

    def channels(index):
        return jnp.concatenate([part[index] for part in parts], axis=0)

    image[0:half, :] = channels(count)
    image[(side + 1) * half :, :] = channels(count + 1)
    wide = lax.broadcasted_iota(jnp.int32, (half, side), 1)

    def around(edge):
        value = channels(count + edge).astype(F32)
        before = jnp.where(wide == 0, 0.0, pltpu.roll(value, 1, 1))
        after = jnp.where(wide == side - 1, 0.0, pltpu.roll(value, side - 1, 1))
        return jnp.concatenate([before, value, after], axis=0).astype(BF16)

    left = dot(matrix[0:outs, :], around(2))
    right = dot(matrix[2 * outs :, :], around(3))
    if last:
        left = left + before_ref[side]
        right = right + before_ref[side + 1]
    else:
        out_ref[side] = left
        out_ref[side + 1] = right
    for copy in copies:
        copy.wait()

    def remap(r):
        lhs = jnp.concatenate([channels(slots[k, r]) for k in range(taps)], axis=1)
        rhs = jnp.concatenate([table_ref[weights[k, r]] for k in range(taps)], axis=0)
        return dot(lhs, rhs).astype(BF16)

    def place(r):
        image[(r + 1) * half : (r + 2) * half, :] = remap(r)

    lane = lax.broadcasted_iota(jnp.int32, (outs, side), 1)

    def multiply(i):
        x0 = image[i * half : (i + 3) * half, :]
        x1 = image[(i + 1) * half : (i + 4) * half, :]
        return dot(matrix[...], jnp.concatenate([x0, x1], axis=1))

    def combine(i, y):
        at_left = pltpu.roll(left, (side - i) % side, 1) if last else 0.0
        at_right = pltpu.roll(right, side - 1 - i, 1) if last else 0.0
        from_left = jnp.where(lane == 0, at_left, pltpu.roll(y[:outs], 1, 1))
        from_right = jnp.where(lane == side - 1, at_right, pltpu.roll(y[2 * outs :], side - 1, 1))
        total = y[outs : 2 * outs] + from_left + from_right
        if last:
            at = i % SEND * (outs + 1)
            spread[at : at + outs, :] = total + before_ref[i]
        else:
            out_ref[i] = total

    sent = []

    def finish(i, y):
        for h in range(2):
            combine(i + h, y[:, h * side : (h + 1) * side])
        if last and (i + 2) % SEND == 0:
            rows = pl.ds(i + 2 - SEND, SEND)
            for o in range(outs):
                staged[o, rows, :] = spread[pl.ds(o, SEND, stride=outs + 1), :].astype(BF16)
            sent.append(
                pltpu.make_async_copy(staged.at[:, rows, :], out_ref.at[:, rows, :], out_sems.at[(i + 2) // SEND - 1])
            )
            sent[-1].start()

    for r in range(AHEAD + 1):
        place(r)
    for i in range(0, side, 2):
        y = multiply(i)
        for r in range(i + AHEAD + 1, min(i + AHEAD + 3, side)):
            place(r)
        finish(i, y)
    for copy in sent:
        copy.wait()


def body(source, send_list, block_slot, weight_index, remap_table, neighbour_tile, neighbour_edge, conv_weight):
    kinds, side = remap_table.shape[:2]
    chans = source.shape[0]
    tiles, cap = send_list.shape[1:]
    taps = block_slot.shape[1]
    blocks = source.shape[1] // side
    count = tiles * cap
    all_chans, outs = conv_weight.shape[2:]
    parts = lax.axis_size("chan")
    rows = round_up(2 * taps + tiles, 16)
    params = pltpu.CompilerParams(vmem_limit_bytes=LIMIT)
    slots, weights = in_hbm(block_slot.T), in_hbm(weight_index.T)
    filters = in_hbm(conv_weight.transpose(0, 1, 3, 2))
    packed, slots, weights, table, filters = pl.pallas_call(
        pack_kernel,
        out_shape=[
            jax.ShapeDtypeStruct((blocks * chans + rows, side), BF16),
            jax.ShapeDtypeStruct(slots.shape, jnp.int32),
            jax.ShapeDtypeStruct(weights.shape, jnp.int32),
            jax.ShapeDtypeStruct(remap_table.shape, BF16),
            jax.ShapeDtypeStruct(filters.shape, BF16),
        ],
        in_specs=[HBM] * 8,
        out_specs=[VMEM] * 5,
        scratch_shapes=[
            pltpu.VMEM((tiles, cap), jnp.int32),
            pltpu.VMEM(neighbour_tile.shape, jnp.int32),
            pltpu.VMEM(neighbour_edge.shape, jnp.int32),
            pltpu.SemaphoreType.DMA((blocks + 7,)),
        ],
        compiler_params=params,
        name="pack",
    )(
        slots, weights, in_hbm(send_list), in_hbm(neighbour_tile), in_hbm(neighbour_edge), in_hbm(source),
        in_hbm(remap_table), filters,
    )
    gathered = lax.all_gather(packed, "tile", axis=1, tiled=True)
    mine = pl.pallas_call(
        functools.partial(edge_kernel, (side, chans, blocks, tiles, cap, taps, rows)),
        out_shape=jax.ShapeDtypeStruct(((count + 4) * chans, side), BF16),
        in_specs=[VMEM, VMEM],
        out_specs=VMEM,
        scratch_shapes=[
            pltpu.VMEM((2 * tiles * rows, side), jnp.int32),
            pltpu.SMEM((tiles * rows, side), jnp.int32),
            pltpu.VMEM((count * kinds // side * chans, side * side // kinds), BF16),
            pltpu.VMEM((side, side), F32),
            pltpu.SemaphoreType.DMA,
        ],
        compiler_params=params,
        name="edges",
    )(gathered, table)

    def swap(value, flip):
        return lax.ppermute(value, "chan", [(i, i ^ flip) for i in range(parts)])

    def spread(held, bit):
        while bit:
            for flip in list(held):
                held[flip ^ bit] = swap(held[flip], bit)
            bit //= 2
        return [held[f].reshape(count + 4, chans, side) for f in sorted(held)]

    many = parts // 2
    half = all_chans // 2
    mine, filters = lax.optimization_barrier((mine, filters))
    near = spread({0: mine}, many // 2)
    def matrix(last, filters):
        return pl.pallas_call(
            functools.partial(filter_kernel, chans, last),
            out_shape=jax.ShapeDtypeStruct((3 * outs, 3 * half), BF16),
            in_specs=[VMEM],
            out_specs=VMEM,
            compiler_params=params,
            name="filters",
        )(filters)

    near_filters = matrix(False, filters)
    mine, near_filters = lax.optimization_barrier((mine, near_filters))
    across = swap(mine, many)
    dims = (side, chans, cap, tiles, all_chans, outs)
    scratch = [
        pltpu.SMEM(slots.shape, jnp.int32),
        pltpu.SMEM(weights.shape, jnp.int32),
        pltpu.VMEM(((side + 2) * half, side), BF16),
    ]
    flops = 2 * side * half * taps * side * side + 2 * side * side * 9 * half * outs
    cost = pl.CostEstimate(flops=flops, bytes_accessed=(side + 2) * outs * side * 4, transcendentals=0)
    so_far = pl.pallas_call(
        functools.partial(tile_kernel, dims, False, many),
        out_shape=jax.ShapeDtypeStruct((side + 2, outs, side), F32),
        in_specs=[VMEM] * (many + 4),
        out_specs=VMEM,
        scratch_shapes=scratch + [pltpu.SemaphoreType.DMA((2,))],
        compiler_params=params,
        cost_estimate=cost,
        name="near",
    )(*near, slots, weights, table, near_filters)
    filters, so_far = lax.optimization_barrier((filters, so_far))
    far_filters = matrix(True, filters)
    across, so_far, far_filters = lax.optimization_barrier((across, so_far, far_filters))
    far = spread({many: across}, many // 2)
    return pl.pallas_call(
        functools.partial(tile_kernel, dims, True, many),
        out_shape=jax.ShapeDtypeStruct((outs, side, side), BF16),
        in_specs=[VMEM] * (many + 5),
        out_specs=HBM,
        scratch_shapes=scratch
        + [
            pltpu.VMEM((round_up(SEND * (outs + 1), 8), side), F32),
            pltpu.VMEM((outs, side, side), BF16),
            pltpu.SemaphoreType.DMA((side // SEND,)),
            pltpu.SemaphoreType.DMA((2,)),
        ],
        compiler_params=params,
        cost_estimate=cost,
        name="far",
    )(*far, so_far, slots, weights, table, far_filters)


def solution(mesh):
    in_specs = (
        P("chan", ("group", "tile")),
        P("tile", None, None),
        P("tile", None),
        P("tile", None),
        P(),
        P("tile", None),
        P("tile", None),
        P(None, None, None, "chan"),
    )
    out_specs = P("chan", ("group", "tile"), None)
    return jax.shard_map(body, mesh=mesh, in_specs=in_specs, out_specs=out_specs, check_vma=False)
```

```python
import functools

import jax
import jax.numpy as jnp
from jax import lax
from jax.experimental import pallas as pl
from jax.experimental.pallas import tpu as pltpu
from jax.sharding import PartitionSpec as P

F32 = jnp.float32
BF16 = jnp.bfloat16
VMEM = pl.BlockSpec(memory_space=pltpu.VMEM)
HBM = pl.BlockSpec(memory_space=pltpu.HBM)
LIMIT = 32 * 2**20
SEND = 16
AHEAD = 8


def round_up(value, step):
    return -(-value // step) * step


def in_hbm(value):
    return pltpu.with_memory_space_constraint(value, pltpu.HBM)


def dot(a, b):
    return jnp.dot(a, b, preferred_element_type=F32)


def start_all(sems, pairs):
    copies = [pltpu.make_async_copy(src, dst, sems.at[n]) for n, (src, dst) in enumerate(pairs)]
    for copy in copies:
        copy.start()
    return copies


def pack_kernel(
    slots_hbm, weights_hbm, lists_hbm, neigh_hbm, codes_hbm, source_hbm, table_hbm, filters_hbm,
    out_ref, slots, weights, table_ref, filters, lists, neigh, codes, sems,
):
    side = out_ref.shape[1]
    chans = source_hbm.shape[0]
    blocks = source_hbm.shape[1] // side
    base = blocks * chans
    copies = start_all(
        sems,
        [(slots_hbm, slots), (weights_hbm, weights), (lists_hbm.at[0], lists), (neigh_hbm, neigh), (codes_hbm, codes)]
        + [
            (source_hbm.at[:, pl.ds(block * side, side)], out_ref.at[pl.ds(block * chans, chans), :])
            for block in range(blocks)
        ]
        + [(table_hbm, table_ref), (filters_hbm, filters)],
    )
    for copy in copies[:5]:
        copy.wait()
    taps = slots.shape[0]
    tiles, cap = lists.shape
    rows = out_ref.shape[0] - base
    sides = jnp.concatenate([neigh[...], codes[...]], axis=1).astype(F32)
    wide = jnp.concatenate(
        [
            lists[...].astype(F32),
            jnp.concatenate([sides, jnp.zeros((tiles - 1, sides.shape[1]), F32)], axis=0),
            jnp.zeros((tiles, side - cap - sides.shape[1]), F32),
        ],
        axis=1,
    )
    parts = [slots[...].astype(F32), weights[...].astype(F32), wide]
    if rows > 2 * taps + tiles:
        parts.append(jnp.zeros((rows - 2 * taps - tiles, side), F32))
    out_ref[base:, :] = jnp.concatenate(parts, axis=0).astype(BF16)
    for copy in copies[5:]:
        copy.wait()


def lay_filters(chans, filters, near_ref, far_ref):
    outs, all_chans = filters.shape[2:]
    half = all_chans // 2
    me = lax.axis_index("chan")
    lane = lax.broadcasted_iota(jnp.int32, (outs, all_chans), 1)
    for b in range(3):
        first, second = [], []
        for a in range(3):
            value = filters[a, b].astype(F32)
            width = chans
            bit = 1
            while width < all_chans:
                other = jnp.where(
                    lane // width % 2 == 0, pltpu.roll(value, all_chans - width, 1), pltpu.roll(value, width, 1)
                )
                value = jnp.where((me & bit) != 0, other, value)
                width *= 2
                bit *= 2
            first.append(value)
            second.append(pltpu.roll(value, half, 1))
        at = slice(b * outs, (b + 1) * outs)
        near_ref[at, :all_chans] = jnp.where(lane < half, first[0], second[1]).astype(BF16)
        near_ref[at, all_chans:] = first[2][:, :half].astype(BF16)
        far_ref[at, :all_chans] = jnp.where(lane < half, second[0], first[1]).astype(BF16)
        far_ref[at, all_chans:] = second[2][:, :half].astype(BF16)


def edge_kernel(
    dims, gathered_ref, table_ref, filters, out_ref, near_ref, far_ref, ints, scalars, picked, columns, sem
):
    side, chans, blocks, tiles, cap, taps, rows = dims
    count = tiles * cap
    base = blocks * chans
    kinds = table_ref.shape[0]
    per_group = side // kinds
    me = lax.axis_index("tile")
    tables = jnp.concatenate([gathered_ref[base:, band * side : (band + 1) * side] for band in range(tiles)], axis=0)
    ints[: tiles * rows, :] = tables.astype(F32).astype(jnp.int32)
    copy = pltpu.make_async_copy(ints.at[pl.ds(0, tiles * rows), :], scalars, sem)
    copy.start()
    row = lax.broadcasted_iota(jnp.int32, (side, side), 0)
    flip = (lax.broadcasted_iota(jnp.int32, (side, side), 1) + row == side - 1).astype(BF16)
    ints[tiles * rows :, :] = dot(tables, flip).astype(jnp.int32)
    lane = lax.broadcasted_iota(jnp.int32, (side, side), 1)
    total = jnp.zeros((side, side), F32)
    for kind in range(kinds):
        moved = pltpu.roll(table_ref[kind].astype(F32), per_group * kind + 1, 1)
        total = jnp.where(lane // per_group == kind, moved, total)
    columns[...] = total
    lay_filters(chans, filters, near_ref, far_ref)
    copy.wait()
    own_row = me * rows + 2 * taps
    neigh = [scalars[own_row, cap + s] for s in range(4)]
    codes = [scalars[own_row, cap + 4 + s] for s in range(4)]

    def block_of(owner, slot):
        band = slot // cap
        local = scalars[band * rows + 2 * taps + owner, slot % cap]
        return gathered_ref[pl.ds(pl.multiple_of(local * chans, chans), chans), pl.ds(pl.multiple_of(band * side, side), side)]

    for slot in range(count):
        out_ref[slot * chans : (slot + 1) * chans, :] = block_of(me, slot)
    for s in range(4):
        owner = neigh[s]
        edge = codes[s] % 4
        dest = pl.ds((count + s) * chans, chans)

        @pl.when(edge < 2)
        def _():
            at = jnp.where(edge == 0, 0, side - 1)
            acc = jnp.zeros((chans, side), F32)
            for k in range(taps):
                slot = scalars[owner * rows + k, at]
                kind = scalars[owner * rows + taps + k, at]
                acc = acc + dot(block_of(owner, slot), table_ref[kind])
            out_ref[dest, :] = acc.astype(BF16)

            @pl.when(codes[s] >= 4)
            def _():
                out_ref[dest, :] = dot(acc.astype(BF16), flip).astype(BF16)

        @pl.when(edge >= 2)
        def _():
            for slot in range(count):
                group, member = slot // per_group, slot % per_group
                picked[group * chans : (group + 1) * chans, member * side : (member + 1) * side] = block_of(owner, slot)
            col = columns[...]
            col = jnp.where(edge == 2, pltpu.roll(col, side - 1, 1), col)
            col = jnp.where(lane % per_group == 0, col, 0.0)
            spread = jnp.concatenate(
                [col if m == 0 else pltpu.roll(col, m, 1) for m in range(per_group)], axis=0
            ).astype(BF16)
            z = dot(picked[...], spread)
            z_hi = z.astype(BF16)
            z_lo = (z - z_hi.astype(F32)).astype(BF16)
            first = owner * rows + jnp.where(codes[s] >= 4, tiles * rows, 0)
            slots = ints[pl.ds(first, taps), :]
            inside = slots % per_group + ints[pl.ds(first + taps, taps), :] * per_group
            spots = [jnp.where(row == inside[k : k + 1], 1.0, 0.0).astype(BF16) for k in range(taps)]
            acc = jnp.zeros((2 * chans, side), F32)
            for group in range(count // per_group):
                here = jnp.where(slots // per_group == group, 1.0, 0.0).astype(BF16)
                hits = sum(spots[k] * here[k : k + 1] for k in range(taps))
                at = slice(group * chans, (group + 1) * chans)
                acc = acc + dot(jnp.concatenate([z_hi[at], z_lo[at]], axis=0), hits)
            out_ref[dest, :] = (acc[:chans] + acc[chans:]).astype(BF16)


def tile_kernel(dims, last, many, *refs):
    side, chans, cap, tiles, all_chans, outs = dims
    parts = refs[:many]
    refs = refs[many:]
    if last:
        before_ref, *refs = refs
    slots_ref, weights_ref, table_ref, matrix, out_ref, slots, weights, image, *refs = refs
    if last:
        spread, staged, out_sems, sems = refs
    else:
        (sems,) = refs
    taps = slots.shape[0]
    count = tiles * cap
    half = chans * many
    copies = start_all(sems, [(slots_ref, slots), (weights_ref, weights)])

    def channels(index):
        return jnp.concatenate([part[index] for part in parts], axis=0)

    image[0:half, :] = channels(count)
    image[(side + 1) * half :, :] = channels(count + 1)
    wide = lax.broadcasted_iota(jnp.int32, (half, side), 1)

    def around(edge):
        value = channels(count + edge).astype(F32)
        before = jnp.where(wide == 0, 0.0, pltpu.roll(value, 1, 1))
        after = jnp.where(wide == side - 1, 0.0, pltpu.roll(value, side - 1, 1))
        return jnp.concatenate([before, value, after], axis=0).astype(BF16)

    left = dot(matrix[0:outs, :], around(2))
    right = dot(matrix[2 * outs :, :], around(3))
    if last:
        left = left + before_ref[side]
        right = right + before_ref[side + 1]
    else:
        out_ref[side] = left
        out_ref[side + 1] = right
    for copy in copies:
        copy.wait()

    def remap(r):
        lhs = jnp.concatenate([channels(slots[k, r]) for k in range(taps)], axis=1)
        rhs = jnp.concatenate([table_ref[weights[k, r]] for k in range(taps)], axis=0)
        return dot(lhs, rhs).astype(BF16)

    def place(r):
        image[(r + 1) * half : (r + 2) * half, :] = remap(r)

    lane = lax.broadcasted_iota(jnp.int32, (outs, side), 1)

    def multiply(i):
        x0 = image[i * half : (i + 3) * half, :]
        x1 = image[(i + 1) * half : (i + 4) * half, :]
        return dot(matrix[...], jnp.concatenate([x0, x1], axis=1))

    def combine(i, y):
        at_left = pltpu.roll(left, (side - i) % side, 1) if last else 0.0
        at_right = pltpu.roll(right, side - 1 - i, 1) if last else 0.0
        from_left = jnp.where(lane == 0, at_left, pltpu.roll(y[:outs], 1, 1))
        from_right = jnp.where(lane == side - 1, at_right, pltpu.roll(y[2 * outs :], side - 1, 1))
        total = y[outs : 2 * outs] + from_left + from_right
        if last:
            at = i % SEND * (outs + 1)
            spread[at : at + outs, :] = total + before_ref[i]
        else:
            out_ref[i] = total

    sent = []

    def finish(i, y):
        for h in range(2):
            combine(i + h, y[:, h * side : (h + 1) * side])
        if last and (i + 2) % SEND == 0:
            rows = pl.ds(i + 2 - SEND, SEND)
            for o in range(outs):
                staged[o, rows, :] = spread[pl.ds(o, SEND, stride=outs + 1), :].astype(BF16)
            sent.append(
                pltpu.make_async_copy(staged.at[:, rows, :], out_ref.at[:, rows, :], out_sems.at[(i + 2) // SEND - 1])
            )
            sent[-1].start()

    for r in range(AHEAD + 1):
        place(r)
    for i in range(0, side, 2):
        y = multiply(i)
        for r in range(i + AHEAD + 1, min(i + AHEAD + 3, side)):
            place(r)
        finish(i, y)
    for copy in sent:
        copy.wait()


def body(source, send_list, block_slot, weight_index, remap_table, neighbour_tile, neighbour_edge, conv_weight):
    kinds, side = remap_table.shape[:2]
    chans = source.shape[0]
    tiles, cap = send_list.shape[1:]
    taps = block_slot.shape[1]
    blocks = source.shape[1] // side
    count = tiles * cap
    all_chans, outs = conv_weight.shape[2:]
    parts = lax.axis_size("chan")
    rows = round_up(2 * taps + tiles, 16)
    params = pltpu.CompilerParams(vmem_limit_bytes=LIMIT)
    slots, weights = in_hbm(block_slot.T), in_hbm(weight_index.T)
    filters = in_hbm(conv_weight.transpose(0, 1, 3, 2))
    packed, slots, weights, table, filters = pl.pallas_call(
        pack_kernel,
        out_shape=[
            jax.ShapeDtypeStruct((blocks * chans + rows, side), BF16),
            jax.ShapeDtypeStruct(slots.shape, jnp.int32),
            jax.ShapeDtypeStruct(weights.shape, jnp.int32),
            jax.ShapeDtypeStruct(remap_table.shape, BF16),
            jax.ShapeDtypeStruct(filters.shape, BF16),
        ],
        in_specs=[HBM] * 8,
        out_specs=[VMEM] * 5,
        scratch_shapes=[
            pltpu.VMEM((tiles, cap), jnp.int32),
            pltpu.VMEM(neighbour_tile.shape, jnp.int32),
            pltpu.VMEM(neighbour_edge.shape, jnp.int32),
            pltpu.SemaphoreType.DMA((blocks + 7,)),
        ],
        compiler_params=params,
        name="pack",
    )(
        slots, weights, in_hbm(send_list), in_hbm(neighbour_tile), in_hbm(neighbour_edge), in_hbm(source),
        in_hbm(remap_table), filters,
    )
    gathered = lax.all_gather(packed, "tile", axis=1, tiled=True)
    many = parts // 2
    half = all_chans // 2
    matrix_shape = jax.ShapeDtypeStruct((3 * outs, 3 * half), BF16)
    mine, near_filters, far_filters = pl.pallas_call(
        functools.partial(edge_kernel, (side, chans, blocks, tiles, cap, taps, rows)),
        out_shape=[jax.ShapeDtypeStruct(((count + 4) * chans, side), BF16), matrix_shape, matrix_shape],
        in_specs=[VMEM] * 3,
        out_specs=[VMEM] * 3,
        scratch_shapes=[
            pltpu.VMEM((2 * tiles * rows, side), jnp.int32),
            pltpu.SMEM((tiles * rows, side), jnp.int32),
            pltpu.VMEM((count * kinds // side * chans, side * side // kinds), BF16),
            pltpu.VMEM((side, side), F32),
            pltpu.SemaphoreType.DMA,
        ],
        compiler_params=params,
        name="edges",
    )(gathered, table, filters)

    def swap(value, flip):
        return lax.ppermute(value, "chan", [(i, i ^ flip) for i in range(parts)])

    def spread(held, bit):
        while bit:
            for flip in list(held):
                held[flip ^ bit] = swap(held[flip], bit)
            bit //= 2
        return [held[f].reshape(count + 4, chans, side) for f in sorted(held)]

    near = spread({0: mine}, many // 2)
    across = swap(mine, many)
    dims = (side, chans, cap, tiles, all_chans, outs)
    scratch = [
        pltpu.SMEM(slots.shape, jnp.int32),
        pltpu.SMEM(weights.shape, jnp.int32),
        pltpu.VMEM(((side + 2) * half, side), BF16),
    ]
    flops = 2 * side * half * taps * side * side + 2 * side * side * 9 * half * outs
    cost = pl.CostEstimate(flops=flops, bytes_accessed=(side + 2) * outs * side * 4, transcendentals=0)
    so_far = pl.pallas_call(
        functools.partial(tile_kernel, dims, False, many),
        out_shape=jax.ShapeDtypeStruct((side + 2, outs, side), F32),
        in_specs=[VMEM] * (many + 4),
        out_specs=VMEM,
        scratch_shapes=scratch + [pltpu.SemaphoreType.DMA((2,))],
        compiler_params=params,
        cost_estimate=cost,
        name="near",
    )(*near, slots, weights, table, near_filters)
    across, so_far = lax.optimization_barrier((across, so_far))
    far = spread({many: across}, many // 2)
    return pl.pallas_call(
        functools.partial(tile_kernel, dims, True, many),
        out_shape=jax.ShapeDtypeStruct((outs, side, side), BF16),
        in_specs=[VMEM] * (many + 5),
        out_specs=HBM,
        scratch_shapes=scratch
        + [
            pltpu.VMEM((round_up(SEND * (outs + 1), 8), side), F32),
            pltpu.VMEM((outs, side, side), BF16),
            pltpu.SemaphoreType.DMA((side // SEND,)),
            pltpu.SemaphoreType.DMA((2,)),
        ],
        compiler_params=params,
        cost_estimate=cost,
        name="far",
    )(*far, so_far, slots, weights, table, far_filters)


def solution(mesh):
    in_specs = (
        P("chan", ("group", "tile")),
        P("tile", None, None),
        P("tile", None),
        P("tile", None),
        P(),
        P("tile", None),
        P("tile", None),
        P(None, None, None, "chan"),
    )
    out_specs = P("chan", ("group", "tile"), None)
    return jax.shard_map(body, mesh=mesh, in_specs=in_specs, out_specs=out_specs, check_vma=False)
```

```python
import functools

import jax
import jax.numpy as jnp
from jax import lax
from jax.experimental import pallas as pl
from jax.experimental.pallas import tpu as pltpu
from jax.sharding import PartitionSpec as P

F32 = jnp.float32
BF16 = jnp.bfloat16
VMEM = pl.BlockSpec(memory_space=pltpu.VMEM)
HBM = pl.BlockSpec(memory_space=pltpu.HBM)
LIMIT = 32 * 2**20
SEND = 16
AHEAD = 8


def round_up(value, step):
    return -(-value // step) * step


def in_hbm(value):
    return pltpu.with_memory_space_constraint(value, pltpu.HBM)


def dot(a, b):
    return jnp.dot(a, b, preferred_element_type=F32)


def start_all(sems, pairs):
    copies = [pltpu.make_async_copy(src, dst, sems.at[n]) for n, (src, dst) in enumerate(pairs)]
    for copy in copies:
        copy.start()
    return copies


def pack_kernel(
    slots_hbm, weights_hbm, lists_hbm, neigh_hbm, codes_hbm, source_hbm, table_hbm, filters_hbm,
    out_ref, slots, weights, table_ref, filters, lists, neigh, codes, sems,
):
    side = out_ref.shape[1]
    chans = source_hbm.shape[0]
    blocks = source_hbm.shape[1] // side
    base = blocks * chans
    copies = start_all(
        sems,
        [(slots_hbm, slots), (weights_hbm, weights), (lists_hbm.at[0], lists), (neigh_hbm, neigh), (codes_hbm, codes)]
        + [
            (source_hbm.at[:, pl.ds(block * side, side)], out_ref.at[pl.ds(block * chans, chans), :])
            for block in range(blocks)
        ]
        + [(table_hbm, table_ref), (filters_hbm, filters)],
    )
    for copy in copies[:5]:
        copy.wait()
    taps = slots.shape[0]
    tiles, cap = lists.shape
    rows = out_ref.shape[0] - base
    sides = jnp.concatenate([neigh[...], codes[...]], axis=1).astype(F32)
    wide = jnp.concatenate(
        [
            lists[...].astype(F32),
            jnp.concatenate([sides, jnp.zeros((tiles - 1, sides.shape[1]), F32)], axis=0),
            jnp.zeros((tiles, side - cap - sides.shape[1]), F32),
        ],
        axis=1,
    )
    parts = [slots[...].astype(F32), weights[...].astype(F32), wide]
    if rows > 2 * taps + tiles:
        parts.append(jnp.zeros((rows - 2 * taps - tiles, side), F32))
    out_ref[base:, :] = jnp.concatenate(parts, axis=0).astype(BF16)
    for copy in copies[5:]:
        copy.wait()


def edge_kernel(dims, gathered_ref, table_ref, out_ref, ints, scalars, picked, columns, sems):
    side, chans, blocks, tiles, cap, taps, rows = dims
    count = tiles * cap
    base = blocks * chans
    kinds = table_ref.shape[0]
    per_group = side // kinds
    me = lax.axis_index("tile")
    tables = jnp.concatenate([gathered_ref[base:, band * side : (band + 1) * side] for band in range(tiles)], axis=0)
    values = tables.astype(F32).astype(jnp.int32)
    lists = pl.ds(0, tiles * tiles)
    others = pl.ds(tiles * tiles, tiles * 2 * taps)
    start = tiles * (tiles + 2 * taps)
    for band in range(tiles):
        ints[band * tiles : (band + 1) * tiles, :] = values[band * rows + 2 * taps : band * rows + 2 * taps + tiles]
    lists_copy = pltpu.make_async_copy(ints.at[lists, :], scalars.at[lists, :], sems.at[0])
    lists_copy.start()
    for band in range(tiles):
        at = tiles * tiles + band * 2 * taps
        ints[at : at + 2 * taps, :] = values[band * rows : band * rows + 2 * taps]
    others_copy = pltpu.make_async_copy(ints.at[others, :], scalars.at[others, :], sems.at[1])
    others_copy.start()
    ints[start : start + tiles * rows, :] = values
    row = lax.broadcasted_iota(jnp.int32, (side, side), 0)
    flip = (lax.broadcasted_iota(jnp.int32, (side, side), 1) + row == side - 1).astype(BF16)
    ints[start + tiles * rows :, :] = dot(tables, flip).astype(jnp.int32)
    lane = lax.broadcasted_iota(jnp.int32, (side, side), 1)
    total = jnp.zeros((side, side), F32)
    for kind in range(kinds):
        moved = pltpu.roll(table_ref[kind].astype(F32), per_group * kind + 1, 1)
        total = jnp.where(lane // per_group == kind, moved, total)
    columns[...] = total
    lists_copy.wait()
    own_row = me * tiles
    neigh = [scalars[own_row, cap + s] for s in range(4)]
    codes = [scalars[own_row, cap + 4 + s] for s in range(4)]

    def block_of(owner, slot):
        band = slot // cap
        local = scalars[band * tiles + owner, slot % cap]
        return gathered_ref[pl.ds(pl.multiple_of(local * chans, chans), chans), pl.ds(pl.multiple_of(band * side, side), side)]

    for slot in range(count):
        out_ref[slot * chans : (slot + 1) * chans, :] = block_of(me, slot)
    for s in range(4):
        owner = neigh[s]
        edge = codes[s] % 4
        dest = pl.ds((count + s) * chans, chans)

        @pl.when(edge >= 2)
        def _():
            for slot in range(count):
                group, member = slot // per_group, slot % per_group
                picked[group * chans : (group + 1) * chans, member * side : (member + 1) * side] = block_of(owner, slot)
            col = columns[...]
            col = jnp.where(edge == 2, pltpu.roll(col, side - 1, 1), col)
            col = jnp.where(lane % per_group == 0, col, 0.0)
            spread = jnp.concatenate(
                [col if m == 0 else pltpu.roll(col, m, 1) for m in range(per_group)], axis=0
            ).astype(BF16)
            z = dot(picked[...], spread)
            z_hi = z.astype(BF16)
            z_lo = (z - z_hi.astype(F32)).astype(BF16)
            first = start + owner * rows + jnp.where(codes[s] >= 4, tiles * rows, 0)
            slots = ints[pl.ds(first, taps), :]
            inside = slots % per_group + ints[pl.ds(first + taps, taps), :] * per_group
            spots = [jnp.where(row == inside[k : k + 1], 1.0, 0.0).astype(BF16) for k in range(taps)]
            acc = jnp.zeros((2 * chans, side), F32)
            for group in range(count // per_group):
                here = jnp.where(slots // per_group == group, 1.0, 0.0).astype(BF16)
                hits = sum(spots[k] * here[k : k + 1] for k in range(taps))
                at = slice(group * chans, (group + 1) * chans)
                acc = acc + dot(jnp.concatenate([z_hi[at], z_lo[at]], axis=0), hits)
            out_ref[dest, :] = (acc[:chans] + acc[chans:]).astype(BF16)

    others_copy.wait()
    for s in range(4):
        owner = neigh[s]
        edge = codes[s] % 4
        dest = pl.ds((count + s) * chans, chans)

        @pl.when(edge < 2)
        def _():
            at = jnp.where(edge == 0, 0, side - 1)
            acc = jnp.zeros((chans, side), F32)
            for k in range(taps):
                slot = scalars[tiles * tiles + owner * 2 * taps + k, at]
                kind = scalars[tiles * tiles + owner * 2 * taps + taps + k, at]
                acc = acc + dot(block_of(owner, slot), table_ref[kind])
            out_ref[dest, :] = acc.astype(BF16)

            @pl.when(codes[s] >= 4)
            def _():
                out_ref[dest, :] = dot(acc.astype(BF16), flip).astype(BF16)


def filter_kernel(chans, last, filters, out_ref):
    outs, all_chans = filters.shape[2:]
    half = all_chans // 2
    me = lax.axis_index("chan")
    lane = lax.broadcasted_iota(jnp.int32, (outs, all_chans), 1)
    for b in range(3):
        first, second = [], []
        for a in range(3):
            value = filters[a, b].astype(F32)
            width = chans
            bit = 1
            while width < all_chans:
                other = jnp.where(
                    lane // width % 2 == 0, pltpu.roll(value, all_chans - width, 1), pltpu.roll(value, width, 1)
                )
                value = jnp.where((me & bit) != 0, other, value)
                width *= 2
                bit *= 2
            first.append(value)
            second.append(pltpu.roll(value, half, 1))
        low, high = (second, first) if last else (first, second)
        at = slice(b * outs, (b + 1) * outs)
        out_ref[at, :all_chans] = jnp.where(lane < half, low[0], high[1]).astype(BF16)
        out_ref[at, all_chans:] = low[2][:, :half].astype(BF16)


def tile_kernel(dims, last, many, *refs):
    side, chans, cap, tiles, all_chans, outs = dims
    parts = refs[:many]
    refs = refs[many:]
    if last:
        before_ref, *refs = refs
    slots_ref, weights_ref, table_ref, matrix, out_ref, slots, weights, image, *refs = refs
    if last:
        spread, staged, out_sems, sems = refs
    else:
        (sems,) = refs
    taps = slots.shape[0]
    count = tiles * cap
    half = chans * many
    copies = start_all(sems, [(slots_ref, slots), (weights_ref, weights)])

    def channels(index):
        return jnp.concatenate([part[index] for part in parts], axis=0)

    image[0:half, :] = channels(count)
    image[(side + 1) * half :, :] = channels(count + 1)
    wide = lax.broadcasted_iota(jnp.int32, (half, side), 1)

    def around(edge):
        value = channels(count + edge).astype(F32)
        before = jnp.where(wide == 0, 0.0, pltpu.roll(value, 1, 1))
        after = jnp.where(wide == side - 1, 0.0, pltpu.roll(value, side - 1, 1))
        return jnp.concatenate([before, value, after], axis=0).astype(BF16)

    left = dot(matrix[0:outs, :], around(2))
    right = dot(matrix[2 * outs :, :], around(3))
    if last:
        left = left + before_ref[side]
        right = right + before_ref[side + 1]
    else:
        out_ref[side] = left
        out_ref[side + 1] = right
    for copy in copies:
        copy.wait()

    def remap(r):
        lhs = jnp.concatenate([channels(slots[k, r]) for k in range(taps)], axis=1)
        rhs = jnp.concatenate([table_ref[weights[k, r]] for k in range(taps)], axis=0)
        return dot(lhs, rhs).astype(BF16)

    def place(r):
        image[(r + 1) * half : (r + 2) * half, :] = remap(r)

    lane = lax.broadcasted_iota(jnp.int32, (outs, side), 1)

    def multiply(i):
        x0 = image[i * half : (i + 3) * half, :]
        x1 = image[(i + 1) * half : (i + 4) * half, :]
        return dot(matrix[...], jnp.concatenate([x0, x1], axis=1))

    def combine(i, y):
        at_left = pltpu.roll(left, (side - i) % side, 1) if last else 0.0
        at_right = pltpu.roll(right, side - 1 - i, 1) if last else 0.0
        from_left = jnp.where(lane == 0, at_left, pltpu.roll(y[:outs], 1, 1))
        from_right = jnp.where(lane == side - 1, at_right, pltpu.roll(y[2 * outs :], side - 1, 1))
        total = y[outs : 2 * outs] + from_left + from_right
        if last:
            at = i % SEND * (outs + 1)
            spread[at : at + outs, :] = total + before_ref[i]
        else:
            out_ref[i] = total

    sent = []

    def finish(i, y):
        for h in range(2):
            combine(i + h, y[:, h * side : (h + 1) * side])
        if last and (i + 2) % SEND == 0:
            rows = pl.ds(i + 2 - SEND, SEND)
            for o in range(outs):
                staged[o, rows, :] = spread[pl.ds(o, SEND, stride=outs + 1), :].astype(BF16)
            sent.append(
                pltpu.make_async_copy(staged.at[:, rows, :], out_ref.at[:, rows, :], out_sems.at[(i + 2) // SEND - 1])
            )
            sent[-1].start()

    for r in range(AHEAD + 1):
        place(r)
    for i in range(0, side, 2):
        y = multiply(i)
        for r in range(i + AHEAD + 1, min(i + AHEAD + 3, side)):
            place(r)
        finish(i, y)
    for copy in sent:
        copy.wait()


def body(source, send_list, block_slot, weight_index, remap_table, neighbour_tile, neighbour_edge, conv_weight):
    kinds, side = remap_table.shape[:2]
    chans = source.shape[0]
    tiles, cap = send_list.shape[1:]
    taps = block_slot.shape[1]
    blocks = source.shape[1] // side
    count = tiles * cap
    all_chans, outs = conv_weight.shape[2:]
    parts = lax.axis_size("chan")
    rows = round_up(2 * taps + tiles, 16)
    params = pltpu.CompilerParams(vmem_limit_bytes=LIMIT)
    slots, weights = in_hbm(block_slot.T), in_hbm(weight_index.T)
    filters = in_hbm(conv_weight.transpose(0, 1, 3, 2))
    packed, slots, weights, table, filters = pl.pallas_call(
        pack_kernel,
        out_shape=[
            jax.ShapeDtypeStruct((blocks * chans + rows, side), BF16),
            jax.ShapeDtypeStruct(slots.shape, jnp.int32),
            jax.ShapeDtypeStruct(weights.shape, jnp.int32),
            jax.ShapeDtypeStruct(remap_table.shape, BF16),
            jax.ShapeDtypeStruct(filters.shape, BF16),
        ],
        in_specs=[HBM] * 8,
        out_specs=[VMEM] * 5,
        scratch_shapes=[
            pltpu.VMEM((tiles, cap), jnp.int32),
            pltpu.VMEM(neighbour_tile.shape, jnp.int32),
            pltpu.VMEM(neighbour_edge.shape, jnp.int32),
            pltpu.SemaphoreType.DMA((blocks + 7,)),
        ],
        compiler_params=params,
        name="pack",
    )(
        slots, weights, in_hbm(send_list), in_hbm(neighbour_tile), in_hbm(neighbour_edge), in_hbm(source),
        in_hbm(remap_table), filters,
    )
    gathered = lax.all_gather(packed, "tile", axis=1, tiled=True)
    mine = pl.pallas_call(
        functools.partial(edge_kernel, (side, chans, blocks, tiles, cap, taps, rows)),
        out_shape=jax.ShapeDtypeStruct(((count + 4) * chans, side), BF16),
        in_specs=[VMEM, VMEM],
        out_specs=VMEM,
        scratch_shapes=[
            pltpu.VMEM((tiles * (tiles + 2 * taps + 2 * rows), side), jnp.int32),
            pltpu.SMEM((tiles * (tiles + 2 * taps), side), jnp.int32),
            pltpu.VMEM((count * kinds // side * chans, side * side // kinds), BF16),
            pltpu.VMEM((side, side), F32),
            pltpu.SemaphoreType.DMA((2,)),
        ],
        compiler_params=params,
        name="edges",
    )(gathered, table)

    def swap(value, flip):
        return lax.ppermute(value, "chan", [(i, i ^ flip) for i in range(parts)])

    def spread(held, bit):
        while bit:
            for flip in list(held):
                held[flip ^ bit] = swap(held[flip], bit)
            bit //= 2
        return [held[f].reshape(count + 4, chans, side) for f in sorted(held)]

    many = parts // 2
    half = all_chans // 2
    mine, filters = lax.optimization_barrier((mine, filters))
    near = spread({0: mine}, many // 2)
    def matrix(last, filters):
        return pl.pallas_call(
            functools.partial(filter_kernel, chans, last),
            out_shape=jax.ShapeDtypeStruct((3 * outs, 3 * half), BF16),
            in_specs=[VMEM],
            out_specs=VMEM,
            compiler_params=params,
            name="filters",
        )(filters)

    near_filters = matrix(False, filters)
    across = swap(mine, many)
    dims = (side, chans, cap, tiles, all_chans, outs)
    scratch = [
        pltpu.SMEM(slots.shape, jnp.int32),
        pltpu.SMEM(weights.shape, jnp.int32),
        pltpu.VMEM(((side + 2) * half, side), BF16),
    ]
    flops = 2 * side * half * taps * side * side + 2 * side * side * 9 * half * outs
    cost = pl.CostEstimate(flops=flops, bytes_accessed=(side + 2) * outs * side * 4, transcendentals=0)
    so_far = pl.pallas_call(
        functools.partial(tile_kernel, dims, False, many),
        out_shape=jax.ShapeDtypeStruct((side + 2, outs, side), F32),
        in_specs=[VMEM] * (many + 4),
        out_specs=VMEM,
        scratch_shapes=scratch + [pltpu.SemaphoreType.DMA((2,))],
        compiler_params=params,
        cost_estimate=cost,
        name="near",
    )(*near, slots, weights, table, near_filters)
    filters, so_far = lax.optimization_barrier((filters, so_far))
    far_filters = matrix(True, filters)
    across, so_far, far_filters = lax.optimization_barrier((across, so_far, far_filters))
    far = spread({many: across}, many // 2)
    return pl.pallas_call(
        functools.partial(tile_kernel, dims, True, many),
        out_shape=jax.ShapeDtypeStruct((outs, side, side), BF16),
        in_specs=[VMEM] * (many + 5),
        out_specs=HBM,
        scratch_shapes=scratch
        + [
            pltpu.VMEM((round_up(SEND * (outs + 1), 8), side), F32),
            pltpu.VMEM((outs, side, side), BF16),
            pltpu.SemaphoreType.DMA((side // SEND,)),
            pltpu.SemaphoreType.DMA((2,)),
        ],
        compiler_params=params,
        cost_estimate=cost,
        name="far",
    )(*far, so_far, slots, weights, table, far_filters)


def solution(mesh):
    in_specs = (
        P("chan", ("group", "tile")),
        P("tile", None, None),
        P("tile", None),
        P("tile", None),
        P(),
        P("tile", None),
        P("tile", None),
        P(None, None, None, "chan"),
    )
    out_specs = P("chan", ("group", "tile"), None)
    return jax.shard_map(body, mesh=mesh, in_specs=in_specs, out_specs=out_specs, check_vma=False)
```

```python
import functools

import jax
import jax.numpy as jnp
from jax import lax
from jax.experimental import pallas as pl
from jax.experimental.pallas import tpu as pltpu
from jax.sharding import PartitionSpec as P

F32 = jnp.float32
BF16 = jnp.bfloat16
VMEM = pl.BlockSpec(memory_space=pltpu.VMEM)
HBM = pl.BlockSpec(memory_space=pltpu.HBM)
LIMIT = 32 * 2**20
SEND = 16
AHEAD = 8
PIECES = 4


def round_up(value, step):
    return -(-value // step) * step


def in_hbm(value):
    return pltpu.with_memory_space_constraint(value, pltpu.HBM)


def dot(a, b):
    return jnp.dot(a, b, preferred_element_type=F32)


def start_all(sems, pairs):
    copies = [pltpu.make_async_copy(src, dst, sems.at[n]) for n, (src, dst) in enumerate(pairs)]
    for copy in copies:
        copy.start()
    return copies


def pack_kernel(
    slots_hbm, weights_hbm, lists_hbm, neigh_hbm, codes_hbm, source_hbm, table_hbm, filters_hbm,
    out_ref, slots, weights, table_ref, filters, lists, neigh, codes, sems,
):
    side = out_ref.shape[1]
    chans = source_hbm.shape[0]
    blocks = source_hbm.shape[1] // side
    base = blocks * chans
    copies = start_all(
        sems,
        [(slots_hbm, slots), (weights_hbm, weights), (lists_hbm.at[0], lists), (neigh_hbm, neigh), (codes_hbm, codes)]
        + [
            (source_hbm.at[:, pl.ds(block * side, side)], out_ref.at[pl.ds(block * chans, chans), :])
            for block in range(blocks)
        ]
        + [(table_hbm, table_ref), (filters_hbm, filters)],
    )
    for copy in copies[:5]:
        copy.wait()
    taps = slots.shape[0]
    tiles, cap = lists.shape
    rows = out_ref.shape[0] - base
    sides = jnp.concatenate([neigh[...], codes[...]], axis=1).astype(F32)
    wide = jnp.concatenate(
        [
            lists[...].astype(F32),
            jnp.concatenate([sides, jnp.zeros((tiles - 1, sides.shape[1]), F32)], axis=0),
            jnp.zeros((tiles, side - cap - sides.shape[1]), F32),
        ],
        axis=1,
    )
    parts = [slots[...].astype(F32), weights[...].astype(F32), wide]
    if rows > 2 * taps + tiles:
        parts.append(jnp.zeros((rows - 2 * taps - tiles, side), F32))
    out_ref[base:, :] = jnp.concatenate(parts, axis=0).astype(BF16)
    for copy in copies[5:]:
        copy.wait()


def edge_kernel(dims, gathered_ref, table_ref, out_ref, ints, scalars, picked, columns, sems):
    side, chans, blocks, tiles, cap, taps, rows = dims
    count = tiles * cap
    base = blocks * chans
    kinds = table_ref.shape[0]
    per_group = side // kinds
    me = lax.axis_index("tile")
    tables = jnp.concatenate([gathered_ref[base:, band * side : (band + 1) * side] for band in range(tiles)], axis=0)
    values = tables.astype(F32).astype(jnp.int32)
    lists = pl.ds(0, tiles * tiles)
    others = pl.ds(tiles * tiles, tiles * 2 * taps)
    start = tiles * (tiles + 2 * taps)
    for band in range(tiles):
        ints[band * tiles : (band + 1) * tiles, :] = values[band * rows + 2 * taps : band * rows + 2 * taps + tiles]
    lists_copy = pltpu.make_async_copy(ints.at[lists, :], scalars.at[lists, :], sems.at[0])
    lists_copy.start()
    for band in range(tiles):
        at = tiles * tiles + band * 2 * taps
        ints[at : at + 2 * taps, :] = values[band * rows : band * rows + 2 * taps]
    others_copy = pltpu.make_async_copy(ints.at[others, :], scalars.at[others, :], sems.at[1])
    others_copy.start()
    ints[start : start + tiles * rows, :] = values
    row = lax.broadcasted_iota(jnp.int32, (side, side), 0)
    flip = (lax.broadcasted_iota(jnp.int32, (side, side), 1) + row == side - 1).astype(BF16)
    ints[start + tiles * rows :, :] = dot(tables, flip).astype(jnp.int32)
    lane = lax.broadcasted_iota(jnp.int32, (side, side), 1)
    total = jnp.zeros((side, side), F32)
    for kind in range(kinds):
        moved = pltpu.roll(table_ref[kind].astype(F32), per_group * kind + 1, 1)
        total = jnp.where(lane // per_group == kind, moved, total)
    columns[...] = total
    lists_copy.wait()
    own_row = me * tiles
    neigh = [scalars[own_row, cap + s] for s in range(4)]
    codes = [scalars[own_row, cap + 4 + s] for s in range(4)]

    def block_of(owner, slot):
        band = slot // cap
        local = scalars[band * tiles + owner, slot % cap]
        return gathered_ref[pl.ds(pl.multiple_of(local * chans, chans), chans), pl.ds(pl.multiple_of(band * side, side), side)]

    for slot in range(count):
        out_ref[slot * chans : (slot + 1) * chans, :] = block_of(me, slot)
    for s in range(4):
        owner = neigh[s]
        edge = codes[s] % 4
        dest = pl.ds((count + s) * chans, chans)

        @pl.when(edge >= 2)
        def _():
            for slot in range(count):
                group, member = slot // per_group, slot % per_group
                picked[group * chans : (group + 1) * chans, member * side : (member + 1) * side] = block_of(owner, slot)
            col = columns[...]
            col = jnp.where(edge == 2, pltpu.roll(col, side - 1, 1), col)
            col = jnp.where(lane % per_group == 0, col, 0.0)
            spread = jnp.concatenate(
                [col if m == 0 else pltpu.roll(col, m, 1) for m in range(per_group)], axis=0
            ).astype(BF16)
            z = dot(picked[...], spread)
            z_hi = z.astype(BF16)
            z_lo = (z - z_hi.astype(F32)).astype(BF16)
            first = start + owner * rows + jnp.where(codes[s] >= 4, tiles * rows, 0)
            slots = ints[pl.ds(first, taps), :]
            inside = slots % per_group + ints[pl.ds(first + taps, taps), :] * per_group
            spots = [jnp.where(row == inside[k : k + 1], 1.0, 0.0).astype(BF16) for k in range(taps)]
            acc = jnp.zeros((2 * chans, side), F32)
            for group in range(count // per_group):
                here = jnp.where(slots // per_group == group, 1.0, 0.0).astype(BF16)
                hits = sum(spots[k] * here[k : k + 1] for k in range(taps))
                at = slice(group * chans, (group + 1) * chans)
                acc = acc + dot(jnp.concatenate([z_hi[at], z_lo[at]], axis=0), hits)
            out_ref[dest, :] = (acc[:chans] + acc[chans:]).astype(BF16)

    others_copy.wait()
    for s in range(4):
        owner = neigh[s]
        edge = codes[s] % 4
        dest = pl.ds((count + s) * chans, chans)

        @pl.when(edge < 2)
        def _():
            at = jnp.where(edge == 0, 0, side - 1)
            acc = jnp.zeros((chans, side), F32)
            for k in range(taps):
                slot = scalars[tiles * tiles + owner * 2 * taps + k, at]
                kind = scalars[tiles * tiles + owner * 2 * taps + taps + k, at]
                acc = acc + dot(block_of(owner, slot), table_ref[kind])
            out_ref[dest, :] = acc.astype(BF16)

            @pl.when(codes[s] >= 4)
            def _():
                out_ref[dest, :] = dot(acc.astype(BF16), flip).astype(BF16)


def filter_kernel(chans, last, filters, out_ref):
    outs, all_chans = filters.shape[2:]
    half = all_chans // 2
    me = lax.axis_index("chan")
    lane = lax.broadcasted_iota(jnp.int32, (outs, all_chans), 1)
    for b in range(3):
        first, second = [], []
        for a in range(3):
            value = filters[a, b].astype(F32)
            width = chans
            bit = 1
            while width < all_chans:
                other = jnp.where(
                    lane // width % 2 == 0, pltpu.roll(value, all_chans - width, 1), pltpu.roll(value, width, 1)
                )
                value = jnp.where((me & bit) != 0, other, value)
                width *= 2
                bit *= 2
            first.append(value)
            second.append(pltpu.roll(value, half, 1))
        low, high = (second, first) if last else (first, second)
        at = slice(b * outs, (b + 1) * outs)
        out_ref[at, :all_chans] = jnp.where(lane < half, low[0], high[1]).astype(BF16)
        out_ref[at, all_chans:] = low[2][:, :half].astype(BF16)


def tile_kernel(dims, last, many, *refs):
    side, chans, cap, tiles, all_chans, outs = dims
    parts = refs[:many]
    refs = refs[many:]
    if last:
        before_ref, *refs = refs
    slots_ref, weights_ref, table_ref, matrix, out_ref, slots, weights, image, *refs = refs
    if last:
        spread, staged, out_sems, sems = refs
    else:
        (sems,) = refs
    taps = slots.shape[0]
    count = tiles * cap
    half = chans * many
    copies = start_all(sems, [(slots_ref, slots), (weights_ref, weights)])

    def channels(index):
        return jnp.concatenate([part[index] for part in parts], axis=0)

    image[0:half, :] = channels(count)
    image[(side + 1) * half :, :] = channels(count + 1)
    wide = lax.broadcasted_iota(jnp.int32, (half, side), 1)

    def around(edge):
        value = channels(count + edge).astype(F32)
        before = jnp.where(wide == 0, 0.0, pltpu.roll(value, 1, 1))
        after = jnp.where(wide == side - 1, 0.0, pltpu.roll(value, side - 1, 1))
        return jnp.concatenate([before, value, after], axis=0).astype(BF16)

    left = dot(matrix[0:outs, :], around(2))
    right = dot(matrix[2 * outs :, :], around(3))
    if last:
        left = left + before_ref[side]
        right = right + before_ref[side + 1]
    else:
        out_ref[side] = left
        out_ref[side + 1] = right
    for copy in copies:
        copy.wait()

    def remap(r):
        lhs = jnp.concatenate([channels(slots[k, r]) for k in range(taps)], axis=1)
        rhs = jnp.concatenate([table_ref[weights[k, r]] for k in range(taps)], axis=0)
        return dot(lhs, rhs).astype(BF16)

    def place(r):
        image[(r + 1) * half : (r + 2) * half, :] = remap(r)

    lane = lax.broadcasted_iota(jnp.int32, (outs, side), 1)

    def multiply(i):
        x0 = image[i * half : (i + 3) * half, :]
        x1 = image[(i + 1) * half : (i + 4) * half, :]
        return dot(matrix[...], jnp.concatenate([x0, x1], axis=1))

    def combine(i, y):
        at_left = pltpu.roll(left, (side - i) % side, 1) if last else 0.0
        at_right = pltpu.roll(right, side - 1 - i, 1) if last else 0.0
        from_left = jnp.where(lane == 0, at_left, pltpu.roll(y[:outs], 1, 1))
        from_right = jnp.where(lane == side - 1, at_right, pltpu.roll(y[2 * outs :], side - 1, 1))
        total = y[outs : 2 * outs] + from_left + from_right
        if last:
            at = i % SEND * (outs + 1)
            spread[at : at + outs, :] = total + before_ref[i]
        else:
            out_ref[i] = total

    sent = []

    def finish(i, y):
        for h in range(2):
            combine(i + h, y[:, h * side : (h + 1) * side])
        if last and (i + 2) % SEND == 0:
            rows = pl.ds(i + 2 - SEND, SEND)
            step = outs // PIECES if i + 2 == side else outs
            for begin in range(0, outs, step):
                for o in range(begin, begin + step):
                    staged[o, rows, :] = spread[pl.ds(o, SEND, stride=outs + 1), :].astype(BF16)
                some = pl.ds(begin, step)
                sent.append(
                    pltpu.make_async_copy(staged.at[some, rows, :], out_ref.at[some, rows, :], out_sems.at[len(sent)])
                )
                sent[-1].start()

    for r in range(AHEAD + 1):
        place(r)
    for i in range(0, side, 2):
        for r in range(i + AHEAD + 1, min(i + AHEAD + 3, side)):
            place(r)
        finish(i, multiply(i))
    for copy in sent:
        copy.wait()


def body(source, send_list, block_slot, weight_index, remap_table, neighbour_tile, neighbour_edge, conv_weight):
    kinds, side = remap_table.shape[:2]
    chans = source.shape[0]
    tiles, cap = send_list.shape[1:]
    taps = block_slot.shape[1]
    blocks = source.shape[1] // side
    count = tiles * cap
    all_chans, outs = conv_weight.shape[2:]
    parts = lax.axis_size("chan")
    rows = round_up(2 * taps + tiles, 16)
    params = pltpu.CompilerParams(vmem_limit_bytes=LIMIT)
    slots, weights = in_hbm(block_slot.T), in_hbm(weight_index.T)
    filters = in_hbm(conv_weight.transpose(0, 1, 3, 2))
    packed, slots, weights, table, filters = pl.pallas_call(
        pack_kernel,
        out_shape=[
            jax.ShapeDtypeStruct((blocks * chans + rows, side), BF16),
            jax.ShapeDtypeStruct(slots.shape, jnp.int32),
            jax.ShapeDtypeStruct(weights.shape, jnp.int32),
            jax.ShapeDtypeStruct(remap_table.shape, BF16),
            jax.ShapeDtypeStruct(filters.shape, BF16),
        ],
        in_specs=[HBM] * 8,
        out_specs=[VMEM] * 5,
        scratch_shapes=[
            pltpu.VMEM((tiles, cap), jnp.int32),
            pltpu.VMEM(neighbour_tile.shape, jnp.int32),
            pltpu.VMEM(neighbour_edge.shape, jnp.int32),
            pltpu.SemaphoreType.DMA((blocks + 7,)),
        ],
        compiler_params=params,
        name="pack",
    )(
        slots, weights, in_hbm(send_list), in_hbm(neighbour_tile), in_hbm(neighbour_edge), in_hbm(source),
        in_hbm(remap_table), filters,
    )
    gathered = lax.all_gather(packed, "tile", axis=1, tiled=True)
    mine = pl.pallas_call(
        functools.partial(edge_kernel, (side, chans, blocks, tiles, cap, taps, rows)),
        out_shape=jax.ShapeDtypeStruct(((count + 4) * chans, side), BF16),
        in_specs=[VMEM, VMEM],
        out_specs=VMEM,
        scratch_shapes=[
            pltpu.VMEM((tiles * (tiles + 2 * taps + 2 * rows), side), jnp.int32),
            pltpu.SMEM((tiles * (tiles + 2 * taps), side), jnp.int32),
            pltpu.VMEM((count * kinds // side * chans, side * side // kinds), BF16),
            pltpu.VMEM((side, side), F32),
            pltpu.SemaphoreType.DMA((2,)),
        ],
        compiler_params=params,
        name="edges",
    )(gathered, table)

    def swap(value, flip):
        return lax.ppermute(value, "chan", [(i, i ^ flip) for i in range(parts)])

    def spread(held, bit):
        while bit:
            for flip in list(held):
                held[flip ^ bit] = swap(held[flip], bit)
            bit //= 2
        return [held[f].reshape(count + 4, chans, side) for f in sorted(held)]

    many = parts // 2
    half = all_chans // 2
    mine, filters = lax.optimization_barrier((mine, filters))
    near = spread({0: mine}, many // 2)
    def matrix(last, filters):
        return pl.pallas_call(
            functools.partial(filter_kernel, chans, last),
            out_shape=jax.ShapeDtypeStruct((3 * outs, 3 * half), BF16),
            in_specs=[VMEM],
            out_specs=VMEM,
            compiler_params=params,
            name="filters",
        )(filters)

    near_filters = matrix(False, filters)
    across = swap(mine, many)
    dims = (side, chans, cap, tiles, all_chans, outs)
    scratch = [
        pltpu.SMEM(slots.shape, jnp.int32),
        pltpu.SMEM(weights.shape, jnp.int32),
        pltpu.VMEM(((side + 2) * half, side), BF16),
    ]
    flops = 2 * side * half * taps * side * side + 2 * side * side * 9 * half * outs
    cost = pl.CostEstimate(flops=flops, bytes_accessed=(side + 2) * outs * side * 4, transcendentals=0)
    so_far = pl.pallas_call(
        functools.partial(tile_kernel, dims, False, many),
        out_shape=jax.ShapeDtypeStruct((side + 2, outs, side), F32),
        in_specs=[VMEM] * (many + 4),
        out_specs=VMEM,
        scratch_shapes=scratch + [pltpu.SemaphoreType.DMA((2,))],
        compiler_params=params,
        cost_estimate=cost,
        name="near",
    )(*near, slots, weights, table, near_filters)
    filters, so_far = lax.optimization_barrier((filters, so_far))
    far_filters = matrix(True, filters)
    across, so_far, far_filters = lax.optimization_barrier((across, so_far, far_filters))
    far = spread({many: across}, many // 2)
    return pl.pallas_call(
        functools.partial(tile_kernel, dims, True, many),
        out_shape=jax.ShapeDtypeStruct((outs, side, side), BF16),
        in_specs=[VMEM] * (many + 5),
        out_specs=HBM,
        scratch_shapes=scratch
        + [
            pltpu.VMEM((round_up(SEND * (outs + 1), 8), side), F32),
            pltpu.VMEM((outs, side, side), BF16),
            pltpu.SemaphoreType.DMA((side // SEND + PIECES - 1,)),
            pltpu.SemaphoreType.DMA((2,)),
        ],
        compiler_params=params,
        cost_estimate=cost,
        name="far",
    )(*far, so_far, slots, weights, table, far_filters)


def solution(mesh):
    in_specs = (
        P("chan", ("group", "tile")),
        P("tile", None, None),
        P("tile", None),
        P("tile", None),
        P(),
        P("tile", None),
        P("tile", None),
        P(None, None, None, "chan"),
    )
    out_specs = P("chan", ("group", "tile"), None)
    return jax.shard_map(body, mesh=mesh, in_specs=in_specs, out_specs=out_specs, check_vma=False)
```

```python
import functools

import jax
import jax.numpy as jnp
from jax import lax
from jax.experimental import pallas as pl
from jax.experimental.pallas import tpu as pltpu
from jax.sharding import PartitionSpec as P

F32 = jnp.float32
BF16 = jnp.bfloat16
VMEM = pl.BlockSpec(memory_space=pltpu.VMEM)
HBM = pl.BlockSpec(memory_space=pltpu.HBM)
LIMIT = 32 * 2**20
SEND = 16
AHEAD = 8
PIECES = 4


def round_up(value, step):
    return -(-value // step) * step


def in_hbm(value):
    return pltpu.with_memory_space_constraint(value, pltpu.HBM)


def dot(a, b):
    return jnp.dot(a, b, preferred_element_type=F32)


def start_all(sems, pairs):
    copies = [pltpu.make_async_copy(src, dst, sems.at[n]) for n, (src, dst) in enumerate(pairs)]
    for copy in copies:
        copy.start()
    return copies


def pack_kernel(
    slots_hbm, weights_hbm, lists_hbm, neigh_hbm, codes_hbm, source_hbm, table_hbm, filters_hbm,
    out_ref, slots, weights, table_ref, filters, lists, neigh, codes, sems,
):
    side = out_ref.shape[1]
    chans = source_hbm.shape[0]
    blocks = source_hbm.shape[1] // side
    base = blocks * chans
    copies = start_all(
        sems,
        [(slots_hbm, slots), (weights_hbm, weights), (lists_hbm.at[0], lists), (neigh_hbm, neigh), (codes_hbm, codes)]
        + [
            (source_hbm.at[:, pl.ds(block * side, side)], out_ref.at[pl.ds(block * chans, chans), :])
            for block in range(blocks)
        ]
        + [(table_hbm, table_ref), (filters_hbm, filters)],
    )
    for copy in copies[:5]:
        copy.wait()
    taps = slots.shape[0]
    tiles, cap = lists.shape
    rows = out_ref.shape[0] - base
    sides = jnp.concatenate([neigh[...], codes[...]], axis=1).astype(F32)
    wide = jnp.concatenate(
        [
            lists[...].astype(F32),
            jnp.concatenate([sides, jnp.zeros((tiles - 1, sides.shape[1]), F32)], axis=0),
            jnp.zeros((tiles, side - cap - sides.shape[1]), F32),
        ],
        axis=1,
    )
    parts = [slots[...].astype(F32), weights[...].astype(F32), wide]
    if rows > 2 * taps + tiles:
        parts.append(jnp.zeros((rows - 2 * taps - tiles, side), F32))
    out_ref[base:, :] = jnp.concatenate(parts, axis=0).astype(BF16)
    for copy in copies[5:]:
        copy.wait()


def edge_kernel(dims, gathered_ref, table_ref, out_ref, ints, scalars, picked, columns, sems):
    side, chans, blocks, tiles, cap, taps, rows = dims
    count = tiles * cap
    base = blocks * chans
    kinds = table_ref.shape[0]
    per_group = side // kinds
    me = lax.axis_index("tile")
    tables = jnp.concatenate([gathered_ref[base:, band * side : (band + 1) * side] for band in range(tiles)], axis=0)
    values = tables.astype(F32).astype(jnp.int32)
    lists = pl.ds(0, tiles * tiles)
    others = pl.ds(tiles * tiles, tiles * 2 * taps)
    start = tiles * (tiles + 2 * taps)
    for band in range(tiles):
        ints[band * tiles : (band + 1) * tiles, :] = values[band * rows + 2 * taps : band * rows + 2 * taps + tiles]
    lists_copy = pltpu.make_async_copy(ints.at[lists, :], scalars.at[lists, :], sems.at[0])
    lists_copy.start()
    for band in range(tiles):
        at = tiles * tiles + band * 2 * taps
        ints[at : at + 2 * taps, :] = values[band * rows : band * rows + 2 * taps]
    others_copy = pltpu.make_async_copy(ints.at[others, :], scalars.at[others, :], sems.at[1])
    others_copy.start()
    ints[start : start + tiles * rows, :] = values
    row = lax.broadcasted_iota(jnp.int32, (side, side), 0)
    flip = (lax.broadcasted_iota(jnp.int32, (side, side), 1) + row == side - 1).astype(BF16)
    ints[start + tiles * rows :, :] = dot(tables, flip).astype(jnp.int32)
    lane = lax.broadcasted_iota(jnp.int32, (side, side), 1)
    total = jnp.zeros((side, side), F32)
    for kind in range(kinds):
        moved = pltpu.roll(table_ref[kind].astype(F32), per_group * kind + 1, 1)
        total = jnp.where(lane // per_group == kind, moved, total)
    columns[...] = total
    lists_copy.wait()
    own_row = me * tiles
    neigh = [scalars[own_row, cap + s] for s in range(4)]
    codes = [scalars[own_row, cap + 4 + s] for s in range(4)]

    def block_of(owner, slot):
        band = slot // cap
        local = scalars[band * tiles + owner, slot % cap]
        return gathered_ref[pl.ds(pl.multiple_of(local * chans, chans), chans), pl.ds(pl.multiple_of(band * side, side), side)]

    for slot in range(count):
        out_ref[slot * chans : (slot + 1) * chans, :] = block_of(me, slot)
    for s in range(4):
        owner = neigh[s]
        edge = codes[s] % 4
        dest = pl.ds((count + s) * chans, chans)

        @pl.when(edge >= 2)
        def _():
            for slot in range(count):
                group, member = slot // per_group, slot % per_group
                picked[group * chans : (group + 1) * chans, member * side : (member + 1) * side] = block_of(owner, slot)
            col = columns[...]
            col = jnp.where(edge == 2, pltpu.roll(col, side - 1, 1), col)
            col = jnp.where(lane % per_group == 0, col, 0.0)
            spread = jnp.concatenate(
                [col if m == 0 else pltpu.roll(col, m, 1) for m in range(per_group)], axis=0
            ).astype(BF16)
            z = dot(picked[...], spread)
            z_hi = z.astype(BF16)
            z_lo = (z - z_hi.astype(F32)).astype(BF16)
            first = start + owner * rows + jnp.where(codes[s] >= 4, tiles * rows, 0)
            slots = ints[pl.ds(first, taps), :]
            inside = slots % per_group + ints[pl.ds(first + taps, taps), :] * per_group
            spots = [jnp.where(row == inside[k : k + 1], 1.0, 0.0).astype(BF16) for k in range(taps)]
            acc = jnp.zeros((2 * chans, side), F32)
            for group in range(count // per_group):
                here = jnp.where(slots // per_group == group, 1.0, 0.0).astype(BF16)
                hits = sum(spots[k] * here[k : k + 1] for k in range(taps))
                at = slice(group * chans, (group + 1) * chans)
                acc = acc + dot(jnp.concatenate([z_hi[at], z_lo[at]], axis=0), hits)
            out_ref[dest, :] = (acc[:chans] + acc[chans:]).astype(BF16)

    others_copy.wait()
    for s in range(4):
        owner = neigh[s]
        edge = codes[s] % 4
        dest = pl.ds((count + s) * chans, chans)

        @pl.when(edge < 2)
        def _():
            at = jnp.where(edge == 0, 0, side - 1)
            acc = jnp.zeros((chans, side), F32)
            for k in range(taps):
                slot = scalars[tiles * tiles + owner * 2 * taps + k, at]
                kind = scalars[tiles * tiles + owner * 2 * taps + taps + k, at]
                acc = acc + dot(block_of(owner, slot), table_ref[kind])
            out_ref[dest, :] = acc.astype(BF16)

            @pl.when(codes[s] >= 4)
            def _():
                out_ref[dest, :] = dot(acc.astype(BF16), flip).astype(BF16)


def filter_kernel(chans, last, filters, out_ref):
    outs, all_chans = filters.shape[2:]
    half = all_chans // 2
    me = lax.axis_index("chan")
    lane = lax.broadcasted_iota(jnp.int32, (outs, all_chans), 1)
    for b in range(3):
        first, second = [], []
        for a in range(3):
            value = filters[a, b].astype(F32)
            width = chans
            bit = 1
            while width < all_chans:
                other = jnp.where(
                    lane // width % 2 == 0, pltpu.roll(value, all_chans - width, 1), pltpu.roll(value, width, 1)
                )
                value = jnp.where((me & bit) != 0, other, value)
                width *= 2
                bit *= 2
            first.append(value)
            second.append(pltpu.roll(value, half, 1))
        low, high = (second, first) if last else (first, second)
        at = slice(b * outs, (b + 1) * outs)
        out_ref[at, :all_chans] = jnp.where(lane < half, low[0], high[1]).astype(BF16)
        out_ref[at, all_chans:] = low[2][:, :half].astype(BF16)


def tile_kernel(dims, last, many, *refs):
    side, chans, cap, tiles, all_chans, outs = dims
    parts = refs[:many]
    refs = refs[many:]
    if last:
        before_ref, *refs = refs
    slots_ref, weights_ref, table_ref, matrix, out_ref, slots, weights, image, *refs = refs
    if last:
        spread, staged, out_sems, sems = refs
    else:
        (sems,) = refs
    taps = slots.shape[0]
    count = tiles * cap
    half = chans * many
    copies = start_all(sems, [(slots_ref, slots), (weights_ref, weights)])

    def channels(index):
        return jnp.concatenate([part[index] for part in parts], axis=0)

    image[0:half, :] = channels(count)
    image[(side + 1) * half :, :] = channels(count + 1)
    wide = lax.broadcasted_iota(jnp.int32, (half, side), 1)

    def around(edge):
        value = channels(count + edge).astype(F32)
        before = jnp.where(wide == 0, 0.0, pltpu.roll(value, 1, 1))
        after = jnp.where(wide == side - 1, 0.0, pltpu.roll(value, side - 1, 1))
        return jnp.concatenate([before, value, after], axis=0).astype(BF16)

    left = dot(matrix[0:outs, :], around(2))
    right = dot(matrix[2 * outs :, :], around(3))
    if last:
        left = left + before_ref[side]
        right = right + before_ref[side + 1]
    else:
        out_ref[side] = left
        out_ref[side + 1] = right
    for copy in copies:
        copy.wait()

    def remap(r):
        lhs = jnp.concatenate([channels(slots[k, r]) for k in range(taps)], axis=1)
        rhs = jnp.concatenate([table_ref[weights[k, r]] for k in range(taps)], axis=0)
        return dot(lhs, rhs).astype(BF16)

    def place(r):
        image[(r + 1) * half : (r + 2) * half, :] = remap(r)

    lane = lax.broadcasted_iota(jnp.int32, (outs, side), 1)

    def multiply(i):
        x0 = image[i * half : (i + 3) * half, :]
        x1 = image[(i + 1) * half : (i + 4) * half, :]
        return dot(matrix[...], jnp.concatenate([x0, x1], axis=1))

    def combine(i, y):
        at_left = pltpu.roll(left, (side - i) % side, 1) if last else 0.0
        at_right = pltpu.roll(right, side - 1 - i, 1) if last else 0.0
        from_left = jnp.where(lane == 0, at_left, pltpu.roll(y[:outs], 1, 1))
        from_right = jnp.where(lane == side - 1, at_right, pltpu.roll(y[2 * outs :], side - 1, 1))
        total = y[outs : 2 * outs] + from_left + from_right
        if last:
            at = i % SEND * (outs + 1)
            spread[at : at + outs, :] = total + before_ref[i]
        else:
            out_ref[i] = total

    sent = []

    def finish(i, y):
        for h in range(2):
            combine(i + h, y[:, h * side : (h + 1) * side])
        if last and (i + 2) % SEND == 0:
            rows = pl.ds(i + 2 - SEND, SEND)
            step = outs // PIECES if i + 2 == side else outs
            for begin in range(0, outs, step):
                for o in range(begin, begin + step):
                    staged[o, rows, :] = spread[pl.ds(o, SEND, stride=outs + 1), :].astype(BF16)
                some = pl.ds(begin, step)
                sent.append(
                    pltpu.make_async_copy(staged.at[some, rows, :], out_ref.at[some, rows, :], out_sems.at[len(sent)])
                )
                sent[-1].start()

    for r in range(AHEAD + 1):
        place(r)
    for i in range(0, side, 2):
        for r in range(i + AHEAD + 1, min(i + AHEAD + 3, side)):
            place(r)
        finish(i, multiply(i))
    for copy in sent:
        copy.wait()


def body(source, send_list, block_slot, weight_index, remap_table, neighbour_tile, neighbour_edge, conv_weight):
    kinds, side = remap_table.shape[:2]
    chans = source.shape[0]
    tiles, cap = send_list.shape[1:]
    taps = block_slot.shape[1]
    blocks = source.shape[1] // side
    count = tiles * cap
    all_chans, outs = conv_weight.shape[2:]
    parts = lax.axis_size("chan")
    rows = round_up(2 * taps + tiles, 16)
    params = pltpu.CompilerParams(vmem_limit_bytes=LIMIT)
    slots, weights = in_hbm(block_slot.T), in_hbm(weight_index.T)
    filters = in_hbm(conv_weight.transpose(0, 1, 3, 2))
    packed, slots, weights, table, filters = pl.pallas_call(
        pack_kernel,
        out_shape=[
            jax.ShapeDtypeStruct((blocks * chans + rows, side), BF16),
            jax.ShapeDtypeStruct(slots.shape, jnp.int32),
            jax.ShapeDtypeStruct(weights.shape, jnp.int32),
            jax.ShapeDtypeStruct(remap_table.shape, BF16),
            jax.ShapeDtypeStruct(filters.shape, BF16),
        ],
        in_specs=[HBM] * 8,
        out_specs=[VMEM] * 5,
        scratch_shapes=[
            pltpu.VMEM((tiles, cap), jnp.int32),
            pltpu.VMEM(neighbour_tile.shape, jnp.int32),
            pltpu.VMEM(neighbour_edge.shape, jnp.int32),
            pltpu.SemaphoreType.DMA((blocks + 7,)),
        ],
        compiler_params=params,
        name="pack",
    )(
        slots, weights, in_hbm(send_list), in_hbm(neighbour_tile), in_hbm(neighbour_edge), in_hbm(source),
        in_hbm(remap_table), filters,
    )
    gathered = lax.all_gather(packed, "tile", axis=1, tiled=True)
    mine = pl.pallas_call(
        functools.partial(edge_kernel, (side, chans, blocks, tiles, cap, taps, rows)),
        out_shape=jax.ShapeDtypeStruct(((count + 4) * chans, side), BF16),
        in_specs=[VMEM, VMEM],
        out_specs=VMEM,
        scratch_shapes=[
            pltpu.VMEM((tiles * (tiles + 2 * taps + 2 * rows), side), jnp.int32),
            pltpu.SMEM((tiles * (tiles + 2 * taps), side), jnp.int32),
            pltpu.VMEM((count * kinds // side * chans, side * side // kinds), BF16),
            pltpu.VMEM((side, side), F32),
            pltpu.SemaphoreType.DMA((2,)),
        ],
        compiler_params=params,
        name="edges",
    )(gathered, table)

    def swap(value, flip):
        return lax.ppermute(value, "chan", [(i, i ^ flip) for i in range(parts)])

    def spread(held, bit):
        while bit:
            for flip in list(held):
                held[flip ^ bit] = swap(held[flip], bit)
            bit //= 2
        return [held[f].reshape(count + 4, chans, side) for f in sorted(held)]

    many = parts // 2
    half = all_chans // 2
    mine, filters = lax.optimization_barrier((mine, filters))
    near = spread({0: mine}, many // 2)
    def matrix(last, filters):
        return pl.pallas_call(
            functools.partial(filter_kernel, chans, last),
            out_shape=jax.ShapeDtypeStruct((3 * outs, 3 * half), BF16),
            in_specs=[VMEM],
            out_specs=VMEM,
            compiler_params=params,
            name="filters",
        )(filters)

    near_filters = matrix(False, filters)
    across = swap(mine, many)
    dims = (side, chans, cap, tiles, all_chans, outs)
    scratch = [
        pltpu.SMEM(slots.shape, jnp.int32),
        pltpu.SMEM(weights.shape, jnp.int32),
        pltpu.VMEM(((side + 2) * half, side), BF16),
    ]
    flops = 2 * side * half * taps * side * side + 2 * side * side * 9 * half * outs
    cost = pl.CostEstimate(flops=flops, bytes_accessed=(side + 2) * outs * side * 4, transcendentals=0)
    so_far = pl.pallas_call(
        functools.partial(tile_kernel, dims, False, many),
        out_shape=jax.ShapeDtypeStruct((side + 2, outs, side), F32),
        in_specs=[VMEM] * (many + 4),
        out_specs=VMEM,
        scratch_shapes=scratch + [pltpu.SemaphoreType.DMA((2,))],
        compiler_params=params,
        cost_estimate=cost,
        name="near",
    )(*near, slots, weights, table, near_filters)
    across, filters, so_far = lax.optimization_barrier((across, filters, so_far))
    far = spread({many: across}, many // 2)
    far_filters = matrix(True, filters)
    return pl.pallas_call(
        functools.partial(tile_kernel, dims, True, many),
        out_shape=jax.ShapeDtypeStruct((outs, side, side), BF16),
        in_specs=[VMEM] * (many + 5),
        out_specs=HBM,
        scratch_shapes=scratch
        + [
            pltpu.VMEM((round_up(SEND * (outs + 1), 8), side), F32),
            pltpu.VMEM((outs, side, side), BF16),
            pltpu.SemaphoreType.DMA((side // SEND + PIECES - 1,)),
            pltpu.SemaphoreType.DMA((2,)),
        ],
        compiler_params=params,
        cost_estimate=cost,
        name="far",
    )(*far, so_far, slots, weights, table, far_filters)


def solution(mesh):
    in_specs = (
        P("chan", ("group", "tile")),
        P("tile", None, None),
        P("tile", None),
        P("tile", None),
        P(),
        P("tile", None),
        P("tile", None),
        P(None, None, None, "chan"),
    )
    out_specs = P("chan", ("group", "tile"), None)
    return jax.shard_map(body, mesh=mesh, in_specs=in_specs, out_specs=out_specs, check_vma=False)
```

```python
import functools

import jax
import jax.numpy as jnp
from jax import lax
from jax.experimental import pallas as pl
from jax.experimental.pallas import tpu as pltpu
from jax.sharding import PartitionSpec as P

F32 = jnp.float32
BF16 = jnp.bfloat16
VMEM = pl.BlockSpec(memory_space=pltpu.VMEM)
HBM = pl.BlockSpec(memory_space=pltpu.HBM)
LIMIT = 32 * 2**20
SEND = 16
AHEAD = 8
PIECES = 4


def round_up(value, step):
    return -(-value // step) * step


def in_hbm(value):
    return pltpu.with_memory_space_constraint(value, pltpu.HBM)


def dot(a, b):
    return jnp.dot(a, b, preferred_element_type=F32)


def start_all(sems, pairs):
    copies = [pltpu.make_async_copy(src, dst, sems.at[n]) for n, (src, dst) in enumerate(pairs)]
    for copy in copies:
        copy.start()
    return copies


def pack_kernel(
    slots_hbm, weights_hbm, lists_hbm, neigh_hbm, codes_hbm, source_hbm, table_hbm, filters_hbm,
    out_ref, slots, weights, table_ref, filters, lists, neigh, codes, sems,
):
    side = out_ref.shape[1]
    chans = source_hbm.shape[0]
    blocks = source_hbm.shape[1] // side
    base = blocks * chans
    copies = start_all(
        sems,
        [(slots_hbm, slots), (weights_hbm, weights), (lists_hbm.at[0], lists), (neigh_hbm, neigh), (codes_hbm, codes)]
        + [
            (source_hbm.at[:, pl.ds(block * side, side)], out_ref.at[pl.ds(block * chans, chans), :])
            for block in range(blocks)
        ]
        + [(table_hbm, table_ref), (filters_hbm, filters)],
    )
    for copy in copies[:5]:
        copy.wait()
    taps = slots.shape[0]
    tiles, cap = lists.shape
    rows = out_ref.shape[0] - base
    sides = jnp.concatenate([neigh[...], codes[...]], axis=1).astype(F32)
    wide = jnp.concatenate(
        [
            lists[...].astype(F32),
            jnp.concatenate([sides, jnp.zeros((tiles - 1, sides.shape[1]), F32)], axis=0),
            jnp.zeros((tiles, side - cap - sides.shape[1]), F32),
        ],
        axis=1,
    )
    parts = [slots[...].astype(F32), weights[...].astype(F32), wide]
    if rows > 2 * taps + tiles:
        parts.append(jnp.zeros((rows - 2 * taps - tiles, side), F32))
    out_ref[base:, :] = jnp.concatenate(parts, axis=0).astype(BF16)
    for copy in copies[5:]:
        copy.wait()


def edge_kernel(dims, gathered_ref, table_ref, out_ref, ints, scalars, picked, columns, sems):
    side, chans, blocks, tiles, cap, taps, rows = dims
    count = tiles * cap
    base = blocks * chans
    kinds = table_ref.shape[0]
    per_group = side // kinds
    me = lax.axis_index("tile")
    tables = jnp.concatenate([gathered_ref[base:, band * side : (band + 1) * side] for band in range(tiles)], axis=0)
    values = tables.astype(F32).astype(jnp.int32)
    lists = pl.ds(0, tiles * tiles)
    others = pl.ds(tiles * tiles, tiles * 2 * taps)
    start = tiles * (tiles + 2 * taps)
    for band in range(tiles):
        ints[band * tiles : (band + 1) * tiles, :] = values[band * rows + 2 * taps : band * rows + 2 * taps + tiles]
    lists_copy = pltpu.make_async_copy(ints.at[lists, :], scalars.at[lists, :], sems.at[0])
    lists_copy.start()
    for band in range(tiles):
        at = tiles * tiles + band * 2 * taps
        ints[at : at + 2 * taps, :] = values[band * rows : band * rows + 2 * taps]
    others_copy = pltpu.make_async_copy(ints.at[others, :], scalars.at[others, :], sems.at[1])
    others_copy.start()
    ints[start : start + tiles * rows, :] = values
    row = lax.broadcasted_iota(jnp.int32, (side, side), 0)
    flip = (lax.broadcasted_iota(jnp.int32, (side, side), 1) + row == side - 1).astype(BF16)
    ints[start + tiles * rows :, :] = dot(tables, flip).astype(jnp.int32)
    lane = lax.broadcasted_iota(jnp.int32, (side, side), 1)
    total = jnp.zeros((side, side), F32)
    for kind in range(kinds):
        moved = pltpu.roll(table_ref[kind].astype(F32), per_group * kind + 1, 1)
        total = jnp.where(lane // per_group == kind, moved, total)
    for n, moved in enumerate([pltpu.roll(total, side - 1, 1), total]):
        moved = jnp.where(lane % per_group == 0, moved, 0.0)
        for m in range(per_group):
            columns[n, m * side : (m + 1) * side, :] = (moved if m == 0 else pltpu.roll(moved, m, 1)).astype(BF16)
    lists_copy.wait()
    own_row = me * tiles
    neigh = [scalars[own_row, cap + s] for s in range(4)]
    codes = [scalars[own_row, cap + 4 + s] for s in range(4)]

    def block_of(owner, slot):
        band = slot // cap
        local = scalars[band * tiles + owner, slot % cap]
        return gathered_ref[pl.ds(pl.multiple_of(local * chans, chans), chans), pl.ds(pl.multiple_of(band * side, side), side)]

    for slot in range(count):
        out_ref[slot * chans : (slot + 1) * chans, :] = block_of(me, slot)
    for s in range(4):
        owner = neigh[s]
        edge = codes[s] % 4
        dest = pl.ds((count + s) * chans, chans)

        @pl.when(edge >= 2)
        def _():
            for slot in range(count):
                group, member = slot // per_group, slot % per_group
                picked[group * chans : (group + 1) * chans, member * side : (member + 1) * side] = block_of(owner, slot)
            z = dot(picked[...], columns[edge - 2])
            z_hi = z.astype(BF16)
            z_lo = (z - z_hi.astype(F32)).astype(BF16)
            first = start + owner * rows + jnp.where(codes[s] >= 4, tiles * rows, 0)
            slots = ints[pl.ds(first, taps), :]
            inside = slots % per_group + ints[pl.ds(first + taps, taps), :] * per_group
            spots = [jnp.where(row == inside[k : k + 1], 1.0, 0.0).astype(BF16) for k in range(taps)]
            acc = jnp.zeros((2 * chans, side), F32)
            for group in range(count // per_group):
                here = jnp.where(slots // per_group == group, 1.0, 0.0).astype(BF16)
                hits = sum(spots[k] * here[k : k + 1] for k in range(taps))
                at = slice(group * chans, (group + 1) * chans)
                acc = acc + dot(jnp.concatenate([z_hi[at], z_lo[at]], axis=0), hits)
            out_ref[dest, :] = (acc[:chans] + acc[chans:]).astype(BF16)

    others_copy.wait()
    for s in range(4):
        owner = neigh[s]
        edge = codes[s] % 4
        dest = pl.ds((count + s) * chans, chans)

        @pl.when(edge < 2)
        def _():
            at = jnp.where(edge == 0, 0, side - 1)
            acc = jnp.zeros((chans, side), F32)
            for k in range(taps):
                slot = scalars[tiles * tiles + owner * 2 * taps + k, at]
                kind = scalars[tiles * tiles + owner * 2 * taps + taps + k, at]
                acc = acc + dot(block_of(owner, slot), table_ref[kind])
            out_ref[dest, :] = acc.astype(BF16)

            @pl.when(codes[s] >= 4)
            def _():
                out_ref[dest, :] = dot(acc.astype(BF16), flip).astype(BF16)


def filter_kernel(chans, last, filters, out_ref):
    outs, all_chans = filters.shape[2:]
    half = all_chans // 2
    me = lax.axis_index("chan")
    lane = lax.broadcasted_iota(jnp.int32, (outs, all_chans), 1)
    for b in range(3):
        first, second = [], []
        for a in range(3):
            value = filters[a, b].astype(F32)
            width = chans
            bit = 1
            while width < all_chans:
                other = jnp.where(
                    lane // width % 2 == 0, pltpu.roll(value, all_chans - width, 1), pltpu.roll(value, width, 1)
                )
                value = jnp.where((me & bit) != 0, other, value)
                width *= 2
                bit *= 2
            first.append(value)
            second.append(pltpu.roll(value, half, 1))
        low, high = (second, first) if last else (first, second)
        at = slice(b * outs, (b + 1) * outs)
        out_ref[at, :all_chans] = jnp.where(lane < half, low[0], high[1]).astype(BF16)
        out_ref[at, all_chans:] = low[2][:, :half].astype(BF16)


def tile_kernel(dims, last, many, *refs):
    side, chans, cap, tiles, all_chans, outs = dims
    parts = refs[:many]
    refs = refs[many:]
    if last:
        before_ref, *refs = refs
    slots_ref, weights_ref, table_ref, matrix, out_ref, slots, weights, image, *refs = refs
    if last:
        spread, staged, out_sems, sems = refs
    else:
        (sems,) = refs
    taps = slots.shape[0]
    count = tiles * cap
    half = chans * many
    copies = start_all(sems, [(slots_ref, slots), (weights_ref, weights)])

    def channels(index):
        return jnp.concatenate([part[index] for part in parts], axis=0)

    image[0:half, :] = channels(count)
    image[(side + 1) * half :, :] = channels(count + 1)
    wide = lax.broadcasted_iota(jnp.int32, (half, side), 1)

    def around(edge):
        value = channels(count + edge).astype(F32)
        before = jnp.where(wide == 0, 0.0, pltpu.roll(value, 1, 1))
        after = jnp.where(wide == side - 1, 0.0, pltpu.roll(value, side - 1, 1))
        return jnp.concatenate([before, value, after], axis=0).astype(BF16)

    left = dot(matrix[0:outs, :], around(2))
    right = dot(matrix[2 * outs :, :], around(3))
    if last:
        left = left + before_ref[side]
        right = right + before_ref[side + 1]
    else:
        out_ref[side] = left
        out_ref[side + 1] = right
    for copy in copies:
        copy.wait()

    def remap(r):
        lhs = jnp.concatenate([channels(slots[k, r]) for k in range(taps)], axis=1)
        rhs = jnp.concatenate([table_ref[weights[k, r]] for k in range(taps)], axis=0)
        return dot(lhs, rhs).astype(BF16)

    def place(r):
        image[(r + 1) * half : (r + 2) * half, :] = remap(r)

    lane = lax.broadcasted_iota(jnp.int32, (outs, side), 1)

    def multiply(i):
        x0 = image[i * half : (i + 3) * half, :]
        x1 = image[(i + 1) * half : (i + 4) * half, :]
        return dot(matrix[...], jnp.concatenate([x0, x1], axis=1))

    def combine(i, y):
        at_left = pltpu.roll(left, (side - i) % side, 1) if last else 0.0
        at_right = pltpu.roll(right, side - 1 - i, 1) if last else 0.0
        from_left = jnp.where(lane == 0, at_left, pltpu.roll(y[:outs], 1, 1))
        from_right = jnp.where(lane == side - 1, at_right, pltpu.roll(y[2 * outs :], side - 1, 1))
        total = y[outs : 2 * outs] + from_left + from_right
        if last:
            at = i % SEND * (outs + 1)
            spread[at : at + outs, :] = total + before_ref[i]
        else:
            out_ref[i] = total

    sent = []

    def finish(i, y):
        for h in range(2):
            combine(i + h, y[:, h * side : (h + 1) * side])
        if last and (i + 2) % SEND == 0:
            rows = pl.ds(i + 2 - SEND, SEND)
            step = outs // PIECES if i + 2 == side else outs
            for begin in range(0, outs, step):
                for o in range(begin, begin + step):
                    staged[o, rows, :] = spread[pl.ds(o, SEND, stride=outs + 1), :].astype(BF16)
                some = pl.ds(begin, step)
                sent.append(
                    pltpu.make_async_copy(staged.at[some, rows, :], out_ref.at[some, rows, :], out_sems.at[len(sent)])
                )
                sent[-1].start()

    for r in range(AHEAD + 1):
        place(r)
    for i in range(0, side, 2):
        for r in range(i + AHEAD + 1, min(i + AHEAD + 3, side)):
            place(r)
        finish(i, multiply(i))
    for copy in sent:
        copy.wait()


def body(source, send_list, block_slot, weight_index, remap_table, neighbour_tile, neighbour_edge, conv_weight):
    kinds, side = remap_table.shape[:2]
    chans = source.shape[0]
    tiles, cap = send_list.shape[1:]
    taps = block_slot.shape[1]
    blocks = source.shape[1] // side
    count = tiles * cap
    all_chans, outs = conv_weight.shape[2:]
    parts = lax.axis_size("chan")
    rows = round_up(2 * taps + tiles, 16)
    params = pltpu.CompilerParams(vmem_limit_bytes=LIMIT)
    slots, weights = in_hbm(block_slot.T), in_hbm(weight_index.T)
    filters = in_hbm(conv_weight.transpose(0, 1, 3, 2))
    packed, slots, weights, table, filters = pl.pallas_call(
        pack_kernel,
        out_shape=[
            jax.ShapeDtypeStruct((blocks * chans + rows, side), BF16),
            jax.ShapeDtypeStruct(slots.shape, jnp.int32),
            jax.ShapeDtypeStruct(weights.shape, jnp.int32),
            jax.ShapeDtypeStruct(remap_table.shape, BF16),
            jax.ShapeDtypeStruct(filters.shape, BF16),
        ],
        in_specs=[HBM] * 8,
        out_specs=[VMEM] * 5,
        scratch_shapes=[
            pltpu.VMEM((tiles, cap), jnp.int32),
            pltpu.VMEM(neighbour_tile.shape, jnp.int32),
            pltpu.VMEM(neighbour_edge.shape, jnp.int32),
            pltpu.SemaphoreType.DMA((blocks + 7,)),
        ],
        compiler_params=params,
        name="pack",
    )(
        slots, weights, in_hbm(send_list), in_hbm(neighbour_tile), in_hbm(neighbour_edge), in_hbm(source),
        in_hbm(remap_table), filters,
    )
    gathered = lax.all_gather(packed, "tile", axis=1, tiled=True)
    mine = pl.pallas_call(
        functools.partial(edge_kernel, (side, chans, blocks, tiles, cap, taps, rows)),
        out_shape=jax.ShapeDtypeStruct(((count + 4) * chans, side), BF16),
        in_specs=[VMEM, VMEM],
        out_specs=VMEM,
        scratch_shapes=[
            pltpu.VMEM((tiles * (tiles + 2 * taps + 2 * rows), side), jnp.int32),
            pltpu.SMEM((tiles * (tiles + 2 * taps), side), jnp.int32),
            pltpu.VMEM((count * kinds // side * chans, side * side // kinds), BF16),
            pltpu.VMEM((2, side // kinds * side, side), BF16),
            pltpu.SemaphoreType.DMA((2,)),
        ],
        compiler_params=params,
        name="edges",
    )(gathered, table)

    def swap(value, flip):
        return lax.ppermute(value, "chan", [(i, i ^ flip) for i in range(parts)])

    def spread(held, bit):
        while bit:
            for flip in list(held):
                held[flip ^ bit] = swap(held[flip], bit)
            bit //= 2
        return [held[f].reshape(count + 4, chans, side) for f in sorted(held)]

    many = parts // 2
    half = all_chans // 2
    mine, filters = lax.optimization_barrier((mine, filters))
    near = spread({0: mine}, many // 2)
    def matrix(last, filters):
        return pl.pallas_call(
            functools.partial(filter_kernel, chans, last),
            out_shape=jax.ShapeDtypeStruct((3 * outs, 3 * half), BF16),
            in_specs=[VMEM],
            out_specs=VMEM,
            compiler_params=params,
            name="filters",
        )(filters)

    near_filters = matrix(False, filters)
    across = swap(mine, many)
    dims = (side, chans, cap, tiles, all_chans, outs)
    scratch = [
        pltpu.SMEM(slots.shape, jnp.int32),
        pltpu.SMEM(weights.shape, jnp.int32),
        pltpu.VMEM(((side + 2) * half, side), BF16),
    ]
    flops = 2 * side * half * taps * side * side + 2 * side * side * 9 * half * outs
    cost = pl.CostEstimate(flops=flops, bytes_accessed=(side + 2) * outs * side * 4, transcendentals=0)
    so_far = pl.pallas_call(
        functools.partial(tile_kernel, dims, False, many),
        out_shape=jax.ShapeDtypeStruct((side + 2, outs, side), F32),
        in_specs=[VMEM] * (many + 4),
        out_specs=VMEM,
        scratch_shapes=scratch + [pltpu.SemaphoreType.DMA((2,))],
        compiler_params=params,
        cost_estimate=cost,
        name="near",
    )(*near, slots, weights, table, near_filters)
    across, filters, so_far = lax.optimization_barrier((across, filters, so_far))
    far = spread({many: across}, many // 2)
    far_filters = matrix(True, filters)
    return pl.pallas_call(
        functools.partial(tile_kernel, dims, True, many),
        out_shape=jax.ShapeDtypeStruct((outs, side, side), BF16),
        in_specs=[VMEM] * (many + 5),
        out_specs=HBM,
        scratch_shapes=scratch
        + [
            pltpu.VMEM((round_up(SEND * (outs + 1), 8), side), F32),
            pltpu.VMEM((outs, side, side), BF16),
            pltpu.SemaphoreType.DMA((side // SEND + PIECES - 1,)),
            pltpu.SemaphoreType.DMA((2,)),
        ],
        compiler_params=params,
        cost_estimate=cost,
        name="far",
    )(*far, so_far, slots, weights, table, far_filters)


def solution(mesh):
    in_specs = (
        P("chan", ("group", "tile")),
        P("tile", None, None),
        P("tile", None),
        P("tile", None),
        P(),
        P("tile", None),
        P("tile", None),
        P(None, None, None, "chan"),
    )
    out_specs = P("chan", ("group", "tile"), None)
    return jax.shard_map(body, mesh=mesh, in_specs=in_specs, out_specs=out_specs, check_vma=False)
```

```python
import functools

import jax
import jax.numpy as jnp
from jax import lax
from jax.experimental import pallas as pl
from jax.experimental.pallas import tpu as pltpu
from jax.sharding import PartitionSpec as P

F32 = jnp.float32
BF16 = jnp.bfloat16
VMEM = pl.BlockSpec(memory_space=pltpu.VMEM)
HBM = pl.BlockSpec(memory_space=pltpu.HBM)
LIMIT = 32 * 2**20
SEND = 16
AHEAD = 8
PIECES = 4


def round_up(value, step):
    return -(-value // step) * step


def in_hbm(value):
    return pltpu.with_memory_space_constraint(value, pltpu.HBM)


def dot(a, b):
    return jnp.dot(a, b, preferred_element_type=F32)


def start_all(sems, pairs):
    copies = [pltpu.make_async_copy(src, dst, sems.at[n]) for n, (src, dst) in enumerate(pairs)]
    for copy in copies:
        copy.start()
    return copies


def pack_kernel(
    slots_hbm, weights_hbm, lists_hbm, neigh_hbm, codes_hbm, source_hbm, table_hbm, filters_hbm,
    out_ref, slots, weights, table_ref, filters, lists, neigh, codes, sems,
):
    side = out_ref.shape[1]
    chans = source_hbm.shape[0]
    blocks = source_hbm.shape[1] // side
    base = blocks * chans
    copies = start_all(
        sems,
        [(slots_hbm, slots), (weights_hbm, weights), (lists_hbm.at[0], lists), (neigh_hbm, neigh), (codes_hbm, codes)]
        + [
            (source_hbm.at[:, pl.ds(block * side, side)], out_ref.at[pl.ds(block * chans, chans), :])
            for block in range(blocks)
        ]
        + [(table_hbm, table_ref), (filters_hbm, filters)],
    )
    for copy in copies[:5]:
        copy.wait()
    taps = slots.shape[0]
    tiles, cap = lists.shape
    rows = out_ref.shape[0] - base
    sides = jnp.concatenate([neigh[...], codes[...]], axis=1).astype(F32)
    wide = jnp.concatenate(
        [
            lists[...].astype(F32),
            jnp.concatenate([sides, jnp.zeros((tiles - 1, sides.shape[1]), F32)], axis=0),
            jnp.zeros((tiles, side - cap - sides.shape[1]), F32),
        ],
        axis=1,
    )
    parts = [slots[...].astype(F32), weights[...].astype(F32), wide]
    if rows > 2 * taps + tiles:
        parts.append(jnp.zeros((rows - 2 * taps - tiles, side), F32))
    out_ref[base:, :] = jnp.concatenate(parts, axis=0).astype(BF16)
    for copy in copies[5:]:
        copy.wait()


def edge_kernel(dims, gathered_ref, table_ref, out_ref, ints, scalars, picked, columns, sems):
    side, chans, blocks, tiles, cap, taps, rows = dims
    count = tiles * cap
    base = blocks * chans
    kinds = table_ref.shape[0]
    per_group = side // kinds
    me = lax.axis_index("tile")
    tables = jnp.concatenate([gathered_ref[base:, band * side : (band + 1) * side] for band in range(tiles)], axis=0)
    values = tables.astype(F32).astype(jnp.int32)
    lists = pl.ds(0, tiles * tiles)
    others = pl.ds(tiles * tiles, tiles * 2 * taps)
    start = tiles * (tiles + 2 * taps)
    for band in range(tiles):
        ints[band * tiles : (band + 1) * tiles, :] = values[band * rows + 2 * taps : band * rows + 2 * taps + tiles]
    lists_copy = pltpu.make_async_copy(ints.at[lists, :], scalars.at[lists, :], sems.at[0])
    lists_copy.start()
    for band in range(tiles):
        at = tiles * tiles + band * 2 * taps
        ints[at : at + 2 * taps, :] = values[band * rows : band * rows + 2 * taps]
    others_copy = pltpu.make_async_copy(ints.at[others, :], scalars.at[others, :], sems.at[1])
    others_copy.start()
    ints[start : start + tiles * rows, :] = values
    row = lax.broadcasted_iota(jnp.int32, (side, side), 0)
    flip = (lax.broadcasted_iota(jnp.int32, (side, side), 1) + row == side - 1).astype(BF16)
    ints[start + tiles * rows :, :] = dot(tables, flip).astype(jnp.int32)
    lane = lax.broadcasted_iota(jnp.int32, (side, side), 1)
    total = jnp.zeros((side, side), F32)
    for kind in range(kinds):
        moved = pltpu.roll(table_ref[kind].astype(F32), per_group * kind + 1, 1)
        total = jnp.where(lane // per_group == kind, moved, total)
    for n, moved in enumerate([pltpu.roll(total, side - 1, 1), total]):
        moved = jnp.where(lane % per_group == 0, moved, 0.0)
        for m in range(per_group):
            columns[n, m * side : (m + 1) * side, :] = (moved if m == 0 else pltpu.roll(moved, m, 1)).astype(BF16)
    lists_copy.wait()
    own_row = me * tiles
    neigh = [scalars[own_row, cap + s] for s in range(4)]
    codes = [scalars[own_row, cap + 4 + s] for s in range(4)]

    def block_of(owner, slot):
        band = slot // cap
        local = scalars[band * tiles + owner, slot % cap]
        return gathered_ref[pl.ds(pl.multiple_of(local * chans, chans), chans), pl.ds(pl.multiple_of(band * side, side), side)]

    for slot in range(count):
        out_ref[slot * chans : (slot + 1) * chans, :] = block_of(me, slot)
    for s in range(4):
        owner = neigh[s]
        edge = codes[s] % 4
        dest = pl.ds((count + s) * chans, chans)

        @pl.when(edge >= 2)
        def _():
            for slot in range(count):
                group, member = slot // per_group, slot % per_group
                picked[group * chans : (group + 1) * chans, member * side : (member + 1) * side] = block_of(owner, slot)
            z = dot(picked[...], columns[edge - 2])
            z_hi = z.astype(BF16)
            z_lo = (z - z_hi.astype(F32)).astype(BF16)
            first = start + owner * rows + jnp.where(codes[s] >= 4, tiles * rows, 0)
            slots = ints[pl.ds(first, taps), :]
            inside = slots % per_group + ints[pl.ds(first + taps, taps), :] * per_group
            spots = [jnp.where(row == inside[k : k + 1], 1.0, 0.0).astype(BF16) for k in range(taps)]
            acc = jnp.zeros((2 * chans, side), F32)
            for group in range(count // per_group):
                here = jnp.where(slots // per_group == group, 1.0, 0.0).astype(BF16)
                hits = sum(spots[k] * here[k : k + 1] for k in range(taps))
                at = slice(group * chans, (group + 1) * chans)
                acc = acc + dot(jnp.concatenate([z_hi[at], z_lo[at]], axis=0), hits)
            out_ref[dest, :] = (acc[:chans] + acc[chans:]).astype(BF16)

    others_copy.wait()
    for s in range(4):
        owner = neigh[s]
        edge = codes[s] % 4
        dest = pl.ds((count + s) * chans, chans)

        @pl.when(edge < 2)
        def _():
            at = jnp.where(edge == 0, 0, side - 1)
            acc = jnp.zeros((chans, side), F32)
            for k in range(taps):
                slot = scalars[tiles * tiles + owner * 2 * taps + k, at]
                kind = scalars[tiles * tiles + owner * 2 * taps + taps + k, at]
                acc = acc + dot(block_of(owner, slot), table_ref[kind])
            out_ref[dest, :] = acc.astype(BF16)

            @pl.when(codes[s] >= 4)
            def _():
                out_ref[dest, :] = dot(acc.astype(BF16), flip).astype(BF16)


def filter_kernel(chans, last, filters, out_ref):
    outs, all_chans = filters.shape[2:]
    half = all_chans // 2
    me = lax.axis_index("chan")
    lane = lax.broadcasted_iota(jnp.int32, (outs, all_chans), 1)
    for b in range(3):
        first, second = [], []
        for a in range(3):
            value = filters[a, b].astype(F32)
            width = chans
            bit = 1
            while width < all_chans:
                other = jnp.where(
                    lane // width % 2 == 0, pltpu.roll(value, all_chans - width, 1), pltpu.roll(value, width, 1)
                )
                value = jnp.where((me & bit) != 0, other, value)
                width *= 2
                bit *= 2
            first.append(value)
            second.append(pltpu.roll(value, half, 1))
        low, high = (second, first) if last else (first, second)
        at = slice(b * outs, (b + 1) * outs)
        out_ref[at, :all_chans] = jnp.where(lane < half, low[0], high[1]).astype(BF16)
        out_ref[at, all_chans:] = low[2][:, :half].astype(BF16)


def tile_kernel(dims, last, many, *refs):
    side, chans, cap, tiles, all_chans, outs = dims
    parts = refs[:many]
    refs = refs[many:]
    if last:
        before_ref, *refs = refs
    slots_ref, weights_ref, table_ref, matrix, out_ref, slots, weights, image, *refs = refs
    if last:
        spread, staged, out_sems, sems = refs
    else:
        filters = matrix
        matrix, sems = refs
    taps = slots.shape[0]
    count = tiles * cap
    half = chans * many
    copies = start_all(sems, [(slots_ref, slots), (weights_ref, weights)])
    if not last:
        filter_kernel(chans, False, filters, matrix)

    def channels(index):
        return jnp.concatenate([part[index] for part in parts], axis=0)

    image[0:half, :] = channels(count)
    image[(side + 1) * half :, :] = channels(count + 1)
    wide = lax.broadcasted_iota(jnp.int32, (half, side), 1)

    def around(edge):
        value = channels(count + edge).astype(F32)
        before = jnp.where(wide == 0, 0.0, pltpu.roll(value, 1, 1))
        after = jnp.where(wide == side - 1, 0.0, pltpu.roll(value, side - 1, 1))
        return jnp.concatenate([before, value, after], axis=0).astype(BF16)

    left = dot(matrix[0:outs, :], around(2))
    right = dot(matrix[2 * outs :, :], around(3))
    if last:
        left = left + before_ref[side]
        right = right + before_ref[side + 1]
    else:
        out_ref[side] = left
        out_ref[side + 1] = right
    for copy in copies:
        copy.wait()

    def remap(r):
        lhs = jnp.concatenate([channels(slots[k, r]) for k in range(taps)], axis=1)
        rhs = jnp.concatenate([table_ref[weights[k, r]] for k in range(taps)], axis=0)
        return dot(lhs, rhs).astype(BF16)

    def place(r):
        image[(r + 1) * half : (r + 2) * half, :] = remap(r)

    lane = lax.broadcasted_iota(jnp.int32, (outs, side), 1)

    def multiply(i):
        x0 = image[i * half : (i + 3) * half, :]
        x1 = image[(i + 1) * half : (i + 4) * half, :]
        return dot(matrix[...], jnp.concatenate([x0, x1], axis=1))

    def combine(i, y):
        at_left = pltpu.roll(left, (side - i) % side, 1) if last else 0.0
        at_right = pltpu.roll(right, side - 1 - i, 1) if last else 0.0
        from_left = jnp.where(lane == 0, at_left, pltpu.roll(y[:outs], 1, 1))
        from_right = jnp.where(lane == side - 1, at_right, pltpu.roll(y[2 * outs :], side - 1, 1))
        total = y[outs : 2 * outs] + from_left + from_right
        if last:
            at = i % SEND * (outs + 1)
            spread[at : at + outs, :] = total + before_ref[i]
        else:
            out_ref[i] = total

    sent = []

    def finish(i, y):
        for h in range(2):
            combine(i + h, y[:, h * side : (h + 1) * side])
        if last and (i + 2) % SEND == 0:
            rows = pl.ds(i + 2 - SEND, SEND)
            step = outs // PIECES if i + 2 == side else outs
            for begin in range(0, outs, step):
                for o in range(begin, begin + step):
                    staged[o, rows, :] = spread[pl.ds(o, SEND, stride=outs + 1), :].astype(BF16)
                some = pl.ds(begin, step)
                sent.append(
                    pltpu.make_async_copy(staged.at[some, rows, :], out_ref.at[some, rows, :], out_sems.at[len(sent)])
                )
                sent[-1].start()

    for r in range(AHEAD + 1):
        place(r)
    for i in range(0, side, 2):
        for r in range(i + AHEAD + 1, min(i + AHEAD + 3, side)):
            place(r)
        finish(i, multiply(i))
    for copy in sent:
        copy.wait()


def body(source, send_list, block_slot, weight_index, remap_table, neighbour_tile, neighbour_edge, conv_weight):
    kinds, side = remap_table.shape[:2]
    chans = source.shape[0]
    tiles, cap = send_list.shape[1:]
    taps = block_slot.shape[1]
    blocks = source.shape[1] // side
    count = tiles * cap
    all_chans, outs = conv_weight.shape[2:]
    parts = lax.axis_size("chan")
    rows = round_up(2 * taps + tiles, 16)
    params = pltpu.CompilerParams(vmem_limit_bytes=LIMIT)
    slots, weights = in_hbm(block_slot.T), in_hbm(weight_index.T)
    filters = in_hbm(conv_weight.transpose(0, 1, 3, 2))
    packed, slots, weights, table, filters = pl.pallas_call(
        pack_kernel,
        out_shape=[
            jax.ShapeDtypeStruct((blocks * chans + rows, side), BF16),
            jax.ShapeDtypeStruct(slots.shape, jnp.int32),
            jax.ShapeDtypeStruct(weights.shape, jnp.int32),
            jax.ShapeDtypeStruct(remap_table.shape, BF16),
            jax.ShapeDtypeStruct(filters.shape, BF16),
        ],
        in_specs=[HBM] * 8,
        out_specs=[VMEM] * 5,
        scratch_shapes=[
            pltpu.VMEM((tiles, cap), jnp.int32),
            pltpu.VMEM(neighbour_tile.shape, jnp.int32),
            pltpu.VMEM(neighbour_edge.shape, jnp.int32),
            pltpu.SemaphoreType.DMA((blocks + 7,)),
        ],
        compiler_params=params,
        name="pack",
    )(
        slots, weights, in_hbm(send_list), in_hbm(neighbour_tile), in_hbm(neighbour_edge), in_hbm(source),
        in_hbm(remap_table), filters,
    )
    gathered = lax.all_gather(packed, "tile", axis=1, tiled=True)
    mine = pl.pallas_call(
        functools.partial(edge_kernel, (side, chans, blocks, tiles, cap, taps, rows)),
        out_shape=jax.ShapeDtypeStruct(((count + 4) * chans, side), BF16),
        in_specs=[VMEM, VMEM],
        out_specs=VMEM,
        scratch_shapes=[
            pltpu.VMEM((tiles * (tiles + 2 * taps + 2 * rows), side), jnp.int32),
            pltpu.SMEM((tiles * (tiles + 2 * taps), side), jnp.int32),
            pltpu.VMEM((count * kinds // side * chans, side * side // kinds), BF16),
            pltpu.VMEM((2, side // kinds * side, side), BF16),
            pltpu.SemaphoreType.DMA((2,)),
        ],
        compiler_params=params,
        name="edges",
    )(gathered, table)

    def swap(value, flip):
        return lax.ppermute(value, "chan", [(i, i ^ flip) for i in range(parts)])

    def spread(held, bit):
        while bit:
            for flip in list(held):
                held[flip ^ bit] = swap(held[flip], bit)
            bit //= 2
        return [held[f].reshape(count + 4, chans, side) for f in sorted(held)]

    many = parts // 2
    half = all_chans // 2
    mine, filters = lax.optimization_barrier((mine, filters))
    near = spread({0: mine}, many // 2)
    def matrix(last, filters):
        return pl.pallas_call(
            functools.partial(filter_kernel, chans, last),
            out_shape=jax.ShapeDtypeStruct((3 * outs, 3 * half), BF16),
            in_specs=[VMEM],
            out_specs=VMEM,
            compiler_params=params,
            name="filters",
        )(filters)

    across = swap(mine, many)
    dims = (side, chans, cap, tiles, all_chans, outs)
    scratch = [
        pltpu.SMEM(slots.shape, jnp.int32),
        pltpu.SMEM(weights.shape, jnp.int32),
        pltpu.VMEM(((side + 2) * half, side), BF16),
    ]
    flops = 2 * side * half * taps * side * side + 2 * side * side * 9 * half * outs
    cost = pl.CostEstimate(flops=flops, bytes_accessed=(side + 2) * outs * side * 4, transcendentals=0)
    so_far = pl.pallas_call(
        functools.partial(tile_kernel, dims, False, many),
        out_shape=jax.ShapeDtypeStruct((side + 2, outs, side), F32),
        in_specs=[VMEM] * (many + 4),
        out_specs=VMEM,
        scratch_shapes=scratch + [pltpu.VMEM((3 * outs, 3 * half), BF16), pltpu.SemaphoreType.DMA((2,))],
        compiler_params=params,
        cost_estimate=cost,
        name="near",
    )(*near, slots, weights, table, filters)
    across, filters, so_far = lax.optimization_barrier((across, filters, so_far))
    far = spread({many: across}, many // 2)
    far_filters = matrix(True, filters)
    return pl.pallas_call(
        functools.partial(tile_kernel, dims, True, many),
        out_shape=jax.ShapeDtypeStruct((outs, side, side), BF16),
        in_specs=[VMEM] * (many + 5),
        out_specs=HBM,
        scratch_shapes=scratch
        + [
            pltpu.VMEM((round_up(SEND * (outs + 1), 8), side), F32),
            pltpu.VMEM((outs, side, side), BF16),
            pltpu.SemaphoreType.DMA((side // SEND + PIECES - 1,)),
            pltpu.SemaphoreType.DMA((2,)),
        ],
        compiler_params=params,
        cost_estimate=cost,
        name="far",
    )(*far, so_far, slots, weights, table, far_filters)


def solution(mesh):
    in_specs = (
        P("chan", ("group", "tile")),
        P("tile", None, None),
        P("tile", None),
        P("tile", None),
        P(),
        P("tile", None),
        P("tile", None),
        P(None, None, None, "chan"),
    )
    out_specs = P("chan", ("group", "tile"), None)
    return jax.shard_map(body, mesh=mesh, in_specs=in_specs, out_specs=out_specs, check_vma=False)
```
